32 devices in a mesh: dp: 2 (over x), row: 4 (over z), col: 4 (over y, core).
Axes of the slice: x: 2, y: 2, z: 4, core: 2. Of those that a mesh axis runs over, the one named last changes fastest.
Arguments:
- block_input: bfloat16 [8192, 2048], P(('dp', 'row'), 'col'), may hold values from -6 to 6
- cotangent: bfloat16 [8192, 2048], P(('dp', 'row'), 'col'), may hold values from -6 to 6
- doc_lengths: int32 [4, 4], P('dp'), may hold values from 1 to 1280, 2048 in all within a row
- layernorm_gain: float32 [2048], P('col'), may hold values from 0.5 to 1.5
- layernorm_bias: float32 [2048], P('col'), may hold values from -2 to 2
- qkv_weight: bfloat16 [3, 2048, 2048], P(None, 'row', 'col'), may hold values from -0.125 to 0.125
- qkv_bias: float32 [3, 2048], P(None, ('row', 'col')), may hold values from -2 to 2
- fc1_weight: bfloat16 [8192, 2048], P('row', 'col'), may hold values from -0.125 to 0.125
- fc1_bias: float32 [8192], P(('row', 'col')), may hold values from -2 to 2
- dense_weight: bfloat16 [2048, 2048], P('col', 'row'), may hold values from -0.375 to 0.375
- fc2_weight: bfloat16 [2048, 8192], P('col', 'row'), may hold values from -0.0625 to 0.0625
- out_bias: float32 [2048], P('col'), may hold values from -2 to 2
Outputs:
- block_output: bfloat16 [8192, 2048], P(('dp', 'row'), 'col')
- input_grad: float32 [8192, 2048], P(('dp', 'row'), 'col')
- ln_gain_grad: float32 [2048], P('col')
- ln_bias_grad: float32 [2048], P('col')
- qkv_weight_grad: float32 [3, 2048, 2048], P(None, 'row', 'col')
- qkv_bias_grad: float32 [3, 2048], P(None, ('row', 'col'))
- fc1_weight_grad: float32 [8192, 2048], P('row', 'col')
- fc1_bias_grad: float32 [8192], P(('row', 'col'))
- dense_weight_grad: float32 [2048, 2048], P('col', 'row')
- fc2_weight_grad: float32 [2048, 8192], P('col', 'row')
- out_bias_grad: float32 [2048], P('col')
The draws below stay inside these ranges and needn't reach their ends.
Inputs may be any that keep to these rules, and one draw needn't show every extreme that they name: `doc_lengths`: each row gives the 4 document lengths of one sequence in order; they sum to 2048, and the largest of each row is exactly 1280.
All inputs are finite; a program needn't handle non-finite values.
Results may differ from the reference program's by a relative error of at most 0.018.
Values may be sent and summed in bfloat16 or wider, within the bound.
No kernel may reach another device: no remote copies, remote signals or barrier semaphores. Data moves between devices by JAX's collectives and lax.ppermute only.
A program may use at most 256 MiB of HBM per device.

```python
import math
import jax
import jax.numpy as jnp
import numpy as np
from jax import lax

MODEL_WIDTH = 2048
HEADS = 32
HEAD_DIM = 64
ROT = 32
FF = 8192
SEQ = 2048
DOCS = 4
SEQS = 4
TOKENS = 8192


def block_levels(key, extent, split, least, top_value):
    level = 1.0
    for dim, shards_of in split:
        steps = jax.random.uniform(jax.random.fold_in(jax.random.fold_in(key, 6), dim), (shards_of,), jnp.float32, least / len(split), top_value / len(split))
        level = level * jnp.repeat(jnp.exp(steps), extent[dim] // shards_of).reshape((-1,) + (1,) * (len(extent) - 1 - dim))
    return level


def profile(number_of, total, most, lean):
    weights = [(1 << 20) // math.isqrt(grade ** lean) + 1 for grade in range(2, number_of + 1)]
    surplus, holding = total - most - (number_of - 1), [1] * (number_of - 1)
    while surplus > 0:
        free = [i for i in range(number_of - 1) if holding[i] < most]
        pool, budget = sum([weights[i] for i in free]), surplus
        for i in free:
            more = min(most - holding[i], max(1, budget * weights[i] // pool), surplus)
            holding[i] = holding[i] + more
            surplus = surplus - more
    return np.array([most] + holding)


def ragged_sizes(key, count, total, bound, lean):
    if count == 2:
        one = jax.random.randint(key, (), max(1, total - bound), min(bound, total - 1) + 1)
        return jnp.stack([one, total - one])
    tallies = jnp.asarray(profile(count, total, bound, lean), jnp.int32)
    twos = (count - 1) // 2
    source_of, taker = tallies[1:1 + 2 * twos:2], tallies[2:2 + 2 * twos:2]
    room = jnp.minimum(source_of - 1, bound - taker)
    passed = jax.random.randint(jax.random.fold_in(key, 1), (twos,), 0, 1 << 20) % (room + 1)
    tallies = tallies.at[1:1 + 2 * twos:2].set(source_of - passed).at[2:2 + 2 * twos:2].set(taker + passed)
    return tallies[jax.random.permutation(jax.random.fold_in(key, 2), count)]


def bell_draw(own_key, extent, spread, reach, pieces=(), kind=jnp.bfloat16):
    loudness = block_levels(own_key, extent, pieces, -0.22, 0.18) if pieces else 1.0
    drawn = jax.random.normal(own_key, extent, jnp.float32) * spread * loudness
    return jnp.minimum(jnp.maximum(drawn, -reach), reach).astype(kind)


def setup_inputs(seed: int = 0) -> dict:
    key_of = jax.random.split(jax.random.key(seed), 13)
    return {
        "block_input": bell_draw(key_of[0], (TOKENS, MODEL_WIDTH), 1.0, 6.0, ((0, 8), (1, 4))),
        "cotangent": bell_draw(key_of[1], (TOKENS, MODEL_WIDTH), 1.0, 6.0, ((0, 8), (1, 4))),
        "doc_lengths": jax.vmap(lambda own: ragged_sizes(own, DOCS, SEQ, SEQ * 5 // 8, 1))(jax.random.split(key_of[2], SEQS)).reshape((SEQS, DOCS)).astype(jnp.int32),
        "layernorm_gain": jnp.clip(1.0 + 0.1 * jax.random.normal(key_of[3], (MODEL_WIDTH,), jnp.float32), 0.5, 1.5),
        "layernorm_bias": bell_draw(key_of[4], (MODEL_WIDTH,), 0.3, 2.0, ((0, 4),), jnp.float32),
        "qkv_weight": bell_draw(key_of[5], (3, MODEL_WIDTH, MODEL_WIDTH), MODEL_WIDTH ** -0.5, 0.125, ((1, 4), (2, 4))),
        "qkv_bias": bell_draw(key_of[6], (3, MODEL_WIDTH), 0.3, 2.0, ((1, 16),), jnp.float32),
        "fc1_weight": bell_draw(key_of[7], (FF, MODEL_WIDTH), MODEL_WIDTH ** -0.5, 0.125, ((0, 4), (1, 4))),
        "fc1_bias": bell_draw(key_of[8], (FF,), 0.3, 2.0, ((0, 16),), jnp.float32),
        "dense_weight": bell_draw(key_of[9], (MODEL_WIDTH, MODEL_WIDTH), (MODEL_WIDTH // 8) ** -0.5, 0.375, ((0, 4), (1, 4))),
        "fc2_weight": bell_draw(key_of[10], (MODEL_WIDTH, FF), FF ** -0.5, 0.0625, ((0, 4), (1, 4))),
        "out_bias": bell_draw(key_of[11], (MODEL_WIDTH,), 0.3, 2.0, ((0, 4),), jnp.float32),
    }


EPSILON = 1e-05
MASKED = -1e+30

@jax.custom_vjp
def low(v):
    return lax.optimization_barrier(v.astype(jnp.bfloat16)).astype(jnp.float32)

@jax.custom_vjp
def low_back(v):
    return v

def low_keep(v):
    return (low(v), None)

def low_pass(kept, grad):
    return (grad,)

def back_keep(v):
    return (v, None)

def back_low(kept, grad):
    return (low(grad),)
low.defvjp(low_keep, low_pass)
low_back.defvjp(back_keep, back_low)

def matmul(left, right):
    return jnp.dot(left, right, precision=lax.Precision.HIGHEST, preferred_element_type=jnp.float32)

def segment_ids(doc_lengths):
    ends = jnp.cumsum(doc_lengths, axis=1).astype(jnp.int32)
    place = jnp.arange(SEQ, dtype=jnp.int32)
    return lax.optimization_barrier(jnp.sum((place[None, :, None] >= ends[:, None, :]).astype(jnp.int32), axis=2)).astype(jnp.int32)

def rotary_tables(count):
    place = (jnp.arange(count, dtype=jnp.int32) % SEQ).astype(jnp.float32)
    freqs = jnp.exp(jnp.arange(ROT // 2, dtype=jnp.float32) * (-2.0 * math.log(10000.0) / ROT))
    angle = place[:, None] * freqs[None, :]
    return (jnp.cos(angle)[:, None, :], jnp.sin(angle)[:, None, :])

def rotate(values, cosine, sine):
    half = ROT // 2
    first = values[..., :half]
    second = values[..., half:ROT]
    return jnp.concatenate([first * cosine - second * sine, second * cosine + first * sine, values[..., ROT:]], axis=-1)

def to_items(values):
    count = values.shape[0] // SEQ
    return values.reshape(count, SEQ, HEADS, HEAD_DIM).transpose(0, 2, 1, 3).reshape(count * HEADS, SEQ, HEAD_DIM)

def from_items(values):
    count = values.shape[0] // HEADS
    return values.reshape(count, HEADS, SEQ, HEAD_DIM).transpose(0, 2, 1, 3).reshape(count * SEQ, HEADS * HEAD_DIM)

def attend_one(item):
    query, keys, values, segment = item
    place = jnp.arange(SEQ, dtype=jnp.int32)
    allowed = (place[:, None] >= place[None, :]) & (segment[:, None] == segment[None, :])
    scores = low_back(jnp.dot(query, keys.T, precision=lax.Precision.HIGHEST, preferred_element_type=jnp.float32) * HEAD_DIM ** (-0.5))
    scores = jnp.where(allowed, scores, MASKED)
    peak = lax.optimization_barrier(jnp.max(scores, axis=1, keepdims=True))
    exponent = jnp.exp(scores - peak)
    probs = low(exponent / lax.optimization_barrier(jnp.sum(exponent, axis=1, keepdims=True)))
    return matmul(probs, values)

def reference(block_input, cotangent, doc_lengths, layernorm_gain, layernorm_bias, qkv_weight, qkv_bias, fc1_weight, fc1_bias, dense_weight, fc2_weight, out_bias):
    segments = segment_ids(doc_lengths)
    seg_items = jnp.repeat(segments, HEADS, axis=0)
    cosine, sine = rotary_tables(block_input.shape[0])

    def forward(inputs, gain, shift, qkv_w, qkv_b, fc1_w, fc1_b, dense_w, fc2_w, bias_out):
        row_average = lax.optimization_barrier(jnp.mean(inputs, axis=1, keepdims=True))
        meansq = lax.optimization_barrier(jnp.mean(inputs * inputs, axis=1, keepdims=True))
        inverse_deviation = lax.rsqrt(meansq - row_average * row_average + EPSILON)
        normed_output = low((inputs - row_average) * inverse_deviation * gain + shift)
        query = low_back(matmul(normed_output, qkv_w[0].T) + qkv_b[0])
        keys = low_back(matmul(normed_output, qkv_w[1].T) + qkv_b[1])
        values = low_back(matmul(normed_output, qkv_w[2].T) + qkv_b[2])
        query = low(rotate(query.reshape(-1, HEADS, HEAD_DIM), cosine, sine))
        keys = low(rotate(keys.reshape(-1, HEADS, HEAD_DIM), cosine, sine))
        values = low(values.reshape(-1, HEADS, HEAD_DIM))
        attended = lax.map(jax.checkpoint(attend_one), (to_items(query), to_items(keys), to_items(values), seg_items))
        attended = low(low_back(from_items(attended)))
        fc_pre = low_back(matmul(normed_output, fc1_w.T) + fc1_b)
        activated = low(jax.nn.gelu(fc_pre, approximate=True))
        branch = low_back(matmul(attended, dense_w.T) + matmul(activated, fc2_w.T) + bias_out)
        return inputs + branch
    params = (block_input.astype(jnp.float32), layernorm_gain.astype(jnp.float32), layernorm_bias.astype(jnp.float32), qkv_weight.astype(jnp.float32), qkv_bias.astype(jnp.float32), fc1_weight.astype(jnp.float32), fc1_bias.astype(jnp.float32), dense_weight.astype(jnp.float32), fc2_weight.astype(jnp.float32), out_bias.astype(jnp.float32))
    result, pull = jax.vjp(forward, *params)
    grads = pull(cotangent.astype(jnp.float32))
    return (result.astype(jnp.bfloat16), grads[0], grads[1], grads[2], grads[3], grads[4], grads[5], grads[6], grads[7], grads[8], grads[9])
```

```python
import functools
import math

import jax
import jax.numpy as jnp
from jax import lax
from jax.experimental import pallas as pl
from jax.experimental.pallas import tpu as pltpu
from jax.sharding import Mesh
from jax.sharding import PartitionSpec as P

MODEL_WIDTH = 2048
HEAD_DIM = 64
ROT = 32
SEQ = 2048
EPSILON = 1e-05
MASKED = -1e30
SCALE = HEAD_DIM ** (-0.5)
VMEM = 60 * 1024 * 1024

BF = jnp.bfloat16
F32 = jnp.float32


def swap(value, axis):
    return lax.ppermute(value, axis, [(0, 1), (1, 0)])


def nt(left, right):
    return lax.dot_general(left, right, (((1,), (1,)), ((), ())), preferred_element_type=F32)


def tn(left, right):
    return lax.dot_general(left, right, (((0,), (0,)), ((), ())), preferred_element_type=F32)


def nn(left, right):
    return lax.dot_general(left, right, (((1,), (0,)), ((), ())), preferred_element_type=F32)


def params():
    return pltpu.CompilerParams(vmem_limit_bytes=VMEM)


def cost(flops, nbytes, transcendentals=0):
    return pl.CostEstimate(
        flops=int(flops), bytes_accessed=int(nbytes), transcendentals=int(transcendentals)
    )


def whole(shape):
    return pl.BlockSpec(shape, lambda *_: (0,) * len(shape))


def pack_kernel(order, sx, qkv, fc1, dense, fc2, near, same, far):
    step = pl.program_id(0)
    x = sx[0]

    def write(put):
        fc2_t = fc2[...].T
        put(0, jnp.where(x == 0, fc2_t[:256], fc2_t[256:]))
        put(256, jnp.where(x == 0, fc2_t[256:], fc2_t[:256]))
        put(512, jnp.where(x == 0, fc1[:256], fc1[256:]))
        put(768, jnp.where(x == 0, fc1[256:], fc1[:256]))
        dense_t = dense[...].T
        for s in range(2):
            base = 1024 + 256 * s
            for part in range(3):
                low, high = qkv[part, :64], qkv[part, 64:]
                first, second = (low, high) if s == 0 else (high, low)
                put(base + 64 * part, jnp.where(x == 0, first, second))
            low, high = dense_t[:64], dense_t[64:]
            first, second = (low, high) if s == 0 else (high, low)
            put(base + 192, jnp.where(x == 0, first, second))

    def into(ref, lead):
        def put(row, value):
            if lead:
                ref[0, row : row + value.shape[0], :] = value
            else:
                ref[row : row + value.shape[0], :] = value

        return put

    @pl.when(step < 2)
    def _():
        write(into(near, True))

    @pl.when(step == 2)
    def _():
        write(into(far, False))

    @pl.when(step == 3)
    def _():
        write(into(same, False))


def pack(order, sx, qkv, fc1, dense, fc2):
    rows = 1536
    return pl.pallas_call(
        pack_kernel,
        grid_spec=pltpu.PrefetchScalarGridSpec(
            num_scalar_prefetch=2,
            grid=(4,),
            in_specs=[
                pl.BlockSpec((3, 128, 512), lambda i, o, x: (0, o[i], 0)),
                pl.BlockSpec((512, 512), lambda i, o, x: (o[i], 0)),
                pl.BlockSpec((512, 128), lambda i, o, x: (0, o[i])),
                pl.BlockSpec((512, 512), lambda i, o, x: (0, o[i])),
            ],
            out_specs=[
                pl.BlockSpec((1, rows, 512), lambda i, o, x: (jnp.minimum(i, 1), 0, 0)),
                pl.BlockSpec((rows, 512), lambda i, o, x: (0, 0)),
                pl.BlockSpec((rows, 512), lambda i, o, x: (0, 0)),
            ],
        ),
        out_shape=[
            jax.ShapeDtypeStruct((2, rows, 512), BF),
            jax.ShapeDtypeStruct((rows, 512), BF),
            jax.ShapeDtypeStruct((rows, 512), BF),
        ],
        compiler_params=params(),
        cost_estimate=cost(0, 4 * rows * 512 * 4),
    )(order, sx, qkv, fc1, dense, fc2)


def unpack_mlp_kernel(order, sx, first, second, fc1_out, fc2_out):
    x = sx[0]
    a, b = first[0].astype(F32), second[0].astype(F32)
    low, high = jnp.where(x == 0, a, b), jnp.where(x == 0, b, a)
    fc1_out[:256, :] = low[256:]
    fc1_out[256:, :] = high[256:]
    fc2_out[:, :256] = low[:256].T
    fc2_out[:, 256:] = high[:256].T


def unpack_mlp(order, sx, first, second):
    piece = pl.BlockSpec((1, 512, 512), lambda i, o, x: (o[i], 0, 0))
    return pl.pallas_call(
        unpack_mlp_kernel,
        grid_spec=pltpu.PrefetchScalarGridSpec(
            num_scalar_prefetch=2,
            grid=(4,),
            in_specs=[piece, piece],
            out_specs=[
                pl.BlockSpec((512, 512), lambda i, o, x: (i, 0)),
                pl.BlockSpec((512, 512), lambda i, o, x: (0, i)),
            ],
        ),
        out_shape=[
            jax.ShapeDtypeStruct((2048, 512), F32),
            jax.ShapeDtypeStruct((512, 2048), F32),
        ],
        compiler_params=params(),
        cost_estimate=cost(0, 12 * 1024 * 1024),
    )(order, sx, first, second)


def unpack_att_kernel(order, sx, first, second, qkv_out, dense_out):
    x = sx[0]
    a, b = first[0].astype(F32), second[0].astype(F32)
    low, high = jnp.where(x == 0, a, b), jnp.where(x == 0, b, a)
    for part in range(3):
        qkv_out[part, :64, :] = low[64 * part : 64 * part + 64]
        qkv_out[part, 64:, :] = high[64 * part : 64 * part + 64]
    dense_out[...] = jnp.concatenate([low[192:], high[192:]], axis=0).T


def unpack_att(order, sx, first, second):
    piece = pl.BlockSpec((1, 256, 512), lambda i, o, x: (o[i], 0, 0))
    return pl.pallas_call(
        unpack_att_kernel,
        grid_spec=pltpu.PrefetchScalarGridSpec(
            num_scalar_prefetch=2,
            grid=(4,),
            in_specs=[piece, piece],
            out_specs=[
                pl.BlockSpec((3, 128, 512), lambda i, o, x: (0, i, 0)),
                pl.BlockSpec((512, 128), lambda i, o, x: (0, i)),
            ],
        ),
        out_shape=[
            jax.ShapeDtypeStruct((3, 512, 512), F32),
            jax.ShapeDtypeStruct((512, 512), F32),
        ],
        compiler_params=params(),
        cost_estimate=cost(0, 6 * 1024 * 1024),
    )(order, sx, first, second)


def norm_kernel(place, xs, scale, normed, stats):
    total = jnp.zeros((256, 1), F32)
    square = jnp.zeros((256, 1), F32)
    for q in range(4):
        value = xs[0, q].astype(F32)
        total += jnp.sum(value, axis=1, keepdims=True)
        square += jnp.sum(value * value, axis=1, keepdims=True)
    average = total / MODEL_WIDTH
    inverse = lax.rsqrt(square / MODEL_WIDTH - average * average + EPSILON)
    for r in range(4):
        value = xs[0, place[r]].astype(F32)
        centered = (value - average) * inverse
        normed[:, 512 * r : 512 * r + 512] = (
            centered * scale[2 * r : 2 * r + 1, :] + scale[2 * r + 1 : 2 * r + 2, :]
        ).astype(BF)
    stats[:, :128] = jnp.broadcast_to(average, (256, 128))
    stats[:, 128:] = jnp.broadcast_to(inverse, (256, 128))


def norm_tokens(place, gathered, scale):
    return pl.pallas_call(
        norm_kernel,
        grid_spec=pltpu.PrefetchScalarGridSpec(
            num_scalar_prefetch=1,
            grid=(8,),
            in_specs=[
                pl.BlockSpec((1, 4, 256, 512), lambda i, o: (i // 4, 0, i % 4, 0)),
                pl.BlockSpec((8, 512), lambda i, o: (0, 0)),
            ],
            out_specs=[
                pl.BlockSpec((256, 2048), lambda i, o: (i, 0)),
                pl.BlockSpec((256, 256), lambda i, o: (i, 0)),
            ],
        ),
        out_shape=[
            jax.ShapeDtypeStruct((SEQ, MODEL_WIDTH), BF),
            jax.ShapeDtypeStruct((SEQ, 256), F32),
        ],
        compiler_params=params(),
        cost_estimate=cost(SEQ * MODEL_WIDTH * 8, SEQ * MODEL_WIDTH * 4 + SEQ * 1024),
    )(place, gathered, scale)


def order_kernel(place, xs, out):
    for r in range(4):
        out[:, 512 * r : 512 * r + 512] = xs[0, place[r]]


def order_tokens(place, gathered):
    return pl.pallas_call(
        order_kernel,
        grid_spec=pltpu.PrefetchScalarGridSpec(
            num_scalar_prefetch=1,
            grid=(8,),
            in_specs=[pl.BlockSpec((1, 4, 256, 512), lambda i, o: (i // 4, 0, i % 4, 0))],
            out_specs=pl.BlockSpec((256, 2048), lambda i, o: (i, 0)),
        ),
        out_shape=jax.ShapeDtypeStruct((SEQ, MODEL_WIDTH), BF),
        compiler_params=params(),
        cost_estimate=cost(0, SEQ * MODEL_WIDTH * 4),
    )(place, gathered)


ROOT = math.sqrt(2.0 / math.pi)
CUBIC = 0.044715
TILE = 512


def store_grad(out, row, value):
    for at, r in enumerate((0, 2, 1, 3)):
        out[at, row : row + value.shape[0], :] = value[:, 512 * r : 512 * r + 512].astype(BF)


def mlp_kernel(n, c, v0, v1, w0, w1, bias, act_out, dfc_out, grad0, grad1, sums, acc):
    step = pl.program_id(0)

    @pl.when(step == 0)
    def _():
        acc[...] = jnp.zeros_like(acc)
        sums[...] = jnp.zeros_like(sums)

    for s, (v, w) in enumerate(((v0, w0), (v1, w1))):
        cols = slice(256 * s, 256 * s + 256)
        pre = nt(n[...], w[...]) + bias[:, cols]
        back = nt(c[...], v[...])
        square = pre * pre
        angle = jnp.tanh(ROOT * pre * (1.0 + CUBIC * square))
        half = 0.5 * (1.0 + angle)
        act = (pre * half).astype(BF)
        slope = half + 0.5 * pre * (1.0 - angle * angle) * (ROOT * (1.0 + 3.0 * CUBIC * square))
        dfc = back * slope
        sums[:, cols] += jnp.sum(dfc, axis=0, keepdims=True)
        dfc = dfc.astype(BF)
        act_out[:, cols] = act
        dfc_out[:, cols] = dfc
        acc[512 * s : 512 * s + 256] += tn(act, c[...])
        acc[512 * s + 256 : 512 * s + 512] += tn(dfc, n[...])

    @pl.when(step == SEQ // TILE - 1)
    def _():
        store_grad(grad0, 0, acc[:512])
        store_grad(grad1, 0, acc[512:])


def mlp(normed, cot, v, w, bias):
    tile = pl.BlockSpec((TILE, MODEL_WIDTH), lambda i: (i, 0))
    weight = whole((256, MODEL_WIDTH))
    units = pl.BlockSpec((TILE, 512), lambda i: (i, 0))
    grad = whole((4, 512, 512))
    return pl.pallas_call(
        mlp_kernel,
        grid=(SEQ // TILE,),
        in_specs=[tile, tile, weight, weight, weight, weight, whole((1, 512))],
        out_specs=[units, units, grad, grad, whole((1, 512))],
        out_shape=[
            jax.ShapeDtypeStruct((SEQ, 512), BF),
            jax.ShapeDtypeStruct((SEQ, 512), BF),
            jax.ShapeDtypeStruct((4, 512, 512), BF),
            jax.ShapeDtypeStruct((4, 512, 512), BF),
            jax.ShapeDtypeStruct((1, 512), F32),
        ],
        scratch_shapes=[pltpu.VMEM((1024, MODEL_WIDTH), F32)],
        compiler_params=params(),
        cost_estimate=cost(8 * SEQ * MODEL_WIDTH * 512, 28 * 1024 * 1024, SEQ * 512),
    )(normed, cot, v[0], v[1], w[0], w[1], bias)


def rotated(value, tables, sign):
    return (
        value * tables[0]
        + pltpu.roll(value, 112, 1) * (sign * tables[1])
        + pltpu.roll(value, 16, 1) * (sign * tables[2])
    )


def heads_kernel(n, c, w0, w1, bias, tables, q_out, k_out, v_out, d_out, joined):
    @pl.when(pl.program_id(0) == 0)
    def _():
        for part in range(4):
            joined[128 * part : 128 * part + 64] = w0[64 * part : 64 * part + 64]
            joined[128 * part + 64 : 128 * part + 128] = w1[64 * part : 64 * part + 64]

    pre = nt(n[...], joined[:384]) + bias[...]
    q_out[...] = (rotated(pre[:, :128], tables, 1.0) * SCALE).astype(BF)
    k_out[...] = rotated(pre[:, 128:256], tables, 1.0).astype(BF)
    v_out[...] = pre[:, 256:].astype(BF)
    d_out[...] = nt(c[...], joined[384:]).astype(BF)


def heads(normed, cot, w, bias, tables):
    tile = pl.BlockSpec((TILE, MODEL_WIDTH), lambda i: (i, 0))
    weight = whole((256, MODEL_WIDTH))
    head = pl.BlockSpec((TILE, 128), lambda i: (i, 0))
    return pl.pallas_call(
        heads_kernel,
        grid=(SEQ // TILE,),
        in_specs=[
            tile,
            tile,
            weight,
            weight,
            whole((1, 384)),
            pl.BlockSpec((3, TILE, 128), lambda i: (0, i, 0)),
        ],
        out_specs=[head] * 4,
        out_shape=[jax.ShapeDtypeStruct((SEQ, 128), BF)] * 4,
        scratch_shapes=[pltpu.VMEM((512, MODEL_WIDTH), BF)],
        compiler_params=params(),
        cost_estimate=cost(2 * SEQ * MODEL_WIDTH * 512, 24 * 1024 * 1024),
    )(normed, cot, w[0], w[1], bias, tables)


BLOCK = 256
BLOCKS = SEQ // BLOCK


def attend_kernel(
    low, q, k, v, d, start, tables, o_out, dq_out, dk_out, dv_out, sums, scores, dk_acc, dv_acc
):
    i = pl.program_id(0)

    @pl.when(i == 0)
    def _():
        dk_acc[...] = jnp.zeros_like(dk_acc)
        dv_acc[...] = jnp.zeros_like(dv_acc)
        sums[...] = jnp.zeros_like(sums)

    lane = lax.broadcasted_iota(jnp.int32, (BLOCK, 128), 1)
    masks = (lane < HEAD_DIM, lane >= HEAD_DIM)
    zero = jnp.zeros((BLOCK, 128), BF)
    queries = [jnp.where(m, q[...], zero) for m in masks]
    grads = [jnp.where(m, d[...], zero) for m in masks]
    col = lax.broadcasted_iota(jnp.int32, (BLOCK, BLOCK), 1)
    row = lax.broadcasted_iota(jnp.int32, (BLOCK, BLOCK), 0) + i * BLOCK
    begin = start[:, :1]

    def at(j):
        return pl.ds(pl.multiple_of(j * BLOCK, BLOCK), BLOCK)

    def score(j, peaks):
        keys = k[at(j), :]
        here = col + j * BLOCK
        allowed = (here >= begin) & (here <= row)
        new = []
        for h in range(2):
            s = jnp.where(allowed, nt(queries[h], keys), MASKED)
            scores[h, j] = s
            new.append(jnp.maximum(peaks[h], jnp.maximum(s[:, :128], s[:, 128:])))
        return tuple(new)

    floor = jnp.full((BLOCK, 128), MASKED, F32)
    peaks = lax.fori_loop(low[i], i + 1, score, (floor, floor))
    peaks = [jnp.max(p, axis=1, keepdims=True) for p in peaks]

    def weigh(j, carry):
        sums_, outs = carry
        values = v[at(j), :]
        new_sums, new_outs = [], []
        for h in range(2):
            p = jnp.exp(scores[h, j] - peaks[h])
            scores[h, j] = p
            new_sums.append(sums_[h] + p[:, :128] + p[:, 128:])
            new_outs.append(outs[h] + nn(p.astype(BF), values))
        return tuple(new_sums), tuple(new_outs)

    blank = jnp.zeros((BLOCK, 128), F32)
    totals, outs = lax.fori_loop(low[i], i + 1, weigh, ((blank, blank), (blank, blank)))
    inverse = [1.0 / jnp.sum(t, axis=1, keepdims=True) for t in totals]
    outs = [outs[h] * inverse[h] for h in range(2)]
    o_out[...] = jnp.where(masks[0], outs[0], outs[1]).astype(BF)
    deltas = [
        jnp.sum(outs[h] * grads[h].astype(F32), axis=1, keepdims=True) for h in range(2)
    ]

    def back(j, carry):
        keys, values = k[at(j), :], v[at(j), :]
        new = []
        dk, dv = dk_acc[at(j), :], dv_acc[at(j), :]
        for h in range(2):
            probs = scores[h, j] * inverse[h]
            d_probs = nt(grads[h], values)
            d_scores = (probs * (d_probs - deltas[h])).astype(BF)
            new.append(carry[h] + nn(d_scores, keys))
            dk += tn(d_scores, queries[h])
            dv += tn(probs.astype(BF), grads[h])
        dk_acc[at(j), :] = dk
        dv_acc[at(j), :] = dv
        return tuple(new)

    dq = lax.fori_loop(low[i], i + 1, back, (blank, blank))
    dq = jnp.where(masks[0], dq[0], dq[1]) * SCALE
    here = [tables[t, at(i), :] for t in range(3)]
    dq = rotated(dq, here, -1.0)
    dq_out[...] = dq.astype(BF)
    sums[0:1, :] += jnp.sum(dq, axis=0, keepdims=True)

    @pl.when(i == BLOCKS - 1)
    def _():
        for j in range(BLOCKS):
            rows = slice(j * BLOCK, (j + 1) * BLOCK)
            dk = rotated(dk_acc[rows], [tables[t, rows] for t in range(3)], -1.0)
            dv = dv_acc[rows]
            dk_out[rows, :] = dk.astype(BF)
            dv_out[rows, :] = dv.astype(BF)
            sums[1:2, :] += jnp.sum(dk, axis=0, keepdims=True)
            sums[2:3, :] += jnp.sum(dv, axis=0, keepdims=True)


def attend(low, q, k, v, d, start, tables):
    tile = pl.BlockSpec((BLOCK, 128), lambda i, o: (i, 0))
    full = pl.BlockSpec((SEQ, 128), lambda i, o: (0, 0))
    head = jax.ShapeDtypeStruct((SEQ, 128), BF)
    return pl.pallas_call(
        attend_kernel,
        grid_spec=pltpu.PrefetchScalarGridSpec(
            num_scalar_prefetch=1,
            grid=(BLOCKS,),
            in_specs=[
                tile,
                full,
                full,
                tile,
                tile,
                pl.BlockSpec((3, SEQ, 128), lambda i, o: (0, 0, 0)),
            ],
            out_specs=[tile, tile, full, full, pl.BlockSpec((8, 128), lambda i, o: (0, 0))],
            scratch_shapes=[
                pltpu.VMEM((2, BLOCKS, BLOCK, BLOCK), F32),
                pltpu.VMEM((SEQ, 128), F32),
                pltpu.VMEM((SEQ, 128), F32),
            ],
        ),
        out_shape=[head, head, head, head, jax.ShapeDtypeStruct((8, 128), F32)],
        compiler_params=params(),
        cost_estimate=cost(6 * 2 * 2 * SEQ * SEQ * 64, 8 * 1024 * 1024, SEQ * SEQ),
    )(low, q, k, v, d, start, tables)


def att_grad_kernel(n, c, dq, dk, dv, o, grad0, grad1, acc):
    step = pl.program_id(0)

    @pl.when(step == 0)
    def _():
        acc[...] = jnp.zeros_like(acc)

    acc[:384] += tn(jnp.concatenate([dq[...], dk[...], dv[...]], axis=1), n[...])
    acc[384:] += tn(o[...], c[...])

    @pl.when(step == SEQ // TILE - 1)
    def _():
        for part in range(4):
            store_grad(grad0, 64 * part, acc[128 * part : 128 * part + 64])
            store_grad(grad1, 64 * part, acc[128 * part + 64 : 128 * part + 128])


def att_grad(normed, cot, dq, dk, dv, o):
    tile = pl.BlockSpec((TILE, MODEL_WIDTH), lambda i: (i, 0))
    head = pl.BlockSpec((TILE, 128), lambda i: (i, 0))
    grad = whole((4, 256, 512))
    return pl.pallas_call(
        att_grad_kernel,
        grid=(SEQ // TILE,),
        in_specs=[tile, tile, head, head, head, head],
        out_specs=[grad, grad],
        out_shape=[jax.ShapeDtypeStruct((4, 256, 512), BF)] * 2,
        scratch_shapes=[pltpu.VMEM((512, MODEL_WIDTH), F32)],
        compiler_params=params(),
        cost_estimate=cost(2 * SEQ * MODEL_WIDTH * 512, 22 * 1024 * 1024),
    )(normed, cot, dq, dk, dv, o)


def project_kernel(parts, zl, *refs):
    count = len(parts)
    lefts, rights = refs[:count], refs[count : -3]
    near, same, joined = refs[-3:]

    @pl.when((pl.program_id(0) == 0) & (pl.program_id(1) == 0))
    def _():
        row, at = 0, 0
        for rows in parts:
            for first, size in rows:
                joined[row : row + size] = rights[at][first : first + size]
                row, at = row + size, at + 1

    left = jnp.concatenate([ref[...] for ref in lefts], axis=1)
    for out, pieces in ((near, (1, 3)), (same, (0, 2))):
        for at, r in enumerate(pieces):
            out[at, 0] = nn(left, joined[:, 512 * r : 512 * r + 512]).astype(BF)


def project(zl, items):
    parts = [[(first, size) for _, first, size in rows] for _, rows in items]
    depth = sum(size for rows in parts for _, size in rows)
    lefts = [left for left, _ in items]
    rights = [right for _, rows in items for right, _, _ in rows]
    half = SEQ // 2
    steps = half // TILE

    def tokens(z, t, s):
        return ((z ^ s[0]) * steps + t, 0)

    out = pl.BlockSpec((2, 1, TILE, 512), lambda z, t, s: (0, z, t, 0))
    shape = jax.ShapeDtypeStruct((2, 2, half, 512), BF)
    return pl.pallas_call(
        functools.partial(project_kernel, parts),
        grid_spec=pltpu.PrefetchScalarGridSpec(
            num_scalar_prefetch=1,
            grid=(2, steps),
            in_specs=[pl.BlockSpec((TILE, left.shape[1]), tokens) for left in lefts]
            + [
                pl.BlockSpec(
                    right.shape, lambda z, t, s: (0, 0), pipeline_mode=pl.Buffered(buffer_count=1)
                )
                for right in rights
            ],
            out_specs=[out, out],
            scratch_shapes=[pltpu.VMEM((depth, MODEL_WIDTH), BF)],
        ),
        out_shape=[shape, shape],
        compiler_params=params(),
        cost_estimate=cost(
            2 * SEQ * MODEL_WIDTH * depth, SEQ * (MODEL_WIDTH + depth) * 2 + 2 * depth * MODEL_WIDTH
        ),
    )(zl, *lefts, *rights)


def add(left, right):
    return (left.astype(F32) + right.astype(F32)).astype(BF)


def scatter_sum(near, same):
    both = add(same, swap(near, "c"))
    mid = both.shape[2] // 2
    from_z = swap(both[1, 1, :mid], "zl")
    from_y = swap(both[1, 1, mid:], "y")
    to_y = jnp.concatenate([add(both[1, 0, :mid], from_z), both[1, 0, mid:]], axis=0)
    to_z = jnp.concatenate([both[0, 1, :mid], add(both[0, 1, mid:], from_y)], axis=0)
    return both[0, 0].astype(F32) + swap(to_y, "y").astype(F32) + swap(to_z, "zl").astype(F32)


def more_dp(value):
    if lax.axis_size("xo") > 1:
        return lax.psum(value, "xo")
    return value


def reduce_grad(own, other):
    mine = add(own[0], swap(own[1], "x"))
    theirs = add(other[0], swap(other[1], "x"))
    back = swap(theirs, "zh")
    far = add(mine[2:], back[2:])
    same = add(mine[:2], back[:2])
    far, same = more_dp(far), more_dp(same)
    near = swap(far, "c")
    across = swap(jnp.stack([same[1], near[1]]), "y")
    first = jnp.concatenate([same[:1], near[:1], across], axis=0)
    return first, swap(first, "x")


def on_device(
    block_input,
    cotangent,
    doc_lengths,
    layernorm_gain,
    layernorm_bias,
    qkv_weight,
    qkv_bias,
    fc1_weight,
    fc1_bias,
    dense_weight,
    fc2_weight,
    out_bias,
):
    x, zh, zl = lax.axis_index("x"), lax.axis_index("zh"), lax.axis_index("zl")
    here = 2 * lax.axis_index("y") + lax.axis_index("c")
    place = jnp.stack([here ^ r for r in range(4)]).astype(jnp.int32)
    sx = x.astype(jnp.int32).reshape(1)
    sz = zl.astype(jnp.int32).reshape(1)

    tokens = lax.all_gather(block_input, ("zl", "y", "c"), axis=0, tiled=False)
    cotangents = lax.all_gather(cotangent, ("zl", "y", "c"), axis=0, tiled=False)

    order = jnp.stack([here ^ r for r in (1, 3, 2, 0)]).astype(jnp.int32)
    near, same, far = pack(order, sx, qkv_weight, fc1_weight, dense_weight, fc2_weight)
    near = swap(near, "c")
    weights = {"own": {}, "other": {}}
    for at, name in enumerate(("fc2", "fc1", "att")):
        rows = slice(512 * at, 512 * at + 512)
        across = swap(jnp.stack([far[rows], near[1, rows]]), "y")
        pieces = (same[rows], near[0, rows], across[0], across[1])
        halves = [
            jnp.concatenate([piece[256 * s : 256 * s + 256] for piece in pieces], axis=1)
            for s in range(2)
        ]
        weights["own"][name] = halves
        first = swap(halves[0], "zh")
        weights["other"][name] = [first, swap(first, "x")]

    scale = jnp.stack([layernorm_gain, layernorm_bias])
    scale = jnp.concatenate([scale, swap(scale, "c")], axis=0)
    scale = jnp.concatenate([scale, swap(scale, "y")], axis=0)
    heads_bias = qkv_bias.reshape(3, 2, HEAD_DIM)
    units_bias = fc1_bias.reshape(2, 256)
    heads_bias = jnp.where(x == 0, heads_bias, heads_bias[:, ::-1])
    units_bias = jnp.where(x == 0, units_bias, units_bias[::-1])
    bias = jnp.concatenate([heads_bias.reshape(1, 384), units_bias.reshape(1, 512)], axis=1)
    biases = {"own": bias, "other": swap(bias, "zh")}

    lengths = lax.dynamic_index_in_dim(doc_lengths, zh, 0, keepdims=False)
    ends = jnp.cumsum(lengths)
    spot = jnp.arange(SEQ, dtype=jnp.int32)
    begin = jnp.sum(jnp.where(spot[:, None] >= ends[None, :], lengths[None, :], 0), axis=1)
    low = (begin[::BLOCK] // BLOCK).astype(jnp.int32)
    start = jnp.broadcast_to(begin[:, None], (SEQ, 128)).astype(jnp.int32)
    freqs = jnp.exp(jnp.arange(ROT // 2, dtype=F32) * (-2.0 * math.log(10000.0) / ROT))
    angle = spot.astype(F32)[:, None] * freqs[None, :]
    cosine, sine = jnp.cos(angle), jnp.sin(angle)
    ones, none = jnp.ones((SEQ, ROT), F32), jnp.zeros((SEQ, ROT // 2), F32)
    tables = jnp.stack(
        [
            jnp.concatenate([cosine, cosine, ones] * 2, axis=1),
            jnp.concatenate([-sine, none, none, none] * 2, axis=1),
            jnp.concatenate([none, sine, none, none] * 2, axis=1),
        ]
    )

    normed, stats = norm_tokens(place, tokens.reshape(2, 4, SEQ // 2, 512), scale)
    cot = order_tokens(place, cotangents.reshape(2, 4, SEQ // 2, 512))

    done = {}
    for block in ("own", "other"):
        w, b = weights[block], biases[block]
        act, dfc, mlp0, mlp1, unit_sums = mlp(normed, cot, w["fc2"], w["fc1"], b[:, 384:])
        q, k, v, d = heads(normed, cot, w["att"], b[:, :384], tables)
        o, dq, dk, dv, head_sums = attend(low, q, k, v, d, start, tables)
        att0, att1 = att_grad(normed, cot, dq, dk, dv, o)
        sums = jnp.concatenate([head_sums[:3].reshape(1, 384), unit_sums], axis=1)
        done[block] = (act, dfc, o, dq, dk, dv, (mlp0, mlp1), (att0, att1), sums)
    own, other = done["own"], done["other"]

    def all_rows(block, name, first, size):
        return [(part, first, size) for part in weights[block][name]]

    branch = scatter_sum(
        *project(
            sz,
            [(own[0], all_rows("own", "fc2", 0, 256)), (other[0], all_rows("other", "fc2", 0, 256))]
            + [(own[2], all_rows("own", "att", 192, 64)), (other[2], all_rows("other", "att", 192, 64))],
        )
    )
    items = [(own[1], all_rows("own", "fc1", 0, 256)), (other[1], all_rows("other", "fc1", 0, 256))]
    for block, values in (("own", own), ("other", other)):
        for part in range(3):
            items.append((values[3 + part], all_rows(block, "att", 64 * part, 64)))
    normed_gradient = scatter_sum(*project(sz, items))

    input_single = block_input.astype(F32)
    result = (input_single + (branch + out_bias)).astype(BF)

    grad_order = place
    fc1_grad, fc2_grad = unpack_mlp(grad_order, sx, *reduce_grad(own[6], other[6]))
    qkv_grad, dense_grad = unpack_att(grad_order, sx, *reduce_grad(own[7], other[7]))

    sums = own[8] + swap(other[8], "zh")
    heads_sum, units_sum = sums[0, :384].reshape(3, 2, HEAD_DIM), sums[0, 384:].reshape(2, 256)
    heads_sum = jnp.where(x == 0, heads_sum, heads_sum[:, ::-1]).reshape(1, 384)
    units_sum = jnp.where(x == 0, units_sum, units_sum[::-1]).reshape(1, 512)
    sums = jnp.concatenate([heads_sum, units_sum], axis=1)
    sums = more_dp(sums + swap(sums, "x"))
    qkv_bias_grad, fc1_bias_grad = sums[0, :384].reshape(3, 128), sums[0, 384:]

    branch_gradient = cotangent.astype(F32)
    mine = lax.dynamic_slice_in_dim(stats, zl * (SEQ // 2), SEQ // 2, axis=0)
    average, inverse = mine[:, :1], mine[:, 128:129]
    centered = (input_single - average) * inverse
    centered_gradient = normed_gradient * layernorm_gain
    row_sums = jnp.stack(
        [jnp.sum(centered_gradient, axis=1), jnp.sum(centered_gradient * centered, axis=1)]
    )
    row_sums = row_sums + swap(row_sums, "c")
    row_sums = row_sums + swap(row_sums, "y")
    input_grad = branch_gradient + inverse * (
        centered_gradient
        - row_sums[0][:, None] / MODEL_WIDTH
        - centered * (row_sums[1][:, None] / MODEL_WIDTH)
    )
    col_sums = jnp.stack(
        [
            jnp.sum(normed_gradient * centered, axis=0),
            jnp.sum(normed_gradient, axis=0),
            jnp.sum(branch_gradient, axis=0),
        ]
    )
    for axis in ("zl", "zh", "x"):
        col_sums = col_sums + swap(col_sums, axis)
    col_sums = more_dp(col_sums)
    return (
        result,
        input_grad,
        col_sums[0],
        col_sums[1],
        qkv_grad,
        qkv_bias_grad,
        fc1_grad,
        fc1_bias_grad,
        dense_grad,
        fc2_grad,
        col_sums[2],
    )


def solution(mesh):
    dp, row, col = mesh.devices.shape
    assert dp % 2 == 0 and row == 4 and col == 4
    parts = Mesh(
        mesh.devices.reshape(dp // 2, 2, 2, 2, 2, 2), ("xo", "x", "zh", "zl", "y", "c")
    )
    data, rows, cols = ("xo", "x"), ("zh", "zl"), ("y", "c")
    return jax.shard_map(
        on_device,
        mesh=parts,
        in_specs=(
            P(data + rows, cols),
            P(data + rows, cols),
            P(data, None),
            P(cols),
            P(cols),
            P(None, rows, cols),
            P(None, rows + cols),
            P(rows, cols),
            P(rows + cols),
            P(cols, rows),
            P(cols, rows),
            P(cols),
        ),
        out_specs=(
            P(data + rows, cols),
            P(data + rows, cols),
            P(cols),
            P(cols),
            P(None, rows, cols),
            P(None, rows + cols),
            P(rows, cols),
            P(rows + cols),
            P(cols, rows),
            P(cols, rows),
            P(cols),
        ),
        check_vma=False,
    )
```

```python
import math

import jax
import jax.numpy as jnp
from jax import lax
from jax.experimental import pallas as pl
from jax.experimental.pallas import tpu as pltpu
from jax.sharding import Mesh
from jax.sharding import PartitionSpec as P

MODEL_WIDTH = 2048
HEAD_DIM = 64
ROT = 32
SEQ = 2048
EPSILON = 1e-05
MASKED = -1e30
SCALE = HEAD_DIM ** (-0.5)
VMEM = 60 * 1024 * 1024

BF = jnp.bfloat16
F32 = jnp.float32


def swap(value, axis):
    return lax.ppermute(value, axis, [(0, 1), (1, 0)])


def swap_all(values, axis):
    return [swap(value, axis) for value in values]


def nt(left, right):
    return lax.dot_general(left, right, (((1,), (1,)), ((), ())), preferred_element_type=F32)


def tn(left, right):
    return lax.dot_general(left, right, (((0,), (0,)), ((), ())), preferred_element_type=F32)


def nn(left, right):
    return lax.dot_general(left, right, (((1,), (0,)), ((), ())), preferred_element_type=F32)


def shape(*dims, dtype=BF):
    return jax.ShapeDtypeStruct(dims, dtype)


def whole(*dims):
    return pl.BlockSpec(dims, lambda *_: (0,) * len(dims))


def call(body, grid, inputs, outputs, scratch=(), prefetch=(), after=(), carry=()):
    count, waits, kept = len(prefetch) + len(inputs), len(after) + len(carry), len(carry)
    results = len(outputs)

    def kernel(*refs):
        own, rest = refs[:count], refs[count + waits :]
        body(*own, *rest[:results], *rest[results + kept :])

    anywhere = pl.BlockSpec(memory_space=pl.ANY)
    results_ = pl.pallas_call(
        kernel,
        grid_spec=pltpu.PrefetchScalarGridSpec(
            num_scalar_prefetch=len(prefetch),
            grid=grid,
            in_specs=[spec for _, spec in inputs] + [anywhere] * waits,
            out_specs=[spec for _, spec in outputs] + [anywhere] * kept,
            scratch_shapes=list(scratch),
        ),
        out_shape=[out for out, _ in outputs] + [shape(*c.shape, dtype=c.dtype) for c in carry],
        input_output_aliases={count + len(after) + i: results + i for i in range(kept)},
        compiler_params=pltpu.CompilerParams(vmem_limit_bytes=VMEM),
        cost_estimate=pl.CostEstimate(flops=1000, bytes_accessed=1000, transcendentals=0),
    )(*prefetch, *[value for value, _ in inputs], *after, *carry)
    return list(results_)


def pack_kernel(order, sx, qkv, fc1, dense, fc2, near1, near3, far2, own):
    step = pl.program_id(0)
    x = sx[0]

    def write(put, parts):
        fc2_t = fc2[...].T
        dense_t = dense[...].T
        for s in range(parts):

            def pick(low, high, s=s):
                return jnp.where(x == s, low, high)

            put(s, 0, pick(fc2_t[:256], fc2_t[256:]))
            put(s, 256, pick(fc1[:256], fc1[256:]))
            for part in range(3):
                put(s, 512 + 64 * part, pick(qkv[part, :64], qkv[part, 64:]))
            put(s, 704, pick(dense_t[:64], dense_t[64:]))

    def both(ref):
        def put(s, row, value):
            ref[s, row : row + value.shape[0], :] = value

        return put

    def one(ref):
        def put(s, row, value):
            ref[row : row + value.shape[0], :] = value

        return put

    for at, (ref, parts) in enumerate(((near3, 1), (near1, 2), (far2, 1), (own, 2))):

        @pl.when(step == at)
        def _(ref=ref, parts=parts):
            write(both(ref) if parts == 2 else one(ref), parts)


def pack(order, sx, qkv, fc1, dense, fc2):
    return call(
        pack_kernel,
        (4,),
        [
            (qkv, pl.BlockSpec((3, 128, 512), lambda i, o, x: (0, o[i], 0))),
            (fc1, pl.BlockSpec((512, 512), lambda i, o, x: (o[i], 0))),
            (dense, pl.BlockSpec((512, 128), lambda i, o, x: (0, o[i]))),
            (fc2, pl.BlockSpec((512, 512), lambda i, o, x: (0, o[i]))),
        ],
        [
            (shape(2, 768, 512), whole(2, 768, 512)),
            (shape(768, 512), whole(768, 512)),
            (shape(768, 512), whole(768, 512)),
            (shape(2, 768, 512), whole(2, 768, 512)),
        ],
        prefetch=(order, sx),
    )


def stack(items, after=()):
    rows = items[0][3]

    def body(*refs):
        out = refs[-1]
        for at, ((_, lead, first, _), ref) in enumerate(zip(items, refs[:-1], strict=True)):
            if isinstance(lead, slice):
                size = ref.shape[1]
                for k in range(lead.start, lead.stop):
                    out[at, size * (k - lead.start) : size * (k - lead.start + 1), :] = ref[k]
            else:
                out[at] = ref[lead, first : first + rows, :]

    return call(
        body,
        (1,),
        [(array, whole(*array.shape)) for array, _, _, _ in items],
        [(shape(len(items), rows, 512), whole(len(items), rows, 512))],
        after=after,
    )[0]


def split_first(far2, near3, own, near1, after=()):
    def body(far2, near3, own, near1, to_y, att_y, z_mlp):
        for at, ref in enumerate((far2, near3)):
            to_y[at] = ref[:512, :]
            att_y[at] = ref[512:, :]
        for at, ref in enumerate((own, near1)):
            z_mlp[at] = ref[0, :512, :]

    flat, deep = whole(768, 512), whole(1, 768, 512)
    mlp_out = (shape(2, 512, 512), whole(2, 512, 512))
    return call(
        body,
        (1,),
        [(far2, flat), (near3, flat), (own, deep), (near1, deep)],
        [mlp_out, (shape(2, 256, 512), whole(2, 256, 512)), mlp_out],
        after=after,
    )


def stack_att(own, near1, far, after=()):
    def body(own, near1, far, out):
        for at, ref in enumerate((own, near1)):
            out[at] = ref[0, 512:, :]
            out[2 + at] = far[at]

    deep = whole(1, 768, 512)
    return call(
        body,
        (1,),
        [(own, deep), (near1, deep), (far, whole(2, 256, 512))],
        [(shape(4, 256, 512), whole(4, 256, 512))],
        after=after,
    )[0]


def gate(after, carry):
    def body(out):
        out[...] = jnp.zeros_like(out)

    token, *carry = call(
        body, (1,), [], [(shape(8, 128, dtype=F32), whole(8, 128))], after=after, carry=carry
    )
    return token, carry


def piece(array, lead, row, rows=256):
    return (
        array,
        pl.BlockSpec(
            (1, rows, 512),
            lambda *_: (lead, row, 0),
            pipeline_mode=pl.Buffered(buffer_count=1),
        ),
    )


def unpack_mlp_kernel(place, sx, first, second, fc1_out, fc2_out):
    x = sx[0]
    a, b = first[0].astype(F32), second[0].astype(F32)
    low, high = jnp.where(x == 0, a, b), jnp.where(x == 0, b, a)
    fc1_out[:256, :] = low[256:]
    fc1_out[256:, :] = high[256:]
    fc2_out[:, :256] = low[:256].T
    fc2_out[:, 256:] = high[:256].T


def unpack_mlp(place, sx, first, second, after=()):
    block = pl.BlockSpec((1, 512, 512), lambda i, o, x: (o[i], 0, 0))
    return call(
        unpack_mlp_kernel,
        (4,),
        [(first, block), (second, block)],
        [
            (shape(2048, 512, dtype=F32), pl.BlockSpec((512, 512), lambda i, o, x: (i, 0))),
            (shape(512, 2048, dtype=F32), pl.BlockSpec((512, 512), lambda i, o, x: (0, i))),
        ],
        prefetch=(place, sx),
        after=after,
    )


def unpack_att_kernel(place, sx, first, second, qkv_out, dense_out):
    x = sx[0]
    a, b = first[0].astype(F32), second[0].astype(F32)
    low, high = jnp.where(x == 0, a, b), jnp.where(x == 0, b, a)
    for part in range(3):
        qkv_out[part, :64, :] = low[64 * part : 64 * part + 64]
        qkv_out[part, 64:, :] = high[64 * part : 64 * part + 64]
    dense_out[...] = jnp.concatenate([low[192:], high[192:]], axis=0).T


def unpack_att(place, sx, first, second, after=()):
    block = pl.BlockSpec((1, 256, 512), lambda i, o, x: (o[i], 0, 0))
    return call(
        unpack_att_kernel,
        (4,),
        [(first, block), (second, block)],
        [
            (shape(3, 512, 512, dtype=F32), pl.BlockSpec((3, 128, 512), lambda i, o, x: (0, i, 0))),
            (shape(512, 512, dtype=F32), pl.BlockSpec((512, 128), lambda i, o, x: (0, i))),
        ],
        prefetch=(place, sx),
        after=after,
    )


def norm_kernel(place, xs, scale, normed, stats):
    total = jnp.zeros((256, 1), F32)
    square = jnp.zeros((256, 1), F32)
    for q in range(4):
        value = xs[0, q].astype(F32)
        total += jnp.sum(value, axis=1, keepdims=True)
        square += jnp.sum(value * value, axis=1, keepdims=True)
    average = total / MODEL_WIDTH
    inverse = lax.rsqrt(square / MODEL_WIDTH - average * average + EPSILON)
    for r in range(4):
        value = xs[0, place[r]].astype(F32)
        centered = (value - average) * inverse
        normed[:, 512 * r : 512 * r + 512] = (
            centered * scale[2 * r : 2 * r + 1, :] + scale[2 * r + 1 : 2 * r + 2, :]
        ).astype(BF)
    stats[:, :128] = jnp.broadcast_to(average, (256, 128))
    stats[:, 128:] = jnp.broadcast_to(inverse, (256, 128))


def norm_tokens(place, gathered, scale, after=()):
    return call(
        norm_kernel,
        (8,),
        [
            (gathered, pl.BlockSpec((1, 4, 256, 512), lambda i, o: (i // 4, 0, i % 4, 0))),
            (scale, whole(8, 512)),
        ],
        [
            (shape(SEQ, MODEL_WIDTH), pl.BlockSpec((256, 2048), lambda i, o: (i, 0))),
            (shape(SEQ, 256, dtype=F32), pl.BlockSpec((256, 256), lambda i, o: (i, 0))),
        ],
        prefetch=(place,),
        after=after,
    )


ROOT = math.sqrt(2.0 / math.pi)
CUBIC = 0.044715
TILE = 512
HALF = SEQ // 2


def token_inputs(normed, cot):
    per = HALF // TILE
    return [
        (normed, pl.BlockSpec((TILE, MODEL_WIDTH), lambda i, *_: (i, 0))),
        (cot, pl.BlockSpec((1, 4, TILE, 512), lambda i, *_: (i // per, 0, i % per, 0))),
    ]


def store_grad(out, row, value):
    for at, r in enumerate((0, 2, 1, 3)):
        out[at, row : row + value.shape[0], :] = value[:, 512 * r : 512 * r + 512].astype(BF)


def mlp_kernel(place, n, c, *refs):
    weights, (bias, act_out, dfc_out, *grads, sums, w1, w2, acc1, acc2) = refs[:8], refs[8:]
    step = pl.program_id(0)

    @pl.when(step == 0)
    def _():
        acc1[...] = jnp.zeros_like(acc1)
        acc2[...] = jnp.zeros_like(acc2)
        sums[...] = jnp.zeros_like(sums)
        for s in range(2):
            for r in range(4):
                rows, cols = slice(256 * s, 256 * s + 256), slice(512 * r, 512 * r + 512)
                w2[rows, cols] = weights[4 * s + r][0, :256, :]
                w1[rows, cols] = weights[4 * s + r][0, 256:, :]

    pre = nt(n[...], w1[...]) + bias[...]
    back = jnp.zeros((TILE, 512), F32)
    for r in range(4):
        back += nt(c[0, place[r]], w2[:, 512 * r : 512 * r + 512])
    square = pre * pre
    angle = jnp.tanh(ROOT * pre * (1.0 + CUBIC * square))
    half = 0.5 * (1.0 + angle)
    act = (pre * half).astype(BF)
    slope = half + 0.5 * pre * (1.0 - angle * angle) * (ROOT * (1.0 + 3.0 * CUBIC * square))
    dfc = back * slope
    sums[...] += jnp.sum(dfc, axis=0, keepdims=True)
    dfc = dfc.astype(BF)
    act_out[...] = act
    dfc_out[...] = dfc
    for r in range(4):
        acc2[:, 512 * r : 512 * r + 512] += tn(act, c[0, place[r]])
    acc1[...] += tn(dfc, n[...])

    @pl.when(step == SEQ // TILE - 1)
    def _():
        for s in range(2):
            store_grad(grads[s], 0, acc2[256 * s : 256 * s + 256])
            store_grad(grads[2 + s], 0, acc1[256 * s : 256 * s + 256])


def mlp(place, normed, cot, weights, bias, after=(), carry=()):
    units = pl.BlockSpec((TILE, 512), lambda i, *_: (i, 0))
    grad = (shape(4, 256, 512), whole(4, 256, 512))
    return call(
        mlp_kernel,
        (SEQ // TILE,),
        token_inputs(normed, cot)
        + [piece(array, lead, 0, 512) for array, lead in weights]
        + [(bias, whole(1, 512))],
        [(shape(SEQ, 512), units)] * 2
        + [grad] * 4
        + [(shape(1, 512, dtype=F32), whole(1, 512))],
        [
            pltpu.VMEM((512, MODEL_WIDTH), BF),
            pltpu.VMEM((512, MODEL_WIDTH), BF),
            pltpu.VMEM((512, MODEL_WIDTH), F32),
            pltpu.VMEM((512, MODEL_WIDTH), F32),
        ],
        prefetch=(place,),
        after=after,
        carry=carry,
    )


def rotated(value, tables, sign):
    return (
        value * tables[0]
        + pltpu.roll(value, 112, 1) * (sign * tables[1])
        + pltpu.roll(value, 16, 1) * (sign * tables[2])
    )


def heads_kernel(place, n, c, *refs):
    weights, (bias, tables, q_out, k_out, v0_out, v1_out, d_out, joined) = refs[:8], refs[8:]

    @pl.when(pl.program_id(0) == 0)
    def _():
        for s in range(2):
            for r in range(4):
                for part in range(4):
                    row = 128 * part + 64 * s
                    joined[row : row + 64, 512 * r : 512 * r + 512] = weights[4 * s + r][
                        0, 64 * part : 64 * part + 64, :
                    ]

    pre = nt(n[...], joined[:384]) + bias[...]
    q_out[...] = (rotated(pre[:, :128], tables, 1.0) * SCALE).astype(BF)
    k_out[...] = rotated(pre[:, 128:256], tables, 1.0).astype(BF)
    value = pre[:, 256:].astype(BF)
    lane = lax.broadcasted_iota(jnp.int32, value.shape, 1)
    one = jnp.ones_like(value)
    v0_out[...] = jnp.where(lane < HEAD_DIM, value, one)
    v1_out[...] = jnp.where(lane < HEAD_DIM, one, value)
    back = jnp.zeros((TILE, 128), F32)
    for r in range(4):
        back += nt(c[0, place[r]], joined[384:, 512 * r : 512 * r + 512])
    d_out[...] = back.astype(BF)


def heads(place, normed, cot, weights, bias, tables, after=()):
    head = pl.BlockSpec((TILE, 128), lambda i, *_: (i, 0))
    return call(
        heads_kernel,
        (SEQ // TILE,),
        token_inputs(normed, cot)
        + [piece(*weight) for weight in weights]
        + [
            (bias, whole(1, 384)),
            (tables, pl.BlockSpec((3, TILE, 128), lambda i, *_: (0, i, 0))),
        ],
        [(shape(SEQ, 128), head)] * 5,
        [pltpu.VMEM((512, MODEL_WIDTH), BF)],
        prefetch=(place,),
        after=after,
    )


BLOCK = 512
BLOCKS = SEQ // BLOCK


def attend_kernel(
    low, q, k, v0, v1, d, start, tables, o_out, dq_out, dk_out, dv_out, sums, scores, probs, dk_acc, dv_acc
):
    i = pl.program_id(0)

    @pl.when(i == 0)
    def _():
        dk_acc[...] = jnp.zeros_like(dk_acc)
        dv_acc[...] = jnp.zeros_like(dv_acc)
        sums[...] = jnp.zeros_like(sums)

    lane = lax.broadcasted_iota(jnp.int32, (BLOCK, 128), 1)
    masks = (lane < HEAD_DIM, lane >= HEAD_DIM)
    zero = jnp.zeros((BLOCK, 128), BF)
    queries = [jnp.where(m, q[...], zero) for m in masks]
    values = (v0, v1)
    col = lax.broadcasted_iota(jnp.int32, (BLOCK, BLOCK), 1)
    row = lax.broadcasted_iota(jnp.int32, (BLOCK, BLOCK), 0) + i * BLOCK
    begin = start[:, :1]

    def at(j):
        return pl.ds(pl.multiple_of(j * BLOCK, BLOCK), BLOCK)

    def score(j, peaks):
        keys = k[at(j), :]
        here = col + j * BLOCK
        allowed = (here >= begin) & (here <= row)
        new = []
        for h in range(2):
            s = jnp.where(allowed, nt(queries[h], keys), MASKED)
            scores[h, j] = s
            peak = peaks[h]
            for lanes in range(0, BLOCK, 128):
                peak = jnp.maximum(peak, s[:, lanes : lanes + 128])
            new.append(peak)
        return tuple(new)

    floor = jnp.full((BLOCK, 128), MASKED, F32)
    peaks = lax.fori_loop(low[i], i + 1, score, (floor, floor))
    peaks = [jnp.max(p, axis=1, keepdims=True) for p in peaks]

    def weigh(j, outs):
        new = []
        for h in range(2):
            p = jnp.exp(scores[h, j] - peaks[h]).astype(BF)
            probs[h, j] = p
            new.append(outs[h] + nn(p, values[h][at(j), :]))
        return tuple(new)

    blank = jnp.zeros((BLOCK, 128), F32)
    outs = lax.fori_loop(low[i], i + 1, weigh, (blank, blank))
    inverse = [1.0 / outs[0][:, HEAD_DIM : HEAD_DIM + 1], 1.0 / outs[1][:, :1]]
    outs = [outs[h] * inverse[h] for h in range(2)]
    o_out[...] = jnp.where(masks[0], outs[0], outs[1]).astype(BF)

    grads, shifted = [], []
    for h in range(2):
        grad = jnp.where(masks[h], d[...].astype(F32) * inverse[h], 0.0).astype(BF)
        wide = grad.astype(F32)
        delta = jnp.sum(wide * outs[h], axis=1, keepdims=True)
        coarse = delta.astype(BF).astype(F32)
        first = HEAD_DIM * (1 - h)
        wide = jnp.where(lane == first, -coarse, wide)
        shifted.append(jnp.where(lane == first + 1, coarse - delta, wide).astype(BF))
        grads.append(grad)

    def back(j, carry):
        keys = k[at(j), :]
        new = []
        dk, dv = dk_acc[at(j), :], dv_acc[at(j), :]
        for h in range(2):
            p = probs[h, j]
            d_scores = (p.astype(F32) * nt(shifted[h], values[h][at(j), :])).astype(BF)
            new.append(carry[h] + nn(d_scores, keys))
            dk += tn(d_scores, queries[h])
            dv += tn(p, grads[h])
        dk_acc[at(j), :] = dk
        dv_acc[at(j), :] = dv
        return tuple(new)

    dq = lax.fori_loop(low[i], i + 1, back, (blank, blank))
    dq = jnp.where(masks[0], dq[0], dq[1]) * SCALE
    dq = rotated(dq, [tables[t, at(i), :] for t in range(3)], -1.0)
    dq_out[...] = dq.astype(BF)
    sums[0:1, :] += jnp.sum(dq, axis=0, keepdims=True)

    @pl.when(i == BLOCKS - 1)
    def _():
        for j in range(8):
            rows = slice(j * 256, j * 256 + 256)
            dk = rotated(dk_acc[rows], [tables[t, rows] for t in range(3)], -1.0)
            dv = dv_acc[rows]
            dk_out[rows, :] = dk.astype(BF)
            dv_out[rows, :] = dv.astype(BF)
            sums[1:2, :] += jnp.sum(dk, axis=0, keepdims=True)
            sums[2:3, :] += jnp.sum(dv, axis=0, keepdims=True)


def attend(low, q, k, v0, v1, d, start, tables, after=()):
    tile = pl.BlockSpec((BLOCK, 128), lambda i, o: (i, 0))
    full = whole(SEQ, 128)
    head = shape(SEQ, 128)
    return call(
        attend_kernel,
        (BLOCKS,),
        [
            (q, tile),
            (k, full),
            (v0, full),
            (v1, full),
            (d, tile),
            (start, tile),
            (tables, whole(3, SEQ, 128)),
        ],
        [
            (head, tile),
            (head, tile),
            (head, full),
            (head, full),
            (shape(8, 128, dtype=F32), whole(8, 128)),
        ],
        [
            pltpu.VMEM((2, BLOCKS, BLOCK, BLOCK), F32),
            pltpu.VMEM((2, BLOCKS, BLOCK, BLOCK), BF),
            pltpu.VMEM((SEQ, 128), F32),
            pltpu.VMEM((SEQ, 128), F32),
        ],
        prefetch=(low,),
        after=after,
    )


def att_grad_kernel(place, n, c, dq, dk, dv, o, grad0, grad1, grad2, acc):
    step = pl.program_id(0)

    @pl.when(step == 0)
    def _():
        acc[...] = jnp.zeros_like(acc)

    acc[:384] += tn(jnp.concatenate([dq[...], dk[...], dv[...]], axis=1), n[...])
    for r in range(4):
        acc[384:, 512 * r : 512 * r + 512] += tn(o[...], c[0, place[r]])

    @pl.when(step == SEQ // TILE - 1)
    def _():
        for part in range(4):
            row, rows = 128 * part, slice(64 * part, 64 * part + 64)
            store_grad(grad0, 64 * part, acc[row : row + 64])
            value = acc[row + 64 : row + 128]
            for at, (grad, r) in enumerate(((grad1, 0), (grad1, 2), (grad2, 1), (grad2, 3))):
                grad[at % 2, rows, :] = value[:, 512 * r : 512 * r + 512].astype(BF)


def att_grad(place, normed, cot, dq, dk, dv, o, after=()):
    head = pl.BlockSpec((TILE, 128), lambda i, *_: (i, 0))
    return call(
        att_grad_kernel,
        (SEQ // TILE,),
        token_inputs(normed, cot) + [(value, head) for value in (dq, dk, dv, o)],
        [(shape(4, 256, 512), whole(4, 256, 512))] + [(shape(2, 256, 512), whole(2, 256, 512))] * 2,
        [pltpu.VMEM((512, MODEL_WIDTH), F32)],
        prefetch=(place,),
        after=after,
    )


def join(joined, spans, rights):
    row = 0
    for at, (first, size) in enumerate(spans):
        for r in range(4):
            joined[row : row + size, 512 * r : 512 * r + 512] = rights[4 * at + r][
                0, first : first + size, :
            ]
        row += size


def project(prefetch, items, tokens, outputs, store, after=()):
    lefts = [left for left, _ in items]
    parts = [part for _, rows in items for part in rows]
    spans = [(first, size) for _, first, size in parts]
    rights = [piece(*one) for pieces, _, _ in parts for one in pieces]

    def body(*refs):
        scalars, refs = refs[: len(prefetch)], refs[len(prefetch) :]
        left_refs, refs = refs[: len(lefts)], refs[len(lefts) :]
        right_refs, refs = refs[: len(rights)], refs[len(rights) :]
        *outs, joined = refs

        @pl.when(pl.program_id(0) == 0)
        def _():
            join(joined, spans, right_refs)

        left = jnp.concatenate([ref[...] for ref in left_refs], axis=1)
        store(scalars, outs, lambda r: nn(left, joined[:, 512 * r : 512 * r + 512]).astype(BF))

    return call(
        body,
        (SEQ // TILE,),
        [(left, pl.BlockSpec((TILE, left.shape[1]), tokens)) for left in lefts] + rights,
        outputs,
        [pltpu.VMEM((sum(size for _, size in spans), MODEL_WIDTH), BF)],
        prefetch=prefetch,
        after=after,
    )


def project_near(sz, items, after=()):
    per = HALF // TILE

    def store(scalars, outs, value):
        for out, pieces in zip(outs, ((1, 3), (0, 2)), strict=True):
            for at, r in enumerate(pieces):
                out[at, 0] = value(r)

    out = pl.BlockSpec((2, 1, TILE, 512), lambda i, *_: (0, i // per, i % per, 0))
    return project(
        (sz,),
        items,
        lambda i, s: (((i // per) ^ s[0]) * per + i % per, 0),
        [(shape(2, 2, HALF, 512), out)] * 2,
        store,
        after,
    )


def added(values):
    total = values[0].astype(F32)
    for value in values[1:]:
        total = total + value.astype(F32)
    return total.astype(BF)


def grad_inputs(values):
    block = pl.BlockSpec((1, 256, 512), lambda i: (i, 0, 0))
    inputs, reads = [], []
    for value in values:
        at = len(inputs)
        if isinstance(value, list):
            inputs += [(one, whole(2, 256, 512)) for one in value]
            reads.append(lambda refs, step, at=at: refs[at + step // 2][step % 2])
        else:
            inputs.append((value, block))
            reads.append(lambda refs, step, at=at: refs[at][0])
    return inputs, reads


def add(left, right, after=()):
    inputs, reads = grad_inputs([left, right])

    def body(*refs):
        for step in range(4):

            @pl.when(pl.program_id(0) == step)
            def _(step=step):
                refs[-1][0] = added([read(refs, step) for read in reads])

    block = pl.BlockSpec((1, 256, 512), lambda i: (i, 0, 0))
    return call(body, (4,), inputs, [(shape(4, 256, 512), block)], after=after)


def total_grad(groups, after=()):
    inputs, reads = [], []
    for group in groups:
        found, read = grad_inputs(group)
        reads.append((len(inputs), len(found), read))
        inputs += found
    rows = 256 * len(groups)

    def body(*refs):
        near, same = refs[-2:]
        for step in range(4):

            @pl.when(pl.program_id(0) == step)
            def _(step=step):
                out = same if step < 2 else near
                for g, (at, size, read) in enumerate(reads):
                    mine = refs[at : at + size]
                    out[step % 2, 256 * g : 256 * g + 256, :] = added([one(mine, step) for one in read])

    out = (shape(2, rows, 512), whole(2, rows, 512))
    return call(body, (4,), inputs, [out, out], after=after)


def quarters(value):
    return [value[256 * k : 256 * k + 256, :] for k in range(value.shape[0] // 256)]


def received(same, near, to_z, to_y, own, for_y, for_z, at=0):
    own[...] = added([same[0, 0], near[0, 0]])
    for_z[...] = added([same[0, 1], near[0, 1]])
    for_y[...] = added([same[1, 0], near[1, 0]])
    far = quarters(added([same[1, 1], near[1, 1]]))
    for k in range(2):
        to_z[at + k] = far[k]
        to_y[at + k] = far[2 + k]


def passed_on(for_y, from_z, for_z, from_y, to_y, to_z, at=0):
    for k in range(4):
        rows = slice(256 * k, 256 * k + 256)
        to_y[k] = added([for_y[rows, :], from_z[at + k]]) if k < 2 else for_y[rows, :]
        to_z[k] = added([for_z[rows, :], from_y[at + k - 2]]) if k >= 2 else for_z[rows, :]


def blocks(count):
    return (shape(count, 256, 512), whole(count, 256, 512))


def scatter_first(same, near, grad_same, grad_near, after=()):
    def body(same, near, grad_same, grad_near, to_z, to_y, own, for_y, for_z):
        received(same, near, to_z, to_y, own, for_y, for_z)
        for at, ref in enumerate((grad_same, grad_near)):
            to_y[2 + 2 * at] = ref[1, :256, :]
            to_y[3 + 2 * at] = ref[1, 256:, :]

    both, pair = whole(2, 2, HALF, 512), whole(2, 512, 512)
    full = (shape(HALF, 512), whole(HALF, 512))
    return call(
        body,
        (1,),
        [(same, both), (near, both), (grad_same, pair), (grad_near, pair)],
        [blocks(2), blocks(6), full, full, full],
        after=after,
    )


def scatter_both(for_y, from_z, for_z, from_y, same, near, grad_same, grad_near, after=()):
    def body(for_y, from_z, for_z, from_y, same, near, grad_same, grad_near, to_z, to_y, *kept):
        passed_on(for_y, from_z, for_z, from_y, to_y, to_z)
        received(same, near, to_z, to_y, *kept, at=4)
        to_y[6] = grad_same[1]
        to_y[7] = grad_near[1]

    both, pair = whole(2, 2, HALF, 512), whole(2, 256, 512)
    flat, full = whole(HALF, 512), (shape(HALF, 512), whole(HALF, 512))
    return call(
        body,
        (1,),
        [
            (for_y, flat),
            (from_z, pair),
            (for_z, flat),
            (from_y, whole(6, 256, 512)),
            (same, both),
            (near, both),
            (grad_same, pair),
            (grad_near, pair),
        ],
        [blocks(6), blocks(8), full, full, full],
        after=after,
    )


def scatter_last(for_y, from_z, for_z, from_y, after=()):
    def body(for_y, from_z, for_z, from_y, to_z, to_y):
        passed_on(for_y, from_z, for_z, from_y, to_y, to_z, at=4)

    flat = whole(HALF, 512)
    return call(
        body,
        (1,),
        [
            (for_y, flat),
            (from_z, whole(6, 256, 512)),
            (for_z, flat),
            (from_y, whole(8, 256, 512)),
        ],
        [blocks(4), blocks(4)],
        after=after,
    )


def more_dp(value):
    if lax.axis_size("xo") > 1:
        return lax.psum(value, "xo")
    return value


def on_device(
    block_input,
    cotangent,
    doc_lengths,
    layernorm_gain,
    layernorm_bias,
    qkv_weight,
    qkv_bias,
    fc1_weight,
    fc1_bias,
    dense_weight,
    fc2_weight,
    out_bias,
):
    x, zh, zl = lax.axis_index("x"), lax.axis_index("zh"), lax.axis_index("zl")
    here = 2 * lax.axis_index("y") + lax.axis_index("c")
    place = jnp.stack([here ^ r for r in range(4)]).astype(jnp.int32)
    sx = x.astype(jnp.int32).reshape(1)
    sz = zl.astype(jnp.int32).reshape(1)

    tokens = lax.all_gather(block_input, ("zl", "y", "c"), axis=0, tiled=False)
    cot = lax.all_gather(cotangent, ("zl", "y", "c"), axis=0, tiled=False)
    tokens, cot = (value.reshape(2, 4, HALF, 512) for value in (tokens, cot))

    scale = jnp.stack([layernorm_gain, layernorm_bias])
    scale = jnp.concatenate([scale, swap(scale, "c")], axis=0)
    heads_bias = qkv_bias.reshape(3, 2, HEAD_DIM)
    units_bias = fc1_bias.reshape(2, 256)
    heads_bias = jnp.where(x == 0, heads_bias, heads_bias[:, ::-1])
    units_bias = jnp.where(x == 0, units_bias, units_bias[::-1])
    own_bias = jnp.concatenate([heads_bias.reshape(1, 384), units_bias.reshape(1, 512)], axis=1)
    other_bias = swap(own_bias, "zh")

    order = jnp.stack([here ^ r for r in (3, 1, 2, 0)]).astype(jnp.int32)
    near1, near3, far2, r0 = pack(order, sx, qkv_weight, fc1_weight, dense_weight, fc2_weight)
    near3 = swap(near3, "c")
    r1 = swap(near1, "c")

    lengths = lax.dynamic_index_in_dim(doc_lengths, zh, 0, keepdims=False)
    ends = jnp.cumsum(lengths)
    spot = jnp.arange(SEQ, dtype=jnp.int32)
    begin = jnp.sum(jnp.where(spot[:, None] >= ends[None, :], lengths[None, :], 0), axis=1)
    low = (begin[::BLOCK] // BLOCK).astype(jnp.int32)
    start = jnp.broadcast_to(begin[:, None], (SEQ, 128)).astype(jnp.int32)
    freqs = jnp.exp(jnp.arange(ROT // 2, dtype=F32) * (-2.0 * math.log(10000.0) / ROT))
    angle = spot.astype(F32)[:, None] * freqs[None, :]
    cosine, sine = jnp.cos(angle), jnp.sin(angle)
    ones, none = jnp.ones((SEQ, ROT), F32), jnp.zeros((SEQ, ROT // 2), F32)
    tables = jnp.stack(
        [
            jnp.concatenate([cosine, cosine, ones] * 2, axis=1),
            jnp.concatenate([-sine, none, none, none] * 2, axis=1),
            jnp.concatenate([none, sine, none, none] * 2, axis=1),
        ]
    )

    def rows(weights, row, first, size):
        return [
            ([(*one[:2], one[2] if row is None else row) for one in weights[4 * s : 4 * s + 4]], first, size)
            for s in range(2)
        ]

    input_single = block_input.astype(F32)
    branch_gradient = cotangent.astype(F32)

    to_y, att_y, other01 = split_first(far2, near3, r0, r1, after=[scale, other_bias])
    r23, other01, att23 = swap(to_y, "y"), swap(other01, "zh"), swap(att_y, "y")
    scale = jnp.concatenate([scale, swap(scale, "y")], axis=0)
    token, (r23, att23, other01) = gate([to_y, scale, tables, start], [r23, att23, other01])

    other23 = swap(r23, "zh")
    own23, next01 = swap(r23, "x"), swap(other01, "x")
    other_r = stack_att(r0, r1, att23, after=[token])
    normed, stats = norm_tokens(place, tokens, scale, after=[token, other_r])
    token, (other23, own23, next01) = gate([stats], [other23, own23, next01])
    mine = lax.dynamic_slice_in_dim(stats, zl * HALF, HALF, axis=0)
    average, inverse = mine[:, :1], mine[:, 128:129]
    centered = (input_single - average) * inverse

    other_r = swap(other_r, "zh")
    next23, next_att23 = swap(other23, "x"), swap(att23, "x")
    own_w = [(r0, 0), (r1, 0), (r23, 0), (r23, 1), (r0, 1), (r1, 1), (own23, 0), (own23, 1)]
    other_w = [(array, i) for array in (other01, other23, next01, next23) for i in range(2)]
    own_act, own_dfc, *own_mlp, own_units = mlp(
        place, normed, cot, own_w, own_bias[:, 384:], after=[token]
    )
    token, (other_r, next23, next_att23, *own_mlp) = gate(
        [own_units], [other_r, next23, next_att23, *own_mlp]
    )
    other_w[6:] = [(next23, 0), (next23, 1)]

    next_r = swap(other_r, "x")
    other_act, other_dfc, *other_mlp, other_units = mlp(
        place, normed, cot, other_w, other_bias[:, 384:], after=[token]
    )
    token, (next_r, *other_mlp) = gate([other_units], [next_r, *other_mlp])

    own_a = [(r0, 0, 2), (r1, 0, 2), (att23, 0, 0), (att23, 1, 0)]
    own_a += [(r0, 1, 2), (r1, 1, 2), (next_att23, 0, 0), (next_att23, 1, 0)]
    other_a = [(array, i, 0) for array in (other_r, next_r) for i in range(4)]
    from_x = swap(other_mlp[1], "x")
    own_heads = heads(place, normed, cot, own_a, own_bias[:, :384], tables, after=[token])
    other_heads = heads(
        place, normed, cot, other_a, other_bias[:, :384], tables, after=[own_heads[0]]
    )
    token, (from_x, other_mlp[3], own_mlp[1]) = gate(
        [other_heads[0]], [from_x, other_mlp[3], own_mlp[1]]
    )

    fc2 = add(other_mlp[0], from_x, after=[token])[0]
    to_fc2 = swap(fc2, "zh")
    from_x, own_fc2 = swap(other_mlp[3], "x"), swap(own_mlp[1], "x")
    other_o, other_dq, other_dk, other_dv, other_sums = attend(
        low, *other_heads, start, tables, after=[fc2]
    )
    other_att = att_grad(
        place, normed, cot, other_dq, other_dk, other_dv, other_o, after=[other_sums]
    )
    other_sums = jnp.concatenate([other_sums[:3].reshape(1, 384), other_units], axis=1)
    token, (to_fc2, from_x, own_fc2, other_att[1], other_att[2], own_mlp[3], other_sums) = gate(
        [other_att[0]], [to_fc2, from_x, own_fc2, *other_att[1:], own_mlp[3], other_sums]
    )

    fc1 = add(other_mlp[2], from_x, after=[token])[0]
    to_fc1 = swap(fc1, "zh")
    other_sums = swap(other_sums, "zh")
    from_x, own_fc1 = swap_all(other_att[1:], "x"), swap(own_mlp[3], "x")
    own_o, own_dq, own_dk, own_dv, own_sums = attend(
        low, *own_heads, start, tables, after=[fc1]
    )
    items = [(own_dfc, rows(own_w, 1, 0, 256)), (other_dfc, rows(other_w, 1, 0, 256))]
    for part, (left, right) in enumerate(
        ((own_dq, other_dq), (own_dk, other_dk), (own_dv, other_dv))
    ):
        items.append((left, rows(own_a, None, 64 * part, 64)))
        items.append((right, rows(other_a, None, 64 * part, 64)))
    dn_near, dn_same = project_near(sz, items, after=[own_sums])
    own_sums = jnp.concatenate([own_sums[:3].reshape(1, 384), own_units], axis=1)
    token, (to_fc1, from_x[0], from_x[1], own_fc1, other_sums, dn_near) = gate(
        [dn_same, own_sums], [to_fc1, *from_x, own_fc1, other_sums, dn_near]
    )

    dn_near = swap(dn_near, "c")
    mlp_near, mlp_same = total_grad(
        [[own_mlp[0], own_fc2, to_fc2], [own_mlp[2], own_fc1, to_fc1]], after=[token]
    )
    mlp_near, mlp_same = swap(more_dp(mlp_near), "c"), more_dp(mlp_same)
    att = add(other_att[0], from_x, after=[mlp_same])[0]
    to_att = swap(att, "zh")
    own_att = att_grad(place, normed, cot, own_dq, own_dk, own_dv, own_o, after=[att])
    own_from_att = swap_all(own_att[1:], "x")
    items = [
        (own_act, rows(own_w, 0, 0, 256)),
        (other_act, rows(other_w, 0, 0, 256)),
        (own_o, rows(own_a, None, 192, 64)),
        (other_o, rows(other_a, None, 192, 64)),
    ]
    near, same = project_near(sz, items, after=[own_att[0]])
    sums = own_sums + other_sums
    heads_sum, units_sum = sums[0, :384].reshape(3, 2, HEAD_DIM), sums[0, 384:].reshape(2, 256)
    heads_sum = jnp.where(x == 0, heads_sum, heads_sum[:, ::-1]).reshape(1, 384)
    units_sum = jnp.where(x == 0, units_sum, units_sum[::-1]).reshape(1, 512)
    sums = jnp.concatenate([heads_sum, units_sum], axis=1)
    token, (to_att, own_from_att[0], own_from_att[1], mlp_near, dn_near, near) = gate(
        [same], [to_att, *own_from_att, mlp_near, dn_near, near]
    )

    near = swap(near, "c")
    to_z, to_y, dn, for_y, for_z = scatter_first(dn_same, dn_near, mlp_same, mlp_near, after=[token])
    from_z, from_y = swap(to_z, "zl"), swap(to_y, "y")
    att_near, att_same = total_grad([[own_att[0], own_from_att, to_att]], after=[dn])
    att_near, att_same = swap(more_dp(att_near), "c"), more_dp(att_same)
    token, (near, from_z, from_y, att_near) = gate([att_same], [near, from_z, from_y, att_near])

    to_z, to_y, branch, branch_y, branch_z = scatter_both(
        for_y, from_z, for_z, from_y, same, near, att_same, att_near, after=[token]
    )
    dn_z, dn_y = swap(to_z, "zl"), swap(to_y, "y")
    mlp_first = stack(
        [(mlp_same, 0, 0, 512), (mlp_near, 0, 0, 512), (from_y, slice(2, 4), 0, 512)]
        + [(from_y, slice(4, 6), 0, 512)],
        after=[to_y],
    )
    mlp_second, sums_x = swap(mlp_first, "x"), swap(sums, "x")
    token, (dn_y, dn_z, mlp_second, sums_x) = gate(
        [mlp_first, sums], [dn_y, dn_z, mlp_second, sums_x]
    )

    dn = dn.astype(F32) + dn_y[:4].reshape(HALF, 512).astype(F32) + dn_z[:4].reshape(HALF, 512).astype(F32)
    row_sums = jnp.stack(
        [jnp.sum(dn * layernorm_gain, axis=1), jnp.sum(dn * layernorm_gain * centered, axis=1)]
    )
    row_sums = row_sums + swap(row_sums, "c")
    row_sums = row_sums + swap(row_sums, "y")
    to_z, to_y = scatter_last(branch_y, dn_z, branch_z, dn_y, after=[token, row_sums])
    branch_z, branch_y = swap(to_z, "zl"), swap(to_y, "y")
    att_first = stack(
        [(att_same, 0, 0, 256), (att_near, 0, 0, 256), (dn_y, 6, 0, 256), (dn_y, 7, 0, 256)],
        after=[to_y],
    )
    att_second = swap(att_first, "x")
    fc1_grad, fc2_grad = unpack_mlp(place, sx, mlp_first, mlp_second, after=[att_first])
    qkv_grad, dense_grad = unpack_att(place, sx, att_first, att_second, after=[fc1_grad])
    sums = more_dp(sums + sums_x)

    qkv_bias_grad, fc1_bias_grad = sums[0, :384].reshape(3, 128), sums[0, 384:]

    branch = branch.astype(F32) + branch_y.reshape(HALF, 512).astype(F32) + branch_z.reshape(HALF, 512).astype(F32)
    result = (input_single + (branch + out_bias)).astype(BF)
    input_grad = branch_gradient + inverse * (
        dn * layernorm_gain
        - row_sums[0][:, None] / MODEL_WIDTH
        - centered * (row_sums[1][:, None] / MODEL_WIDTH)
    )
    col_sums = jnp.stack(
        [
            jnp.sum(dn * centered, axis=0),
            jnp.sum(dn, axis=0),
            jnp.sum(branch_gradient, axis=0),
        ]
    )
    for axis in ("zl", "zh", "x"):
        col_sums = col_sums + swap(col_sums, axis)
    col_sums = more_dp(col_sums)
    return (
        result,
        input_grad,
        col_sums[0],
        col_sums[1],
        qkv_grad,
        qkv_bias_grad,
        fc1_grad,
        fc1_bias_grad,
        dense_grad,
        fc2_grad,
        col_sums[2],
    )


def solution(mesh):
    dp, row, col = mesh.devices.shape
    assert dp % 2 == 0 and row == 4 and col == 4
    parts = Mesh(
        mesh.devices.reshape(dp // 2, 2, 2, 2, 2, 2), ("xo", "x", "zh", "zl", "y", "c")
    )
    data, rows, cols = ("xo", "x"), ("zh", "zl"), ("y", "c")
    return jax.shard_map(
        on_device,
        mesh=parts,
        in_specs=(
            P(data + rows, cols),
            P(data + rows, cols),
            P(data, None),
            P(cols),
            P(cols),
            P(None, rows, cols),
            P(None, rows + cols),
            P(rows, cols),
            P(rows + cols),
            P(cols, rows),
            P(cols, rows),
            P(cols),
        ),
        out_specs=(
            P(data + rows, cols),
            P(data + rows, cols),
            P(cols),
            P(cols),
            P(None, rows, cols),
            P(None, rows + cols),
            P(rows, cols),
            P(rows + cols),
            P(cols, rows),
            P(cols, rows),
            P(cols),
        ),
        check_vma=False,
    )
```

```python
import math

import jax
import jax.numpy as jnp
from jax import lax
from jax.experimental import pallas as pl
from jax.experimental.pallas import tpu as pltpu
from jax.sharding import Mesh
from jax.sharding import PartitionSpec as P

MODEL_WIDTH = 2048
HEAD_DIM = 64
ROT = 32
SEQ = 2048
EPSILON = 1e-05
MASKED = -1e30
SCALE = HEAD_DIM ** (-0.5)
VMEM = 60 * 1024 * 1024

BF = jnp.bfloat16
F32 = jnp.float32


def swap(value, axis):
    return lax.ppermute(value, axis, [(0, 1), (1, 0)])


def swap_all(values, axis):
    return [swap(value, axis) for value in values]


def nt(left, right):
    return lax.dot_general(left, right, (((1,), (1,)), ((), ())), preferred_element_type=F32)


def tn(left, right):
    return lax.dot_general(left, right, (((0,), (0,)), ((), ())), preferred_element_type=F32)


def nn(left, right):
    return lax.dot_general(left, right, (((1,), (0,)), ((), ())), preferred_element_type=F32)


def shape(*dims, dtype=BF):
    return jax.ShapeDtypeStruct(dims, dtype)


def whole(*dims):
    return pl.BlockSpec(dims, lambda *_: (0,) * len(dims))


def call(body, grid, inputs, outputs, scratch=(), prefetch=(), after=(), carry=()):
    count, waits, kept = len(prefetch) + len(inputs), len(after) + len(carry), len(carry)
    results = len(outputs)

    def kernel(*refs):
        own, rest = refs[:count], refs[count + waits :]
        body(*own, *rest[:results], *rest[results + kept :])

    anywhere = pl.BlockSpec(memory_space=pl.ANY)
    results_ = pl.pallas_call(
        kernel,
        grid_spec=pltpu.PrefetchScalarGridSpec(
            num_scalar_prefetch=len(prefetch),
            grid=grid,
            in_specs=[spec for _, spec in inputs] + [anywhere] * waits,
            out_specs=[spec for _, spec in outputs] + [anywhere] * kept,
            scratch_shapes=list(scratch),
        ),
        out_shape=[out for out, _ in outputs] + [shape(*c.shape, dtype=c.dtype) for c in carry],
        input_output_aliases={count + len(after) + i: results + i for i in range(kept)},
        compiler_params=pltpu.CompilerParams(vmem_limit_bytes=VMEM),
        cost_estimate=pl.CostEstimate(flops=1000, bytes_accessed=1000, transcendentals=0),
    )(*prefetch, *[value for value, _ in inputs], *after, *carry)
    return list(results_)


def pack_kernel(order, sx, qkv, fc1, dense, fc2, near1, near3, far2, own):
    step = pl.program_id(0)
    x = sx[0]

    def write(put, parts):
        fc2_t = fc2[...].T
        dense_t = dense[...].T
        for s in range(parts):

            def pick(low, high, s=s):
                return jnp.where(x == s, low, high)

            put(s, 0, pick(fc2_t[:256], fc2_t[256:]))
            put(s, 256, pick(fc1[:256], fc1[256:]))
            for part in range(3):
                put(s, 512 + 64 * part, pick(qkv[part, :64], qkv[part, 64:]))
            put(s, 704, pick(dense_t[:64], dense_t[64:]))

    def both(ref):
        def put(s, row, value):
            ref[s, row : row + value.shape[0], :] = value

        return put

    def one(ref):
        def put(s, row, value):
            ref[row : row + value.shape[0], :] = value

        return put

    for at, (ref, parts) in enumerate(((near3, 1), (near1, 2), (far2, 1), (own, 2))):

        @pl.when(step == at)
        def _(ref=ref, parts=parts):
            write(both(ref) if parts == 2 else one(ref), parts)


def pack(order, sx, qkv, fc1, dense, fc2):
    return call(
        pack_kernel,
        (4,),
        [
            (qkv, pl.BlockSpec((3, 128, 512), lambda i, o, x: (0, o[i], 0))),
            (fc1, pl.BlockSpec((512, 512), lambda i, o, x: (o[i], 0))),
            (dense, pl.BlockSpec((512, 128), lambda i, o, x: (0, o[i]))),
            (fc2, pl.BlockSpec((512, 512), lambda i, o, x: (0, o[i]))),
        ],
        [
            (shape(2, 768, 512), whole(2, 768, 512)),
            (shape(768, 512), whole(768, 512)),
            (shape(768, 512), whole(768, 512)),
            (shape(2, 768, 512), whole(2, 768, 512)),
        ],
        prefetch=(order, sx),
    )


def split_first(far2, near3, own, near1, after=()):
    def body(far2, near3, own, near1, to_y, att_y, z_mlp, z_att):
        for at, ref in enumerate((far2, near3)):
            to_y[at] = ref[:512, :]
            att_y[at] = ref[512:, :]
        for at, ref in enumerate((own, near1)):
            z_mlp[at] = ref[0, :512, :]
            z_att[at] = ref[0, 512:, :]

    flat, deep = whole(768, 512), whole(1, 768, 512)
    mlp_out = (shape(2, 512, 512), whole(2, 512, 512))
    att_out = (shape(2, 256, 512), whole(2, 256, 512))
    return call(
        body,
        (1,),
        [(far2, flat), (near3, flat), (own, deep), (near1, deep)],
        [mlp_out, att_out, mlp_out, att_out],
        after=after,
    )


def gate(after, carry):
    def body(out):
        out[...] = jnp.zeros_like(out)

    token, *carry = call(
        body, (1,), [], [(shape(8, 128, dtype=F32), whole(8, 128))], after=after, carry=carry
    )
    return token, carry


def piece(array, lead, row, rows=256):
    return (
        array,
        pl.BlockSpec(
            (1, rows, 512),
            lambda *_: (lead, row, 0),
            pipeline_mode=pl.Buffered(buffer_count=1),
        ),
    )


def unpack(place, sx, pieces, select, outputs, store, after=()):
    def body(place, sx, *refs):
        for r in range(4):

            @pl.when(place[pl.program_id(0)] == r)
            def _(r=r):
                a = select(refs[r // 2], r % 2).astype(F32)
                b = select(refs[2 + r // 2], r % 2).astype(F32)
                store(jnp.where(sx[0] == 0, a, b), jnp.where(sx[0] == 0, b, a), *refs[4:])

    return call(
        body,
        (4,),
        [(value, whole(*value.shape)) for value in pieces],
        outputs,
        prefetch=(place, sx),
        after=after,
    )


def unpack_fc2(place, sx, pieces, after=()):
    def store(low, high, out):
        out[:, :256] = low.T
        out[:, 256:] = high.T

    block = pl.BlockSpec((512, 512), lambda i, o, x: (0, i))
    out = [(shape(512, 2048, dtype=F32), block)]
    return unpack(place, sx, pieces, lambda ref, k: ref[2 * k], out, store, after)[0]


def unpack_fc1(place, sx, pieces, after=()):
    def store(low, high, out):
        out[:256, :] = low
        out[256:, :] = high

    block = pl.BlockSpec((512, 512), lambda i, o, x: (i, 0))
    out = [(shape(2048, 512, dtype=F32), block)]
    return unpack(place, sx, pieces, lambda ref, k: ref[2 * k + 1], out, store, after)[0]


def unpack_att(place, sx, pieces, after=()):
    def store(low, high, qkv_out, dense_out):
        for part in range(3):
            qkv_out[part, :64, :] = low[64 * part : 64 * part + 64]
            qkv_out[part, 64:, :] = high[64 * part : 64 * part + 64]
        dense_out[...] = jnp.concatenate([low[192:], high[192:]], axis=0).T

    outputs = [
        (shape(3, 512, 512, dtype=F32), pl.BlockSpec((3, 128, 512), lambda i, o, x: (0, i, 0))),
        (shape(512, 512, dtype=F32), pl.BlockSpec((512, 128), lambda i, o, x: (0, i))),
    ]
    return unpack(place, sx, pieces, lambda ref, k: ref[k], outputs, store, after)


def norm_kernel(place, xs, scale, normed, stats):
    total = jnp.zeros((256, 1), F32)
    square = jnp.zeros((256, 1), F32)
    for q in range(4):
        value = xs[0, q].astype(F32)
        total += jnp.sum(value, axis=1, keepdims=True)
        square += jnp.sum(value * value, axis=1, keepdims=True)
    average = total / MODEL_WIDTH
    inverse = lax.rsqrt(square / MODEL_WIDTH - average * average + EPSILON)
    for r in range(4):
        value = xs[0, place[r]].astype(F32)
        centered = (value - average) * inverse
        normed[:, 512 * r : 512 * r + 512] = (
            centered * scale[2 * r : 2 * r + 1, :] + scale[2 * r + 1 : 2 * r + 2, :]
        ).astype(BF)
    stats[:, :128] = jnp.broadcast_to(average, (256, 128))
    stats[:, 128:] = jnp.broadcast_to(inverse, (256, 128))


def norm_tokens(place, gathered, scale, after=()):
    return call(
        norm_kernel,
        (8,),
        [
            (gathered, pl.BlockSpec((1, 4, 256, 512), lambda i, o: (i // 4, 0, i % 4, 0))),
            (scale, whole(8, 512)),
        ],
        [
            (shape(SEQ, MODEL_WIDTH), pl.BlockSpec((256, 2048), lambda i, o: (i, 0))),
            (shape(SEQ, 256, dtype=F32), pl.BlockSpec((256, 256), lambda i, o: (i, 0))),
        ],
        prefetch=(place,),
        after=after,
    )


ROOT = math.sqrt(2.0 / math.pi)
CUBIC = 0.044715
TILE = 512
HALF = SEQ // 2


def token_inputs(normed, cot):
    per = HALF // TILE
    return [
        (normed, pl.BlockSpec((TILE, MODEL_WIDTH), lambda i, *_: (i, 0))),
        (cot, pl.BlockSpec((1, 4, TILE, 512), lambda i, *_: (i // per, 0, i % per, 0))),
    ]


def store_grad(out, row, value):
    for at, r in enumerate((0, 2, 1, 3)):
        out[at, row : row + value.shape[0], :] = value[:, 512 * r : 512 * r + 512].astype(BF)


def mlp_kernel(place, n, c, *refs):
    weights, (bias, act_out, dfc_out, *grads, sums, w1, w2, acc1, acc2) = refs[:8], refs[8:]
    step = pl.program_id(0)

    @pl.when(step == 0)
    def _():
        acc1[...] = jnp.zeros_like(acc1)
        acc2[...] = jnp.zeros_like(acc2)
        sums[...] = jnp.zeros_like(sums)
        for s in range(2):
            for r in range(4):
                rows, cols = slice(256 * s, 256 * s + 256), slice(512 * r, 512 * r + 512)
                w2[rows, cols] = weights[4 * s + r][0, :256, :]
                w1[rows, cols] = weights[4 * s + r][0, 256:, :]

    pre = nt(n[...], w1[...]) + bias[...]
    back = jnp.zeros((TILE, 512), F32)
    for r in range(4):
        back += nt(c[0, place[r]], w2[:, 512 * r : 512 * r + 512])
    square = pre * pre
    angle = jnp.tanh(ROOT * pre * (1.0 + CUBIC * square))
    half = 0.5 * (1.0 + angle)
    act = (pre * half).astype(BF)
    slope = half + 0.5 * pre * (1.0 - angle * angle) * (ROOT * (1.0 + 3.0 * CUBIC * square))
    dfc = back * slope
    sums[...] += jnp.sum(dfc, axis=0, keepdims=True)
    dfc = dfc.astype(BF)
    act_out[...] = act
    dfc_out[...] = dfc
    for r in range(4):
        acc2[:, 512 * r : 512 * r + 512] += tn(act, c[0, place[r]])
    acc1[...] += tn(dfc, n[...])

    @pl.when(step == SEQ // TILE - 1)
    def _():
        for s in range(2):
            store_grad(grads[s], 0, acc2[256 * s : 256 * s + 256])
            store_grad(grads[2 + s], 0, acc1[256 * s : 256 * s + 256])


def mlp(place, normed, cot, weights, bias, after=(), carry=()):
    units = pl.BlockSpec((TILE, 512), lambda i, *_: (i, 0))
    grad = (shape(4, 256, 512), whole(4, 256, 512))
    return call(
        mlp_kernel,
        (SEQ // TILE,),
        token_inputs(normed, cot)
        + [piece(array, lead, 0, 512) for array, lead in weights]
        + [(bias, whole(1, 512))],
        [(shape(SEQ, 512), units)] * 2
        + [grad] * 4
        + [(shape(1, 512, dtype=F32), whole(1, 512))],
        [
            pltpu.VMEM((512, MODEL_WIDTH), BF),
            pltpu.VMEM((512, MODEL_WIDTH), BF),
            pltpu.VMEM((512, MODEL_WIDTH), F32),
            pltpu.VMEM((512, MODEL_WIDTH), F32),
        ],
        prefetch=(place,),
        after=after,
        carry=carry,
    )


def rotated(value, tables, sign):
    return (
        value * tables[0]
        + pltpu.roll(value, 112, 1) * (sign * tables[1])
        + pltpu.roll(value, 16, 1) * (sign * tables[2])
    )


def heads_kernel(place, n, c, *refs):
    weights, refs = refs[:16], refs[16:]
    bias, tables, *outs, joined = refs

    @pl.when(pl.program_id(0) == 0)
    def _():
        for block in range(2):
            for s in range(2):
                for r in range(4):
                    for part in range(4):
                        row = 384 * block + 128 * part if part < 3 else 768 + 128 * block
                        row += 64 * s
                        joined[row : row + 64, 512 * r : 512 * r + 512] = weights[
                            8 * block + 4 * s + r
                        ][0, 64 * part : 64 * part + 64, :]

    pre = nt(n[...], joined[:768]) + bias[...]
    back = jnp.zeros((TILE, 256), F32)
    for r in range(4):
        back += nt(c[0, place[r]], joined[768:, 512 * r : 512 * r + 512])
    lane = lax.broadcasted_iota(jnp.int32, (TILE, 128), 1)
    one = jnp.ones((TILE, 128), BF)
    for block in range(2):
        q_out, k_out, v0_out, v1_out, d_out = outs[5 * block : 5 * block + 5]
        mine = pre[:, 384 * block : 384 * block + 384]
        q_out[...] = (rotated(mine[:, :128], tables, 1.0) * SCALE).astype(BF)
        k_out[...] = rotated(mine[:, 128:256], tables, 1.0).astype(BF)
        value = mine[:, 256:].astype(BF)
        v0_out[...] = jnp.where(lane < HEAD_DIM, value, one)
        v1_out[...] = jnp.where(lane < HEAD_DIM, one, value)
        d_out[...] = back[:, 128 * block : 128 * block + 128].astype(BF)


def heads(place, normed, cot, weights, bias, tables, after=()):
    head = pl.BlockSpec((TILE, 128), lambda i, *_: (i, 0))
    return call(
        heads_kernel,
        (SEQ // TILE,),
        token_inputs(normed, cot)
        + [piece(*weight) for weight in weights]
        + [
            (bias, whole(1, 768)),
            (tables, pl.BlockSpec((3, TILE, 128), lambda i, *_: (0, i, 0))),
        ],
        [(shape(SEQ, 128), head)] * 10,
        [pltpu.VMEM((1024, MODEL_WIDTH), BF)],
        prefetch=(place,),
        after=after,
    )


BLOCK = 512
BLOCKS = SEQ // BLOCK


def attend_kernel(low, *refs):
    ins, (start, tables), refs = refs[:10], refs[10:12], refs[12:]
    outs, refs = refs[:10], refs[10:]
    scores, probs, dk_acc, dv_acc, peak_acc, o_acc, dq_acc = refs
    i = pl.program_id(0)

    @pl.when(i == 0)
    def _():
        dk_acc[...] = jnp.zeros_like(dk_acc)
        dv_acc[...] = jnp.zeros_like(dv_acc)
        for block in range(2):
            outs[5 * block + 4][...] = jnp.zeros_like(outs[5 * block + 4])

    lane = lax.broadcasted_iota(jnp.int32, (BLOCK, 128), 1)
    masks = (lane < HEAD_DIM, lane >= HEAD_DIM)
    zero = jnp.zeros((BLOCK, 128), BF)
    queries = [jnp.where(masks[h % 2], ins[5 * (h // 2)][...], zero) for h in range(4)]
    keys = [ins[5 * (h // 2) + 1] for h in range(4)]
    values = [ins[5 * (h // 2) + 2 + h % 2] for h in range(4)]
    col = lax.broadcasted_iota(jnp.int32, (BLOCK, BLOCK), 1)
    row = lax.broadcasted_iota(jnp.int32, (BLOCK, BLOCK), 0) + i * BLOCK
    begin = start[:, :1]

    def each(step):
        for j in range(BLOCKS):

            @pl.when((j >= low[i]) & (j <= i))
            def _(j=j):
                step(j, slice(j * BLOCK, j * BLOCK + BLOCK))

    peak_acc[...] = jnp.full_like(peak_acc, MASKED)
    o_acc[...] = jnp.zeros_like(o_acc)
    dq_acc[...] = jnp.zeros_like(dq_acc)

    def score(j, at):
        here = col + j * BLOCK
        allowed = (here >= begin) & (here <= row)
        for h in range(4):
            s = jnp.where(allowed, nt(queries[h], keys[h][at, :]), MASKED)
            scores[h, j] = s
            peak = peak_acc[h]
            for lanes in range(0, BLOCK, 128):
                peak = jnp.maximum(peak, s[:, lanes : lanes + 128])
            peak_acc[h] = peak

    each(score)
    peaks = [jnp.max(peak_acc[h], axis=1, keepdims=True) for h in range(4)]

    def weigh(j, at):
        for h in range(4):
            p = jnp.exp(scores[h, j] - peaks[h]).astype(BF)
            probs[h, j] = p
            o_acc[h] += nn(p, values[h][at, :])

    each(weigh)
    grads, shifted = [], []
    for block in range(2):
        scaled = []
        for h in range(2):
            out = o_acc[2 * block + h]
            first = HEAD_DIM * (1 - h)
            inverse = 1.0 / out[:, first : first + 1]
            out = out * inverse
            grad = jnp.where(masks[h], ins[5 * block + 4][...].astype(F32) * inverse, 0.0).astype(BF)
            wide = grad.astype(F32)
            delta = jnp.sum(wide * out, axis=1, keepdims=True)
            coarse = delta.astype(BF).astype(F32)
            wide = jnp.where(lane == first, -coarse, wide)
            shifted.append(jnp.where(lane == first + 1, coarse - delta, wide).astype(BF))
            grads.append(grad)
            scaled.append(out)
        outs[5 * block][...] = jnp.where(masks[0], *scaled).astype(BF)

    def back(j, at):
        for h in range(4):
            p = probs[h, j]
            d_scores = (p.astype(F32) * nt(shifted[h], values[h][at, :])).astype(BF)
            dq_acc[h] += nn(d_scores, keys[h][at, :])
            dk_acc[h // 2, at, :] += tn(d_scores, queries[h])
            dv_acc[h // 2, at, :] += tn(p, grads[h])

    each(back)
    rows = pl.ds(pl.multiple_of(i * BLOCK, BLOCK), BLOCK)
    for block in range(2):
        dq = jnp.where(masks[0], dq_acc[2 * block], dq_acc[2 * block + 1]) * SCALE
        dq = rotated(dq, [tables[t, rows, :] for t in range(3)], -1.0)
        outs[5 * block + 1][...] = dq.astype(BF)
        outs[5 * block + 4][0:1, :] += jnp.sum(dq, axis=0, keepdims=True)

    @pl.when(i == BLOCKS - 1)
    def _():
        for block in range(2):
            _, _, dk_out, dv_out, sums = outs[5 * block : 5 * block + 5]
            for j in range(8):
                rows = slice(j * 256, j * 256 + 256)
                dk = rotated(dk_acc[block, rows], [tables[t, rows] for t in range(3)], -1.0)
                dv = dv_acc[block, rows]
                dk_out[rows, :] = dk.astype(BF)
                dv_out[rows, :] = dv.astype(BF)
                sums[1:2, :] += jnp.sum(dk, axis=0, keepdims=True)
                sums[2:3, :] += jnp.sum(dv, axis=0, keepdims=True)


def attend(low, heads, start, tables, after=()):
    tile = pl.BlockSpec((BLOCK, 128), lambda i, o: (i, 0))
    full = whole(SEQ, 128)
    head = shape(SEQ, 128)
    return call(
        attend_kernel,
        (BLOCKS,),
        [(value, (tile, full, full, full, tile)[at % 5]) for at, value in enumerate(heads)]
        + [(start, tile), (tables, whole(3, SEQ, 128))],
        [
            (head, tile),
            (head, tile),
            (head, full),
            (head, full),
            (shape(8, 128, dtype=F32), whole(8, 128)),
        ]
        * 2,
        [
            pltpu.VMEM((4, BLOCKS, BLOCK, BLOCK), F32),
            pltpu.VMEM((4, BLOCKS, BLOCK, BLOCK), BF),
            pltpu.VMEM((2, SEQ, 128), F32),
            pltpu.VMEM((2, SEQ, 128), F32),
            pltpu.VMEM((4, BLOCK, 128), F32),
            pltpu.VMEM((4, BLOCK, 128), F32),
            pltpu.VMEM((4, BLOCK, 128), F32),
        ],
        prefetch=(low,),
        after=after,
    )


def att_grad_kernel(place, n, c, dq, dk, dv, o, grad0, grad1, grad2, acc):
    step = pl.program_id(0)

    @pl.when(step == 0)
    def _():
        acc[...] = jnp.zeros_like(acc)

    acc[:384] += tn(jnp.concatenate([dq[...], dk[...], dv[...]], axis=1), n[...])
    for r in range(4):
        acc[384:, 512 * r : 512 * r + 512] += tn(o[...], c[0, place[r]])

    @pl.when(step == SEQ // TILE - 1)
    def _():
        for part in range(4):
            row, rows = 128 * part, slice(64 * part, 64 * part + 64)
            store_grad(grad0, 64 * part, acc[row : row + 64])
            value = acc[row + 64 : row + 128]
            for at, (grad, r) in enumerate(((grad1, 0), (grad1, 2), (grad2, 1), (grad2, 3))):
                grad[at % 2, rows, :] = value[:, 512 * r : 512 * r + 512].astype(BF)


def att_grad(place, normed, cot, dq, dk, dv, o, after=()):
    head = pl.BlockSpec((TILE, 128), lambda i, *_: (i, 0))
    return call(
        att_grad_kernel,
        (SEQ // TILE,),
        token_inputs(normed, cot) + [(value, head) for value in (dq, dk, dv, o)],
        [(shape(4, 256, 512), whole(4, 256, 512))] + [(shape(2, 256, 512), whole(2, 256, 512))] * 2,
        [pltpu.VMEM((512, MODEL_WIDTH), F32)],
        prefetch=(place,),
        after=after,
    )


def join(joined, spans, rights):
    row = 0
    for at, (first, size) in enumerate(spans):
        for r in range(4):
            joined[row : row + size, 512 * r : 512 * r + 512] = rights[4 * at + r][
                0, first : first + size, :
            ]
        row += size


def project(prefetch, items, tokens, outputs, store, after=()):
    lefts = [left for left, _ in items]
    parts = [part for _, rows in items for part in rows]
    spans = [(first, size) for _, first, size in parts]
    rights = [piece(*one) for pieces, _, _ in parts for one in pieces]

    def body(*refs):
        scalars, refs = refs[: len(prefetch)], refs[len(prefetch) :]
        left_refs, refs = refs[: len(lefts)], refs[len(lefts) :]
        right_refs, refs = refs[: len(rights)], refs[len(rights) :]
        *outs, joined = refs

        @pl.when(pl.program_id(0) == 0)
        def _():
            join(joined, spans, right_refs)

        left = jnp.concatenate([ref[...] for ref in left_refs], axis=1)
        store(scalars, outs, lambda r: nn(left, joined[:, 512 * r : 512 * r + 512]).astype(BF))

    return call(
        body,
        (SEQ // TILE,),
        [(left, pl.BlockSpec((TILE, left.shape[1]), tokens)) for left in lefts] + rights,
        outputs,
        [pltpu.VMEM((sum(size for _, size in spans), MODEL_WIDTH), BF)],
        prefetch=prefetch,
        after=after,
    )


def project_near(sz, items, after=()):
    per = HALF // TILE

    def store(scalars, outs, value):
        for out, pieces in zip(outs, ((1, 3), (0, 2)), strict=True):
            for at, r in enumerate(pieces):
                out[at, 0] = value(r)

    out = pl.BlockSpec((2, 1, TILE, 512), lambda i, *_: (0, i // per, i % per, 0))
    return project(
        (sz,),
        items,
        lambda i, s: (((i // per) ^ s[0]) * per + i % per, 0),
        [(shape(2, 2, HALF, 512), out)] * 2,
        store,
        after,
    )


def added(values):
    total = values[0].astype(F32)
    for value in values[1:]:
        total = total + value.astype(F32)
    return total.astype(BF)


def grad_inputs(values):
    inputs, reads = [], []
    for value in values:
        at = len(inputs)
        if isinstance(value, list):
            inputs += [(one, whole(2, 256, 512)) for one in value]
            reads.append(lambda refs, step, at=at: refs[at + step // 2][step % 2])
        else:
            inputs.append((value, whole(4, 256, 512)))
            reads.append(lambda refs, step, at=at: refs[at][step])
    return inputs, reads


def add(left, right, after=()):
    inputs, reads = grad_inputs([left, right])

    def body(*refs):
        for step in range(4):
            refs[-1][step] = added([read(refs, step) for read in reads])

    return call(
        body, (1,), inputs, [(shape(4, 256, 512), whole(4, 256, 512))], after=after
    )


def total_grad(groups, after=()):
    inputs, reads = [], []
    for group in groups:
        found, read = grad_inputs(group)
        reads.append((len(inputs), len(found), read))
        inputs += found
    rows = 256 * len(groups)

    def body(*refs):
        near, same = refs[-2:]
        for step in range(4):
            out = same if step < 2 else near
            for g, (at, size, read) in enumerate(reads):
                mine = refs[at : at + size]
                out[step % 2, 256 * g : 256 * g + 256, :] = added([one(mine, step) for one in read])

    out = (shape(2, rows, 512), whole(2, rows, 512))
    return call(body, (1,), inputs, [out, out], after=after)


def quarters(value):
    return [value[256 * k : 256 * k + 256, :] for k in range(value.shape[0] // 256)]


def received(same, near, far_out, own, for_y, for_z):
    own[...] = added([same[0, 0], near[0, 0]])
    for_z[...] = added([same[0, 1], near[0, 1]])
    for_y[...] = added([same[1, 0], near[1, 0]])
    far = quarters(added([same[1, 1], near[1, 1]]))
    for value, (ref, at) in zip(far, far_out, strict=True):
        ref[at] = value


def blocks(count):
    return (shape(count, 256, 512), whole(count, 256, 512))


FLAT = (shape(HALF, 512), whole(HALF, 512))


def scatter_first(same, near, grad_same, grad_near, after=()):
    def body(same, near, grad_same, grad_near, to_z, to_y, to_x, own, for_y, for_z):
        received(same, near, [(to_z, k) for k in range(4)], own, for_y, for_z)
        for out, at in ((to_x, 0), (to_y, 1)):
            for k, ref in enumerate((grad_same, grad_near)):
                out[2 * k] = ref[at, :256, :]
                out[2 * k + 1] = ref[at, 256:, :]

    both, pair = whole(2, 2, HALF, 512), whole(2, 512, 512)
    return call(
        body,
        (1,),
        [(same, both), (near, both), (grad_same, pair), (grad_near, pair)],
        [blocks(4)] * 3 + [FLAT] * 3,
        after=after,
    )


def scatter_second(for_y, from_z, after=()):
    def body(for_y, from_z, to_y):
        for k in range(4):
            rows = slice(256 * k, 256 * k + 256)
            to_y[rows, :] = added([for_y[rows, :], from_z[k]])

    return call(
        body,
        (1,),
        [(for_y, FLAT[1]), (from_z, whole(4, 256, 512))],
        [FLAT],
        after=after,
    )[0]


def scatter_third(same, near, grad_same, grad_near, after=()):
    def body(same, near, grad_same, grad_near, to_z, to_y, to_x, *kept):
        received(same, near, [(to_z, 0), (to_z, 1), (to_z, 2), (to_y, 0)], *kept)
        for k, ref in enumerate((grad_same, grad_near)):
            to_x[k] = ref[0]
            to_y[1 + k] = ref[1]

    both, pair = whole(2, 2, HALF, 512), whole(2, 256, 512)
    return call(
        body,
        (1,),
        [(same, both), (near, both), (grad_same, pair), (grad_near, pair)],
        [blocks(3), blocks(3), blocks(2)] + [FLAT] * 3,
        after=after,
    )


def scatter_last(for_y, from_z, for_z, from_y, after=()):
    def body(for_y, from_z, for_z, from_y, to_z, to_y, kept):
        for k in range(4):
            rows = slice(256 * k, 256 * k + 256)
            to_y[rows, :] = added([for_y[rows, :], from_z[k]]) if k < 3 else for_y[rows, :]
            to_z[rows, :] = for_z[rows, :] if k < 3 else added([for_z[rows, :], from_y[0]])
        for k in range(2):
            kept[k] = from_y[1 + k]

    three = whole(3, 256, 512)
    return call(
        body,
        (1,),
        [(for_y, FLAT[1]), (from_z, three), (for_z, FLAT[1]), (from_y, three)],
        [FLAT, FLAT, blocks(2)],
        after=after,
    )


def more_dp(value):
    if lax.axis_size("xo") > 1:
        return lax.psum(value, "xo")
    return value


def on_device(
    block_input,
    cotangent,
    doc_lengths,
    layernorm_gain,
    layernorm_bias,
    qkv_weight,
    qkv_bias,
    fc1_weight,
    fc1_bias,
    dense_weight,
    fc2_weight,
    out_bias,
):
    x, zh, zl = lax.axis_index("x"), lax.axis_index("zh"), lax.axis_index("zl")
    here = 2 * lax.axis_index("y") + lax.axis_index("c")
    place = jnp.stack([here ^ r for r in range(4)]).astype(jnp.int32)
    sx = x.astype(jnp.int32).reshape(1)
    sz = zl.astype(jnp.int32).reshape(1)

    tokens = lax.all_gather(block_input, ("zl", "y", "c"), axis=0, tiled=False)
    cot = lax.all_gather(cotangent, ("zl", "y", "c"), axis=0, tiled=False)
    tokens, cot = (value.reshape(2, 4, HALF, 512) for value in (tokens, cot))

    scale = jnp.stack([layernorm_gain, layernorm_bias])
    scale = jnp.concatenate([scale, swap(scale, "c")], axis=0)
    heads_bias = qkv_bias.reshape(3, 2, HEAD_DIM)
    units_bias = fc1_bias.reshape(2, 256)
    heads_bias = jnp.where(x == 0, heads_bias, heads_bias[:, ::-1])
    units_bias = jnp.where(x == 0, units_bias, units_bias[::-1])
    own_bias = jnp.concatenate([heads_bias.reshape(1, 384), units_bias.reshape(1, 512)], axis=1)

    order = jnp.stack([here ^ r for r in (3, 1, 2, 0)]).astype(jnp.int32)
    near1, near3, far2, r0 = pack(order, sx, qkv_weight, fc1_weight, dense_weight, fc2_weight)
    near3 = swap(near3, "c")
    r1 = swap(near1, "c")

    lengths = lax.dynamic_index_in_dim(doc_lengths, zh, 0, keepdims=False)
    ends = jnp.cumsum(lengths)
    spot = jnp.arange(SEQ, dtype=jnp.int32)
    begin = jnp.sum(jnp.where(spot[:, None] >= ends[None, :], lengths[None, :], 0), axis=1)
    low = (begin[::BLOCK] // BLOCK).astype(jnp.int32)
    start = jnp.broadcast_to(begin[:, None], (SEQ, 128)).astype(jnp.int32)
    freqs = jnp.exp(jnp.arange(ROT // 2, dtype=F32) * (-2.0 * math.log(10000.0) / ROT))
    angle = spot.astype(F32)[:, None] * freqs[None, :]
    cosine, sine = jnp.cos(angle), jnp.sin(angle)
    ones, none = jnp.ones((SEQ, ROT), F32), jnp.zeros((SEQ, ROT // 2), F32)
    tables = jnp.stack(
        [
            jnp.concatenate([cosine, cosine, ones] * 2, axis=1),
            jnp.concatenate([-sine, none, none, none] * 2, axis=1),
            jnp.concatenate([none, sine, none, none] * 2, axis=1),
        ]
    )

    def rows(weights, row, first, size):
        return [
            ([(*one[:2], one[2] if row is None else row) for one in weights[4 * s : 4 * s + 4]], first, size)
            for s in range(2)
        ]

    input_single = block_input.astype(F32)
    branch_gradient = cotangent.astype(F32)

    to_y, att_y, other01, att01 = split_first(far2, near3, r0, r1, after=[scale])
    r23, other01 = swap(to_y, "y"), swap(other01, "zh")
    scale = jnp.concatenate([scale, swap(scale, "y")], axis=0)
    other_bias = swap(own_bias, "zh")
    token, (r23, other01, att_y, att01) = gate(
        [to_y, scale, other_bias, tables, start], [r23, other01, att_y, att01]
    )

    other23, att23 = swap(r23, "zh"), swap(att_y, "y")
    own23, next01 = swap(r23, "x"), swap(other01, "x")
    normed, stats = norm_tokens(place, tokens, scale, after=[token])
    token, (other23, att23, att01) = gate([stats, own23, next01], [other23, att23, att01])
    mine = lax.dynamic_slice_in_dim(stats, zl * HALF, HALF, axis=0)
    average, inverse = mine[:, :1], mine[:, 128:129]
    centered = (input_single - average) * inverse

    next23, att01 = swap(other23, "x"), swap(att01, "zh")
    token, (att01, att23) = gate([token, next23], [att01, att23])

    own_w = [(r0, 0), (r1, 0), (r23, 0), (r23, 1), (r0, 1), (r1, 1), (own23, 0), (own23, 1)]
    other_w = [(array, i) for array in (other01, other23, next01, next23) for i in range(2)]
    next_att01, other_att23, next_att23 = swap(att01, "x"), swap(att23, "zh"), swap(att23, "x")
    other_act, other_dfc, *other_mlp, other_units = mlp(
        place, normed, cot, other_w, other_bias[:, 384:], after=[token]
    )
    token, (other_att23, other_mlp[1]) = gate(
        [other_units, next_att01, next_att23], [other_att23, other_mlp[1]]
    )

    from_x, next_other23 = swap(other_mlp[1], "x"), swap(other_att23, "x")
    own_act, own_dfc, *own_mlp, own_units = mlp(
        place, normed, cot, own_w, own_bias[:, 384:], after=[token]
    )
    token, (other_mlp[3], own_mlp[1]) = gate(
        [own_units, from_x, next_other23], [other_mlp[3], own_mlp[1]]
    )

    own_a = [(r0, 0, 2), (r1, 0, 2), (att23, 0, 0), (att23, 1, 0)]
    own_a += [(r0, 1, 2), (r1, 1, 2), (next_att23, 0, 0), (next_att23, 1, 0)]
    other_a = [
        (array, i, 0) for array in (att01, other_att23, next_att01, next_other23) for i in range(2)
    ]
    fc2 = add(other_mlp[0], from_x, after=[token])[0]
    to_fc2 = swap(fc2, "zh")
    from_x, own_fc2 = swap(other_mlp[3], "x"), swap(own_mlp[1], "x")
    bias = jnp.concatenate([own_bias[:, :384], other_bias[:, :384]], axis=1)
    qkv = heads(place, normed, cot, own_a + other_a, bias, tables, after=[fc2])
    attended = attend(low, qkv, start, tables)
    own_o, own_dq, own_dk, own_dv, own_sums = attended[:5]
    other_o, other_dq, other_dk, other_dv, other_sums = attended[5:]
    other_sums = jnp.concatenate([other_sums[:3].reshape(1, 384), other_units], axis=1)
    token, (own_mlp[3], other_sums) = gate(
        [own_o, to_fc2, from_x, own_fc2], [own_mlp[3], other_sums]
    )

    fc1 = add(other_mlp[2], from_x, after=[token])[0]
    to_fc1 = swap(fc1, "zh")
    other_att = att_grad(
        place, normed, cot, other_dq, other_dk, other_dv, other_o, after=[fc1]
    )
    other_sums = swap(other_sums, "zh")
    from_x, own_fc1 = swap_all(other_att[1:], "x"), swap(own_mlp[3], "x")
    items = [(own_dfc, rows(own_w, 1, 0, 256)), (other_dfc, rows(other_w, 1, 0, 256))]
    for part, (left, right) in enumerate(
        ((own_dq, other_dq), (own_dk, other_dk), (own_dv, other_dv))
    ):
        items.append((left, rows(own_a, None, 64 * part, 64)))
        items.append((right, rows(other_a, None, 64 * part, 64)))
    dn_near, dn_same = project_near(sz, items, after=[other_att[0]])
    own_sums = jnp.concatenate([own_sums[:3].reshape(1, 384), own_units], axis=1)
    token, (dn_near,) = gate([dn_same, own_sums, to_fc1, *from_x, own_fc1, other_sums], [dn_near])

    dn_near = swap(dn_near, "c")
    mlp_near, mlp_same = total_grad(
        [[own_mlp[0], own_fc2, to_fc2], [own_mlp[2], own_fc1, to_fc1]], after=[token]
    )
    mlp_near, mlp_same = swap(more_dp(mlp_near), "c"), more_dp(mlp_same)
    att = add(other_att[0], from_x, after=[mlp_same])[0]
    to_att = swap(att, "zh")
    own_att = att_grad(place, normed, cot, own_dq, own_dk, own_dv, own_o, after=[att])
    own_from_att = swap_all(own_att[1:], "x")
    items = [
        (own_act, rows(own_w, 0, 0, 256)),
        (other_act, rows(other_w, 0, 0, 256)),
        (own_o, rows(own_a, None, 192, 64)),
        (other_o, rows(other_a, None, 192, 64)),
    ]
    near, same = project_near(sz, items, after=[own_att[0]])
    sums = own_sums + other_sums
    heads_sum, units_sum = sums[0, :384].reshape(3, 2, HEAD_DIM), sums[0, 384:].reshape(2, 256)
    heads_sum = jnp.where(x == 0, heads_sum, heads_sum[:, ::-1]).reshape(1, 384)
    units_sum = jnp.where(x == 0, units_sum, units_sum[::-1]).reshape(1, 512)
    sums = jnp.concatenate([heads_sum, units_sum], axis=1)
    token, (near,) = gate([same, to_att, *own_from_att, mlp_near, dn_near], [near])

    near = swap(near, "c")
    to_z, to_y, mlp01, dn, for_y, for_z = scatter_first(
        dn_same, dn_near, mlp_same, mlp_near, after=[token]
    )
    from_z, mlp23, next01 = swap(to_z, "zl"), swap(to_y, "y"), swap(mlp01, "x")
    att_near, att_same = total_grad([[own_att[0], own_from_att, to_att]], after=[dn])
    att_near, att_same = swap(more_dp(att_near), "c"), more_dp(att_same)
    token, (mlp23,) = gate([att_same, near, from_z, next01, att_near], [mlp23])

    to_y, to_z = scatter_second(for_y, from_z, after=[token]), for_z
    dn_z, dn_y, next23, sums_x = swap(to_z, "zl"), swap(to_y, "y"), swap(mlp23, "x"), swap(sums, "x")
    to_z, to_y, att01, branch, branch_y, branch_z = scatter_third(
        same, near, att_same, att_near, after=[to_y]
    )
    token, (to_z, to_y, att01) = gate(
        [branch, sums, dn_y, dn_z, next23, sums_x], [to_z, to_y, att01]
    )

    from_z, from_y, next_att01 = swap(to_z, "zl"), swap(to_y, "y"), swap(att01, "x")
    dn = dn.astype(F32) + dn_y.astype(F32) + dn_z.astype(F32)
    row_sums = jnp.stack(
        [jnp.sum(dn * layernorm_gain, axis=1), jnp.sum(dn * layernorm_gain * centered, axis=1)]
    )
    col_sums = jnp.stack(
        [
            jnp.sum(dn * centered, axis=0),
            jnp.sum(dn, axis=0),
            jnp.sum(branch_gradient, axis=0),
        ]
    )
    row_sums = row_sums + swap(row_sums, "c")
    col_sums = col_sums + swap(col_sums, "x")
    token, (row_sums, col_sums) = gate([token, from_z, from_y, next_att01], [row_sums, col_sums])

    row_sums = row_sums + swap(row_sums, "y")
    col_sums = col_sums + swap(col_sums, "zl")
    to_z, to_y, att23 = scatter_last(
        branch_y, from_z, branch_z, from_y, after=[token, row_sums, col_sums]
    )
    col_sums = col_sums + swap(col_sums, "zh")
    branch_z, branch_y, next_att23 = swap(to_z, "zl"), swap(to_y, "y"), swap(att23, "x")
    mlp_pieces = (mlp01, mlp23, next01, next23)
    fc2_grad = unpack_fc2(place, sx, mlp_pieces, after=[to_y])
    fc1_grad = unpack_fc1(place, sx, mlp_pieces, after=[fc2_grad])
    qkv_grad, dense_grad = unpack_att(
        place, sx, (att01, att23, next_att01, next_att23), after=[fc1_grad]
    )
    sums = more_dp(sums + sums_x)

    qkv_bias_grad, fc1_bias_grad = sums[0, :384].reshape(3, 128), sums[0, 384:]

    branch = branch.astype(F32) + branch_y.astype(F32) + branch_z.astype(F32)
    result = (input_single + (branch + out_bias)).astype(BF)
    input_grad = branch_gradient + inverse * (
        dn * layernorm_gain
        - row_sums[0][:, None] / MODEL_WIDTH
        - centered * (row_sums[1][:, None] / MODEL_WIDTH)
    )
    col_sums = more_dp(col_sums)
    return (
        result,
        input_grad,
        col_sums[0],
        col_sums[1],
        qkv_grad,
        qkv_bias_grad,
        fc1_grad,
        fc1_bias_grad,
        dense_grad,
        fc2_grad,
        col_sums[2],
    )


def solution(mesh):
    dp, row, col = mesh.devices.shape
    assert dp % 2 == 0 and row == 4 and col == 4
    parts = Mesh(
        mesh.devices.reshape(dp // 2, 2, 2, 2, 2, 2), ("xo", "x", "zh", "zl", "y", "c")
    )
    data, rows, cols = ("xo", "x"), ("zh", "zl"), ("y", "c")
    return jax.shard_map(
        on_device,
        mesh=parts,
        in_specs=(
            P(data + rows, cols),
            P(data + rows, cols),
            P(data, None),
            P(cols),
            P(cols),
            P(None, rows, cols),
            P(None, rows + cols),
            P(rows, cols),
            P(rows + cols),
            P(cols, rows),
            P(cols, rows),
            P(cols),
        ),
        out_specs=(
            P(data + rows, cols),
            P(data + rows, cols),
            P(cols),
            P(cols),
            P(None, rows, cols),
            P(None, rows + cols),
            P(rows, cols),
            P(rows + cols),
            P(cols, rows),
            P(cols, rows),
            P(cols),
        ),
        check_vma=False,
    )
```

```python
import math

import jax
import jax.numpy as jnp
from jax import lax
from jax.experimental import pallas as pl
from jax.experimental.pallas import tpu as pltpu
from jax.sharding import Mesh
from jax.sharding import PartitionSpec as P

MODEL_WIDTH = 2048
HEAD_DIM = 64
ROT = 32
SEQ = 2048
EPSILON = 1e-05
MASKED = -1e30
SCALE = HEAD_DIM ** (-0.5)
VMEM = 60 * 1024 * 1024
ROOM = 12 * 1024 * 1024

BF = jnp.bfloat16
F32 = jnp.float32


def swap(value, axis):
    return lax.ppermute(value, axis, [(0, 1), (1, 0)])


def swap_all(values, axis):
    return [swap(value, axis) for value in values]


def nt(left, right):
    return lax.dot_general(left, right, (((1,), (1,)), ((), ())), preferred_element_type=F32)


def tn(left, right):
    return lax.dot_general(left, right, (((0,), (0,)), ((), ())), preferred_element_type=F32)


def nn(left, right):
    return lax.dot_general(left, right, (((1,), (0,)), ((), ())), preferred_element_type=F32)


def shape(*dims, dtype=BF):
    return jax.ShapeDtypeStruct(dims, dtype)


def whole(*dims):
    return pl.BlockSpec(dims, lambda *_: (0,) * len(dims))


def call(body, grid, inputs, outputs, scratch=(), prefetch=(), after=(), carry=(), large=False):
    count, waits, kept = len(prefetch) + len(inputs), len(after) + len(carry), len(carry)
    results = len(outputs)

    def kernel(*refs):
        own, rest = refs[:count], refs[count + waits :]
        body(*own, *rest[:results], *rest[results + kept :])

    anywhere = pl.BlockSpec(memory_space=pl.ANY)
    need = sum(math.prod(ref.shape) * jnp.dtype(ref.dtype).itemsize for ref in scratch) + ROOM
    for spec, value in [(spec, value) for value, spec in inputs] + [(spec, out) for out, spec in outputs]:
        once = math.prod(spec.block_shape) * jnp.dtype(value.dtype).itemsize
        need += once if spec.pipeline_mode is not None else 2 * once
    need = VMEM if large else min(need, VMEM)
    results_ = pl.pallas_call(
        kernel,
        grid_spec=pltpu.PrefetchScalarGridSpec(
            num_scalar_prefetch=len(prefetch),
            grid=grid,
            in_specs=[spec for _, spec in inputs] + [anywhere] * waits,
            out_specs=[spec for _, spec in outputs] + [anywhere] * kept,
            scratch_shapes=list(scratch),
        ),
        out_shape=[out for out, _ in outputs] + [shape(*c.shape, dtype=c.dtype) for c in carry],
        input_output_aliases={count + len(after) + i: results + i for i in range(kept)},
        compiler_params=pltpu.CompilerParams(vmem_limit_bytes=need),
        cost_estimate=pl.CostEstimate(flops=1000, bytes_accessed=1000, transcendentals=0),
    )(*prefetch, *[value for value, _ in inputs], *after, *carry)
    return list(results_)


def pack_kernel(order, sx, qkv, fc1, dense, fc2, near1, near3, far2, own):
    step = pl.program_id(0)
    x = sx[0]

    def write(put, parts):
        fc2_t = fc2[...].T
        dense_t = dense[...].T
        for s in range(parts):

            def pick(low, high, s=s):
                return jnp.where(x == s, low, high)

            put(s, 0, pick(fc2_t[:256], fc2_t[256:]))
            put(s, 256, pick(fc1[:256], fc1[256:]))
            for part in range(3):
                put(s, 512 + 64 * part, pick(qkv[part, :64], qkv[part, 64:]))
            put(s, 704, pick(dense_t[:64], dense_t[64:]))

    def both(ref):
        def put(s, row, value):
            ref[s, row : row + value.shape[0], :] = value

        return put

    def one(ref):
        def put(s, row, value):
            ref[row : row + value.shape[0], :] = value

        return put

    for at, (ref, parts) in enumerate(((near3, 1), (near1, 2), (far2, 1), (own, 2))):

        @pl.when(step == at)
        def _(ref=ref, parts=parts):
            write(both(ref) if parts == 2 else one(ref), parts)


def pack(order, sx, qkv, fc1, dense, fc2):
    return call(
        pack_kernel,
        (4,),
        [
            (qkv, pl.BlockSpec((3, 128, 512), lambda i, o, x: (0, o[i], 0))),
            (fc1, pl.BlockSpec((512, 512), lambda i, o, x: (o[i], 0))),
            (dense, pl.BlockSpec((512, 128), lambda i, o, x: (0, o[i]))),
            (fc2, pl.BlockSpec((512, 512), lambda i, o, x: (0, o[i]))),
        ],
        [
            (shape(2, 768, 512), whole(2, 768, 512)),
            (shape(768, 512), whole(768, 512)),
            (shape(768, 512), whole(768, 512)),
            (shape(2, 768, 512), whole(2, 768, 512)),
        ],
        large=True,
        prefetch=(order, sx),
    )


def split_first(far2, near3, own, near1, after=()):
    def body(far2, near3, own, near1, to_y, att_y, z_mlp, z_att):
        for at, ref in enumerate((far2, near3)):
            to_y[at] = ref[:512, :]
            att_y[at] = ref[512:, :]
        for at, ref in enumerate((own, near1)):
            z_mlp[at] = ref[0, :512, :]
            z_att[at] = ref[0, 512:, :]

    flat, deep = whole(768, 512), whole(1, 768, 512)
    mlp_out = (shape(2, 512, 512), whole(2, 512, 512))
    att_out = (shape(2, 256, 512), whole(2, 256, 512))
    return call(
        body,
        (1,),
        [(far2, flat), (near3, flat), (own, deep), (near1, deep)],
        [mlp_out, att_out, mlp_out, att_out],
        after=after,
    )


def gate(after, carry):
    def body(out):
        out[...] = jnp.zeros_like(out)

    token, *carry = call(
        body, (1,), [], [(shape(8, 128, dtype=F32), whole(8, 128))], after=after, carry=carry
    )
    return token, carry


def piece(array, lead, row, rows=256):
    return (
        array,
        pl.BlockSpec(
            (1, rows, 512),
            lambda *_: (lead, row, 0),
            pipeline_mode=pl.Buffered(buffer_count=1),
        ),
    )


def unpack(place, sx, pieces, select, outputs, store, after=()):
    count = len(pieces) // 2

    def body(place, sx, *refs):
        for r in range(4):

            @pl.when(place[pl.program_id(0)] == r)
            def _(r=r):
                a = select(refs[:count], r).astype(F32)
                b = select(refs[count : 2 * count], r).astype(F32)
                store(jnp.where(sx[0] == 0, a, b), jnp.where(sx[0] == 0, b, a), *refs[2 * count :])

    return call(
        body,
        (4,),
        [(value, whole(*value.shape)) for value in pieces],
        outputs,
        prefetch=(place, sx),
        after=after,
    )


def unpack_fc2(place, sx, pieces, after=()):
    def store(low, high, out):
        out[:, :256] = low.T
        out[:, 256:] = high.T

    block = pl.BlockSpec((512, 512), lambda i, o, x: (0, i))
    out = [(shape(512, 2048, dtype=F32), block)]
    return unpack(place, sx, pieces, lambda refs, r: refs[r // 2][2 * (r % 2)], out, store, after)[0]


def unpack_fc1(place, sx, pieces, after=()):
    def store(low, high, out):
        out[:256, :] = low
        out[256:, :] = high

    block = pl.BlockSpec((512, 512), lambda i, o, x: (i, 0))
    out = [(shape(2048, 512, dtype=F32), block)]
    return unpack(place, sx, pieces, lambda refs, r: refs[r // 2][2 * (r % 2) + 1], out, store, after)[0]


def unpack_att(place, sx, pieces, after=()):
    def store(low, high, qkv_out, dense_out):
        for part in range(3):
            qkv_out[part, :64, :] = low[64 * part : 64 * part + 64]
            qkv_out[part, 64:, :] = high[64 * part : 64 * part + 64]
        dense_out[...] = jnp.concatenate([low[192:], high[192:]], axis=0).T

    outputs = [
        (shape(3, 512, 512, dtype=F32), pl.BlockSpec((3, 128, 512), lambda i, o, x: (0, i, 0))),
        (shape(512, 512, dtype=F32), pl.BlockSpec((512, 128), lambda i, o, x: (0, i))),
    ]
    return unpack(place, sx, pieces, lambda refs, r: refs[0][r], outputs, store, after)


def norm_kernel(place, xs, scale, normed, stats):
    total = jnp.zeros((256, 1), F32)
    square = jnp.zeros((256, 1), F32)
    for q in range(4):
        value = xs[0, q].astype(F32)
        total += jnp.sum(value, axis=1, keepdims=True)
        square += jnp.sum(value * value, axis=1, keepdims=True)
    average = total / MODEL_WIDTH
    inverse = lax.rsqrt(square / MODEL_WIDTH - average * average + EPSILON)
    for r in range(4):
        value = xs[0, place[r]].astype(F32)
        centered = (value - average) * inverse
        normed[:, 512 * r : 512 * r + 512] = (
            centered * scale[2 * r : 2 * r + 1, :] + scale[2 * r + 1 : 2 * r + 2, :]
        ).astype(BF)
    stats[:, :128] = jnp.broadcast_to(average, (256, 128))
    stats[:, 128:] = jnp.broadcast_to(inverse, (256, 128))


def norm_tokens(place, gathered, scale, after=()):
    return call(
        norm_kernel,
        (8,),
        [
            (gathered, pl.BlockSpec((1, 4, 256, 512), lambda i, o: (i // 4, 0, i % 4, 0))),
            (scale, whole(8, 512)),
        ],
        [
            (shape(SEQ, MODEL_WIDTH), pl.BlockSpec((256, 2048), lambda i, o: (i, 0))),
            (shape(SEQ, 256, dtype=F32), pl.BlockSpec((256, 256), lambda i, o: (i, 0))),
        ],
        prefetch=(place,),
        large=True,
        after=after,
    )


ROOT = math.sqrt(2.0 / math.pi)
CUBIC = 0.044715
TILE = 512
HALF = SEQ // 2


def token_inputs(normed, cot):
    per = HALF // TILE
    return [
        (normed, pl.BlockSpec((TILE, MODEL_WIDTH), lambda i, *_: (i, 0))),
        (cot, pl.BlockSpec((1, 4, TILE, 512), lambda i, *_: (i // per, 0, i % per, 0))),
    ]


def store_grad(out, row, value):
    for at, r in enumerate((0, 2, 1, 3)):
        out[at, row : row + value.shape[0], :] = value[:, 512 * r : 512 * r + 512].astype(BF)


def mlp_kernel(place, n, c, *refs):
    weights, (bias, act_out, dfc_out, *grads, sums, w1, w2, acc1, acc2) = refs[:8], refs[8:]
    step = pl.program_id(0)

    @pl.when(step == 0)
    def _():
        acc1[...] = jnp.zeros_like(acc1)
        acc2[...] = jnp.zeros_like(acc2)
        sums[...] = jnp.zeros_like(sums)
        for s in range(2):
            for r in range(4):
                rows, cols = slice(256 * s, 256 * s + 256), slice(512 * r, 512 * r + 512)
                w2[rows, cols] = weights[4 * s + r][0, :256, :]
                w1[rows, cols] = weights[4 * s + r][0, 256:, :]

    pre = nt(n[...], w1[...]) + bias[...]
    back = jnp.zeros((TILE, 512), F32)
    for r in range(4):
        back += nt(c[0, place[r]], w2[:, 512 * r : 512 * r + 512])
    square = pre * pre
    angle = jnp.tanh(ROOT * pre * (1.0 + CUBIC * square))
    half = 0.5 * (1.0 + angle)
    act = (pre * half).astype(BF)
    slope = half + 0.5 * pre * (1.0 - angle * angle) * (ROOT * (1.0 + 3.0 * CUBIC * square))
    dfc = back * slope
    sums[...] += jnp.sum(dfc, axis=0, keepdims=True)
    dfc = dfc.astype(BF)
    act_out[...] = act
    dfc_out[...] = dfc
    for r in range(4):
        acc2[:, 512 * r : 512 * r + 512] += tn(act, c[0, place[r]])
    acc1[...] += tn(dfc, n[...])

    @pl.when(step == SEQ // TILE - 1)
    def _():
        for s in range(2):
            store_grad(grads[s], 0, acc2[256 * s : 256 * s + 256])
            store_grad(grads[2 + s], 0, acc1[256 * s : 256 * s + 256])


def mlp(place, normed, cot, weights, bias, after=(), carry=()):
    units = pl.BlockSpec((TILE, 512), lambda i, *_: (i, 0))
    grad = (shape(4, 256, 512), whole(4, 256, 512))
    return call(
        mlp_kernel,
        (SEQ // TILE,),
        token_inputs(normed, cot)
        + [piece(array, lead, 0, 512) for array, lead in weights]
        + [(bias, whole(1, 512))],
        [(shape(SEQ, 512), units)] * 2
        + [grad] * 4
        + [(shape(1, 512, dtype=F32), whole(1, 512))],
        [
            pltpu.VMEM((512, MODEL_WIDTH), BF),
            pltpu.VMEM((512, MODEL_WIDTH), BF),
            pltpu.VMEM((512, MODEL_WIDTH), F32),
            pltpu.VMEM((512, MODEL_WIDTH), F32),
        ],
        prefetch=(place,),
        large=True,
        after=after,
        carry=carry,
    )


def rotated(value, tables, sign):
    return (
        value * tables[0]
        + pltpu.roll(value, 112, 1) * (sign * tables[1])
        + pltpu.roll(value, 16, 1) * (sign * tables[2])
    )


def heads_kernel(place, n, c, *refs):
    weights, refs = refs[:16], refs[16:]
    bias, tables, *outs, joined = refs

    @pl.when(pl.program_id(0) == 0)
    def _():
        for block in range(2):
            for s in range(2):
                for r in range(4):
                    for part in range(4):
                        row = 384 * block + 128 * part if part < 3 else 768 + 128 * block
                        row += 64 * s
                        joined[row : row + 64, 512 * r : 512 * r + 512] = weights[
                            8 * block + 4 * s + r
                        ][0, 64 * part : 64 * part + 64, :]

    pre = nt(n[...], joined[:768]) + bias[...]
    back = jnp.zeros((TILE, 256), F32)
    for r in range(4):
        back += nt(c[0, place[r]], joined[768:, 512 * r : 512 * r + 512])
    lane = lax.broadcasted_iota(jnp.int32, (TILE, 128), 1)
    one = jnp.ones((TILE, 128), BF)
    for block in range(2):
        q_out, k_out, v0_out, v1_out, d_out = outs[5 * block : 5 * block + 5]
        mine = pre[:, 384 * block : 384 * block + 384]
        q_out[...] = (rotated(mine[:, :128], tables, 1.0) * SCALE).astype(BF)
        k_out[...] = rotated(mine[:, 128:256], tables, 1.0).astype(BF)
        value = mine[:, 256:].astype(BF)
        v0_out[...] = jnp.where(lane < HEAD_DIM, value, one)
        v1_out[...] = jnp.where(lane < HEAD_DIM, one, value)
        d_out[...] = back[:, 128 * block : 128 * block + 128].astype(BF)


def heads(place, normed, cot, weights, bias, tables, after=()):
    head = pl.BlockSpec((TILE, 128), lambda i, *_: (i, 0))
    return call(
        heads_kernel,
        (SEQ // TILE,),
        token_inputs(normed, cot)
        + [piece(*weight) for weight in weights]
        + [
            (bias, whole(1, 768)),
            (tables, pl.BlockSpec((3, TILE, 128), lambda i, *_: (0, i, 0))),
        ],
        [(shape(SEQ, 128), head)] * 10,
        [pltpu.VMEM((1024, MODEL_WIDTH), BF)],
        prefetch=(place,),
        large=True,
        after=after,
    )


BLOCK = 512
BLOCKS = SEQ // BLOCK


def attend_kernel(low, *refs):
    ins, (start, tables), refs = refs[:10], refs[10:12], refs[12:]
    outs, refs = refs[:10], refs[10:]
    scores, probs, dk_acc, dv_acc, peak_acc, o_acc, dq_acc = refs
    i = pl.program_id(0)

    @pl.when(i == 0)
    def _():
        dk_acc[...] = jnp.zeros_like(dk_acc)
        dv_acc[...] = jnp.zeros_like(dv_acc)
        for block in range(2):
            outs[5 * block + 4][...] = jnp.zeros_like(outs[5 * block + 4])

    lane = lax.broadcasted_iota(jnp.int32, (BLOCK, 128), 1)
    masks = (lane < HEAD_DIM, lane >= HEAD_DIM)
    zero = jnp.zeros((BLOCK, 128), BF)
    queries = [jnp.where(masks[h % 2], ins[5 * (h // 2)][...], zero) for h in range(4)]
    keys = [ins[5 * (h // 2) + 1] for h in range(4)]
    values = [ins[5 * (h // 2) + 2 + h % 2] for h in range(4)]
    col = lax.broadcasted_iota(jnp.int32, (BLOCK, BLOCK), 1)
    row = lax.broadcasted_iota(jnp.int32, (BLOCK, BLOCK), 0) + i * BLOCK
    begin = start[:, :1]

    def each(step):
        for j in range(BLOCKS):

            @pl.when((j >= low[i]) & (j <= i))
            def _(j=j):
                step(j, slice(j * BLOCK, j * BLOCK + BLOCK))

    peak_acc[...] = jnp.full_like(peak_acc, MASKED)
    o_acc[...] = jnp.zeros_like(o_acc)
    dq_acc[...] = jnp.zeros_like(dq_acc)

    def score(j, at):
        here = col + j * BLOCK
        allowed = (here >= begin) & (here <= row)
        for h in range(4):
            s = jnp.where(allowed, nt(queries[h], keys[h][at, :]), MASKED)
            scores[h, j] = s
            peak = peak_acc[h]
            for lanes in range(0, BLOCK, 128):
                peak = jnp.maximum(peak, s[:, lanes : lanes + 128])
            peak_acc[h] = peak

    each(score)
    peaks = [jnp.max(peak_acc[h], axis=1, keepdims=True) for h in range(4)]

    def weigh(j, at):
        for h in range(4):
            p = jnp.exp(scores[h, j] - peaks[h]).astype(BF)
            probs[h, j] = p
            o_acc[h] += nn(p, values[h][at, :])

    each(weigh)
    grads, shifted = [], []
    for block in range(2):
        scaled = []
        for h in range(2):
            out = o_acc[2 * block + h]
            first = HEAD_DIM * (1 - h)
            inverse = 1.0 / out[:, first : first + 1]
            out = out * inverse
            grad = jnp.where(masks[h], ins[5 * block + 4][...].astype(F32) * inverse, 0.0).astype(BF)
            wide = grad.astype(F32)
            delta = jnp.sum(wide * out, axis=1, keepdims=True)
            coarse = delta.astype(BF).astype(F32)
            wide = jnp.where(lane == first, -coarse, wide)
            shifted.append(jnp.where(lane == first + 1, coarse - delta, wide).astype(BF))
            grads.append(grad)
            scaled.append(out)
        outs[5 * block][...] = jnp.where(masks[0], *scaled).astype(BF)

    def back(j, at):
        for h in range(4):
            p = probs[h, j]
            d_scores = (p.astype(F32) * nt(shifted[h], values[h][at, :])).astype(BF)
            dq_acc[h] += nn(d_scores, keys[h][at, :])
            dk_acc[h // 2, at, :] += tn(d_scores, queries[h])
            dv_acc[h // 2, at, :] += tn(p, grads[h])

    each(back)
    rows = pl.ds(pl.multiple_of(i * BLOCK, BLOCK), BLOCK)
    for block in range(2):
        dq = jnp.where(masks[0], dq_acc[2 * block], dq_acc[2 * block + 1]) * SCALE
        dq = rotated(dq, [tables[t, rows, :] for t in range(3)], -1.0)
        outs[5 * block + 1][...] = dq.astype(BF)
        outs[5 * block + 4][0:1, :] += jnp.sum(dq, axis=0, keepdims=True)

    @pl.when(i == BLOCKS - 1)
    def _():
        for block in range(2):
            _, _, dk_out, dv_out, sums = outs[5 * block : 5 * block + 5]
            for j in range(8):
                rows = slice(j * 256, j * 256 + 256)
                dk = rotated(dk_acc[block, rows], [tables[t, rows] for t in range(3)], -1.0)
                dv = dv_acc[block, rows]
                dk_out[rows, :] = dk.astype(BF)
                dv_out[rows, :] = dv.astype(BF)
                sums[1:2, :] += jnp.sum(dk, axis=0, keepdims=True)
                sums[2:3, :] += jnp.sum(dv, axis=0, keepdims=True)


def attend(low, heads, start, tables, after=()):
    tile = pl.BlockSpec((BLOCK, 128), lambda i, o: (i, 0))
    full = whole(SEQ, 128)
    head = shape(SEQ, 128)
    return call(
        attend_kernel,
        (BLOCKS,),
        [(value, (tile, full, full, full, tile)[at % 5]) for at, value in enumerate(heads)]
        + [(start, tile), (tables, whole(3, SEQ, 128))],
        [
            (head, tile),
            (head, tile),
            (head, full),
            (head, full),
            (shape(8, 128, dtype=F32), whole(8, 128)),
        ]
        * 2,
        [
            pltpu.VMEM((4, BLOCKS, BLOCK, BLOCK), F32),
            pltpu.VMEM((4, BLOCKS, BLOCK, BLOCK), BF),
            pltpu.VMEM((2, SEQ, 128), F32),
            pltpu.VMEM((2, SEQ, 128), F32),
            pltpu.VMEM((4, BLOCK, 128), F32),
            pltpu.VMEM((4, BLOCK, 128), F32),
            pltpu.VMEM((4, BLOCK, 128), F32),
        ],
        prefetch=(low,),
        large=True,
        after=after,
    )


def att_grad_kernel(place, n, c, dq, dk, dv, o, grad0, grad1, grad2, acc):
    step = pl.program_id(0)

    @pl.when(step == 0)
    def _():
        acc[...] = jnp.zeros_like(acc)

    acc[:384] += tn(jnp.concatenate([dq[...], dk[...], dv[...]], axis=1), n[...])
    for r in range(4):
        acc[384:, 512 * r : 512 * r + 512] += tn(o[...], c[0, place[r]])

    @pl.when(step == SEQ // TILE - 1)
    def _():
        for part in range(4):
            row, rows = 128 * part, slice(64 * part, 64 * part + 64)
            store_grad(grad0, 64 * part, acc[row : row + 64])
            value = acc[row + 64 : row + 128]
            for at, (grad, r) in enumerate(((grad1, 0), (grad1, 2), (grad2, 1), (grad2, 3))):
                grad[at % 2, rows, :] = value[:, 512 * r : 512 * r + 512].astype(BF)


def att_grad(place, normed, cot, dq, dk, dv, o, after=()):
    head = pl.BlockSpec((TILE, 128), lambda i, *_: (i, 0))
    return call(
        att_grad_kernel,
        (SEQ // TILE,),
        token_inputs(normed, cot) + [(value, head) for value in (dq, dk, dv, o)],
        [(shape(4, 256, 512), whole(4, 256, 512))] + [(shape(2, 256, 512), whole(2, 256, 512))] * 2,
        [pltpu.VMEM((512, MODEL_WIDTH), F32)],
        prefetch=(place,),
        large=True,
        after=after,
    )


def join(joined, spans, rights):
    row = 0
    for at, (first, size) in enumerate(spans):
        for r in range(4):
            joined[row : row + size, 512 * r : 512 * r + 512] = rights[4 * at + r][
                0, first : first + size, :
            ]
        row += size


def project(prefetch, items, tokens, outputs, store, after=()):
    lefts = [left for left, _ in items]
    parts = [part for _, rows in items for part in rows]
    spans = [(first, size) for _, first, size in parts]
    rights = [piece(*one) for pieces, _, _ in parts for one in pieces]

    def body(*refs):
        scalars, refs = refs[: len(prefetch)], refs[len(prefetch) :]
        left_refs, refs = refs[: len(lefts)], refs[len(lefts) :]
        right_refs, refs = refs[: len(rights)], refs[len(rights) :]
        *outs, joined = refs

        @pl.when(pl.program_id(0) == 0)
        def _():
            join(joined, spans, right_refs)

        left = jnp.concatenate([ref[...] for ref in left_refs], axis=1)
        store(scalars, outs, lambda r: nn(left, joined[:, 512 * r : 512 * r + 512]).astype(BF))

    return call(
        body,
        (SEQ // TILE,),
        [(left, pl.BlockSpec((TILE, left.shape[1]), tokens)) for left in lefts] + rights,
        outputs,
        [pltpu.VMEM((sum(size for _, size in spans), MODEL_WIDTH), BF)],
        prefetch=prefetch,
        large=True,
        after=after,
    )


def project_near(sz, items, after=()):
    per = HALF // TILE

    def store(scalars, outs, value):
        for out, pieces in zip(outs, ((1, 3), (0, 2)), strict=True):
            for at, r in enumerate(pieces):
                out[at, 0] = value(r)

    out = pl.BlockSpec((2, 1, TILE, 512), lambda i, *_: (0, i // per, i % per, 0))
    return project(
        (sz,),
        items,
        lambda i, s: (((i // per) ^ s[0]) * per + i % per, 0),
        [(shape(2, 2, HALF, 512), out)] * 2,
        store,
        after,
    )


def added(values):
    total = values[0].astype(F32)
    for value in values[1:]:
        total = total + value.astype(F32)
    return total.astype(BF)


def grad_inputs(values):
    inputs, reads = [], []
    for value in values:
        at = len(inputs)
        if isinstance(value, list):
            inputs += [(one, whole(2, 256, 512)) for one in value]
            reads.append(lambda refs, step, at=at: refs[at + step // 2][step % 2])
        else:
            inputs.append((value, whole(4, 256, 512)))
            reads.append(lambda refs, step, at=at: refs[at][step])
    return inputs, reads


def add(left, right, after=()):
    inputs, reads = grad_inputs([left, right])

    def body(*refs):
        for step in range(4):
            refs[-1][step] = added([read(refs, step) for read in reads])

    return call(
        body, (1,), inputs, [(shape(4, 256, 512), whole(4, 256, 512))], after=after
    )


def total_grad(groups, after=()):
    inputs, reads = [], []
    for group in groups:
        found, read = grad_inputs(group)
        reads.append((len(inputs), len(found), read))
        inputs += found
    rows = 256 * len(groups)

    def body(*refs):
        near, same = refs[-2:]
        for step in range(4):
            out = same if step < 2 else near
            for g, (at, size, read) in enumerate(reads):
                mine = refs[at : at + size]
                out[step % 2, 256 * g : 256 * g + 256, :] = added([one(mine, step) for one in read])

    out = (shape(2, rows, 512), whole(2, rows, 512))
    return call(body, (1,), inputs, [out, out], after=after)


def quarters(value):
    return [value[256 * k : 256 * k + 256, :] for k in range(value.shape[0] // 256)]


def blocks(count):
    return (shape(count, 256, 512), whole(count, 256, 512))


FLAT = (shape(HALF, 512), whole(HALF, 512))


def quarter(array, piece, half):
    return (array, pl.BlockSpec((1, 1, HALF, 512), lambda *_: (piece, half, 0, 0)))


def scatter_far(same, near, counts, grad, after=()):
    over_z, over_y = counts
    groups = grad[0].shape[1] // 256

    def body(same, near, grad_same, grad_near, to_z, to_y, to_x):
        far = quarters(added([same[0, 0], near[0, 0]]))
        for k in range(over_z):
            to_z[k] = far[k]
        for k in range(over_y):
            to_y[k] = far[over_z + k]
        for at, ref in enumerate((grad_same, grad_near)):
            for g in range(groups):
                rows = slice(256 * g, 256 * g + 256)
                to_x[groups * at + g] = ref[0, rows, :]
                to_y[over_y + groups * at + g] = ref[1, rows, :]

    pair = whole(2, 256 * groups, 512)
    return call(
        body,
        (1,),
        [quarter(same, 1, 1), quarter(near, 1, 1), (grad[0], pair), (grad[1], pair)],
        [blocks(over_z), blocks(over_y + 2 * groups), blocks(2 * groups)],
        after=after,
    )


def scatter_kept(same, near, after=(), carry=()):
    places = ((0, 0), (1, 0), (0, 1))

    def body(*refs):
        for at in range(3):
            refs[6 + at][...] = added([refs[2 * at][0, 0], refs[2 * at + 1][0, 0]])

    return call(
        body,
        (1,),
        [quarter(value, *place) for place in places for value in (same, near)],
        [FLAT] * 3,
        after=after,
        carry=carry,
    )


def scatter_second(for_y, from_z, after=()):
    def body(for_y, from_z, to_y):
        for k in range(4):
            rows = slice(256 * k, 256 * k + 256)
            to_y[rows, :] = added([for_y[rows, :], from_z[k]])

    return call(
        body,
        (1,),
        [(for_y, FLAT[1]), (from_z, whole(4, 256, 512))],
        [FLAT],
        after=after,
    )[0]


def scatter_last(for_y, from_z, for_z, from_y, near_grad, after=()):
    def body(for_y, from_z, for_z, from_y, near_grad, to_z, to_y, grad):
        for k in range(4):
            rows = slice(256 * k, 256 * k + 256)
            to_y[rows, :] = added([for_y[rows, :], from_z[k]]) if k < 3 else for_y[rows, :]
            to_z[rows, :] = for_z[rows, :] if k < 3 else added([for_z[rows, :], from_y[0]])
        for k in range(2):
            grad[k] = near_grad[k]
            grad[2 + k] = from_y[1 + k]

    three = whole(3, 256, 512)
    return call(
        body,
        (1,),
        [
            (for_y, FLAT[1]),
            (from_z, three),
            (for_z, FLAT[1]),
            (from_y, three),
            (near_grad, whole(2, 256, 512)),
        ],
        [FLAT, FLAT, blocks(4)],
        after=after,
    )


def more_dp(value):
    if lax.axis_size("xo") > 1:
        return lax.psum(value, "xo")
    return value


def on_device(
    block_input,
    cotangent,
    doc_lengths,
    layernorm_gain,
    layernorm_bias,
    qkv_weight,
    qkv_bias,
    fc1_weight,
    fc1_bias,
    dense_weight,
    fc2_weight,
    out_bias,
):
    x, zh, zl = lax.axis_index("x"), lax.axis_index("zh"), lax.axis_index("zl")
    here = 2 * lax.axis_index("y") + lax.axis_index("c")
    place = jnp.stack([here ^ r for r in range(4)]).astype(jnp.int32)
    sx = x.astype(jnp.int32).reshape(1)
    sz = zl.astype(jnp.int32).reshape(1)

    tokens = lax.all_gather(block_input, ("zl", "y", "c"), axis=0, tiled=False)
    cot = lax.all_gather(cotangent, ("zl", "y", "c"), axis=0, tiled=False)
    tokens, cot = (value.reshape(2, 4, HALF, 512) for value in (tokens, cot))

    scale = jnp.stack([layernorm_gain, layernorm_bias])
    scale = jnp.concatenate([scale, swap(scale, "c")], axis=0)
    heads_bias = qkv_bias.reshape(3, 2, HEAD_DIM)
    units_bias = fc1_bias.reshape(2, 256)
    heads_bias = jnp.where(x == 0, heads_bias, heads_bias[:, ::-1])
    units_bias = jnp.where(x == 0, units_bias, units_bias[::-1])
    own_bias = jnp.concatenate([heads_bias.reshape(1, 384), units_bias.reshape(1, 512)], axis=1)

    order = jnp.stack([here ^ r for r in (3, 1, 2, 0)]).astype(jnp.int32)
    near1, near3, far2, r0 = pack(order, sx, qkv_weight, fc1_weight, dense_weight, fc2_weight)
    near3 = swap(near3, "c")
    r1 = swap(near1, "c")

    lengths = lax.dynamic_index_in_dim(doc_lengths, zh, 0, keepdims=False)
    ends = jnp.cumsum(lengths)
    spot = jnp.arange(SEQ, dtype=jnp.int32)
    begin = jnp.sum(jnp.where(spot[:, None] >= ends[None, :], lengths[None, :], 0), axis=1)
    low = (begin[::BLOCK] // BLOCK).astype(jnp.int32)
    start = jnp.broadcast_to(begin[:, None], (SEQ, 128)).astype(jnp.int32)
    freqs = jnp.exp(jnp.arange(ROT // 2, dtype=F32) * (-2.0 * math.log(10000.0) / ROT))
    angle = spot.astype(F32)[:, None] * freqs[None, :]
    cosine, sine = jnp.cos(angle), jnp.sin(angle)
    ones, none = jnp.ones((SEQ, ROT), F32), jnp.zeros((SEQ, ROT // 2), F32)
    tables = jnp.stack(
        [
            jnp.concatenate([cosine, cosine, ones] * 2, axis=1),
            jnp.concatenate([-sine, none, none, none] * 2, axis=1),
            jnp.concatenate([none, sine, none, none] * 2, axis=1),
        ]
    )

    def rows(weights, row, first, size):
        return [
            ([(*one[:2], one[2] if row is None else row) for one in weights[4 * s : 4 * s + 4]], first, size)
            for s in range(2)
        ]

    input_single = block_input.astype(F32)
    branch_gradient = cotangent.astype(F32)

    to_y, att_y, other01, att01 = split_first(far2, near3, r0, r1, after=[scale])
    r23, other01 = swap(to_y, "y"), swap(other01, "zh")
    scale = jnp.concatenate([scale, swap(scale, "y")], axis=0)
    other_bias = swap(own_bias, "zh")
    token, (r23, other01, att_y, att01) = gate(
        [to_y, scale, other_bias, tables, start], [r23, other01, att_y, att01]
    )

    other23, att23 = swap(r23, "zh"), swap(att_y, "y")
    own23, next01 = swap(r23, "x"), swap(other01, "x")
    normed, stats = norm_tokens(place, tokens, scale, after=[token])
    token, (other23, att23, att01) = gate([stats, own23, next01], [other23, att23, att01])
    mine = lax.dynamic_slice_in_dim(stats, zl * HALF, HALF, axis=0)
    average, inverse = mine[:, :1], mine[:, 128:129]
    centered = (input_single - average) * inverse

    next23, att01 = swap(other23, "x"), swap(att01, "zh")
    token, (att01, att23) = gate([token, next23], [att01, att23])

    own_w = [(r0, 0), (r1, 0), (r23, 0), (r23, 1), (r0, 1), (r1, 1), (own23, 0), (own23, 1)]
    other_w = [(array, i) for array in (other01, other23, next01, next23) for i in range(2)]
    next_att01, other_att23, next_att23 = swap(att01, "x"), swap(att23, "zh"), swap(att23, "x")
    other_act, other_dfc, *other_mlp, other_units = mlp(
        place, normed, cot, other_w, other_bias[:, 384:], after=[token]
    )
    token, (other_att23, other_mlp[1]) = gate(
        [other_units, next_att01, next_att23], [other_att23, other_mlp[1]]
    )

    from_x, next_other23 = swap(other_mlp[1], "x"), swap(other_att23, "x")
    own_act, own_dfc, *own_mlp, own_units = mlp(
        place, normed, cot, own_w, own_bias[:, 384:], after=[token]
    )
    token, (other_mlp[3], own_mlp[1]) = gate(
        [own_units, from_x, next_other23], [other_mlp[3], own_mlp[1]]
    )

    own_a = [(r0, 0, 2), (r1, 0, 2), (att23, 0, 0), (att23, 1, 0)]
    own_a += [(r0, 1, 2), (r1, 1, 2), (next_att23, 0, 0), (next_att23, 1, 0)]
    other_a = [
        (array, i, 0) for array in (att01, other_att23, next_att01, next_other23) for i in range(2)
    ]
    fc2 = add(other_mlp[0], from_x, after=[token])[0]
    to_fc2 = swap(fc2, "zh")
    from_x, own_fc2 = swap(other_mlp[3], "x"), swap(own_mlp[1], "x")
    bias = jnp.concatenate([own_bias[:, :384], other_bias[:, :384]], axis=1)
    qkv = heads(place, normed, cot, own_a + other_a, bias, tables, after=[fc2])
    attended = attend(low, qkv, start, tables)
    own_o, own_dq, own_dk, own_dv, own_sums = attended[:5]
    other_o, other_dq, other_dk, other_dv, other_sums = attended[5:]
    other_sums = jnp.concatenate([other_sums[:3].reshape(1, 384), other_units], axis=1)
    token, (own_mlp[3], other_sums) = gate(
        [own_o, to_fc2, from_x, own_fc2], [own_mlp[3], other_sums]
    )

    fc1 = add(other_mlp[2], from_x, after=[token])[0]
    to_fc1 = swap(fc1, "zh")
    other_att = att_grad(
        place, normed, cot, other_dq, other_dk, other_dv, other_o, after=[fc1]
    )
    other_sums = swap(other_sums, "zh")
    from_x, own_fc1 = swap_all(other_att[1:], "x"), swap(own_mlp[3], "x")
    items = [(own_dfc, rows(own_w, 1, 0, 256)), (other_dfc, rows(other_w, 1, 0, 256))]
    for part, (left, right) in enumerate(
        ((own_dq, other_dq), (own_dk, other_dk), (own_dv, other_dv))
    ):
        items.append((left, rows(own_a, None, 64 * part, 64)))
        items.append((right, rows(other_a, None, 64 * part, 64)))
    dn_near, dn_same = project_near(sz, items, after=[other_att[0]])
    own_sums = jnp.concatenate([own_sums[:3].reshape(1, 384), own_units], axis=1)
    token, (dn_near,) = gate([dn_same, own_sums, to_fc1, *from_x, own_fc1, other_sums], [dn_near])

    sums = own_sums + other_sums
    heads_sum, units_sum = sums[0, :384].reshape(3, 2, HEAD_DIM), sums[0, 384:].reshape(2, 256)
    heads_sum = jnp.where(x == 0, heads_sum, heads_sum[:, ::-1]).reshape(1, 384)
    units_sum = jnp.where(x == 0, units_sum, units_sum[::-1]).reshape(1, 512)
    sums = jnp.concatenate([heads_sum, units_sum], axis=1)
    dn_near, sums_x = swap(dn_near, "c"), swap(sums, "x")
    mlp_near, mlp_same = total_grad(
        [[own_mlp[0], own_fc2, to_fc2], [own_mlp[2], own_fc1, to_fc1]], after=[token]
    )
    mlp_near, mlp_same = swap(more_dp(mlp_near), "c"), more_dp(mlp_same)
    att = add(other_att[0], from_x, after=[mlp_same])[0]
    token, (att,) = gate([dn_near, mlp_near, sums_x], [att])

    to_z, to_y, mlp01 = scatter_far(
        dn_same, dn_near, (4, 0), (mlp_same, mlp_near), after=[token]
    )
    from_z, mlp23 = swap(to_z, "zl"), swap(to_y, "y")
    own_att = att_grad(place, normed, cot, own_dq, own_dk, own_dv, own_o, after=[to_z])
    dn, for_y, for_z = scatter_kept(dn_same, dn_near, after=[own_att[0]])
    own_from_att, to_att = swap_all(own_att[1:], "x"), swap(att, "zh")
    items = [
        (own_act, rows(own_w, 0, 0, 256)),
        (other_act, rows(other_w, 0, 0, 256)),
        (own_o, rows(own_a, None, 192, 64)),
        (other_o, rows(other_a, None, 192, 64)),
    ]
    near, same = project_near(sz, items, after=[dn])
    token, (near, mlp01, mlp23, for_z) = gate(
        [same, to_att, *own_from_att, from_z], [near, mlp01, mlp23, for_z]
    )

    near, dn_z, next01 = swap(near, "c"), swap(for_z, "zl"), swap(mlp01, "x")
    to_y = scatter_second(for_y, from_z, after=[token])
    dn_y = swap(to_y, "y")
    att_near, att_same = total_grad([[own_att[0], own_from_att, to_att]], after=[to_y])
    att_near, att_same = swap(more_dp(att_near), "c"), more_dp(att_same)
    token, (mlp23,) = gate([att_same, near, dn_z, dn_y, next01, att_near], [mlp23])

    next23 = swap(mlp23, "x")
    to_z, to_y, att01 = scatter_far(same, near, (3, 1), (att_same, att_near), after=[token])
    from_z, from_y = swap(to_z, "zl"), swap(to_y, "y")
    branch, branch_y, branch_z, dn_y = scatter_kept(same, near, after=[to_z], carry=[dn_y])
    dn = dn.astype(F32) + dn_y.astype(F32) + dn_z.astype(F32)
    row_sums = jnp.stack(
        [jnp.sum(dn * layernorm_gain, axis=1), jnp.sum(dn * layernorm_gain * centered, axis=1)]
    )
    col_sums = jnp.stack(
        [
            jnp.sum(dn * centered, axis=0),
            jnp.sum(dn, axis=0),
            jnp.sum(branch_gradient, axis=0),
        ]
    )
    row_sums = row_sums + swap(row_sums, "c")
    row_sums = row_sums + swap(row_sums, "y")
    col_sums = col_sums + swap(col_sums, "zl")
    token, (col_sums,) = gate([branch, from_z, from_y, next23, row_sums], [col_sums])

    to_z, to_y, att_pieces = scatter_last(
        branch_y, from_z, branch_z, from_y, att01, after=[token]
    )
    branch_z, branch_y = swap(to_z, "zl"), swap(to_y, "y")
    next_att = swap(att_pieces, "x")
    mlp_pieces = (mlp01, mlp23, next01, next23)
    fc2_grad = unpack_fc2(place, sx, mlp_pieces, after=[to_y])
    fc1_grad = unpack_fc1(place, sx, mlp_pieces, after=[fc2_grad])
    token, (col_sums,) = gate([fc1_grad], [col_sums])
    for axis in ("zh", "x"):
        col_sums = col_sums + swap(col_sums, axis)
    qkv_grad, dense_grad = unpack_att(place, sx, (att_pieces, next_att), after=[token])
    sums = more_dp(sums + sums_x)

    qkv_bias_grad, fc1_bias_grad = sums[0, :384].reshape(3, 128), sums[0, 384:]

    branch = branch.astype(F32) + branch_y.astype(F32) + branch_z.astype(F32)
    result = (input_single + (branch + out_bias)).astype(BF)
    input_grad = branch_gradient + inverse * (
        dn * layernorm_gain
        - row_sums[0][:, None] / MODEL_WIDTH
        - centered * (row_sums[1][:, None] / MODEL_WIDTH)
    )
    col_sums = more_dp(col_sums)
    return (
        result,
        input_grad,
        col_sums[0],
        col_sums[1],
        qkv_grad,
        qkv_bias_grad,
        fc1_grad,
        fc1_bias_grad,
        dense_grad,
        fc2_grad,
        col_sums[2],
    )


def solution(mesh):
    dp, row, col = mesh.devices.shape
    assert dp % 2 == 0 and row == 4 and col == 4
    parts = Mesh(
        mesh.devices.reshape(dp // 2, 2, 2, 2, 2, 2), ("xo", "x", "zh", "zl", "y", "c")
    )
    data, rows, cols = ("xo", "x"), ("zh", "zl"), ("y", "c")
    return jax.shard_map(
        on_device,
        mesh=parts,
        in_specs=(
            P(data + rows, cols),
            P(data + rows, cols),
            P(data, None),
            P(cols),
            P(cols),
            P(None, rows, cols),
            P(None, rows + cols),
            P(rows, cols),
            P(rows + cols),
            P(cols, rows),
            P(cols, rows),
            P(cols),
        ),
        out_specs=(
            P(data + rows, cols),
            P(data + rows, cols),
            P(cols),
            P(cols),
            P(None, rows, cols),
            P(None, rows + cols),
            P(rows, cols),
            P(rows + cols),
            P(cols, rows),
            P(cols, rows),
            P(cols),
        ),
        check_vma=False,
    )
```

```python
import math

import jax
import jax.numpy as jnp
from jax import lax
from jax.experimental import pallas as pl
from jax.experimental.pallas import tpu as pltpu
from jax.sharding import Mesh
from jax.sharding import PartitionSpec as P

MODEL_WIDTH = 2048
HEAD_DIM = 64
ROT = 32
SEQ = 2048
EPSILON = 1e-05
MASKED = -1e30
SCALE = HEAD_DIM ** (-0.5)
VMEM = 60 * 1024 * 1024
ROOM = 12 * 1024 * 1024

BF = jnp.bfloat16
F32 = jnp.float32


def swap(value, axis):
    return lax.ppermute(value, axis, [(0, 1), (1, 0)])


def swap_all(values, axis):
    return [swap(value, axis) for value in values]


def nt(left, right):
    return lax.dot_general(left, right, (((1,), (1,)), ((), ())), preferred_element_type=F32)


def tn(left, right):
    return lax.dot_general(left, right, (((0,), (0,)), ((), ())), preferred_element_type=F32)


def nn(left, right):
    return lax.dot_general(left, right, (((1,), (0,)), ((), ())), preferred_element_type=F32)


def shape(*dims, dtype=BF):
    return jax.ShapeDtypeStruct(dims, dtype)


def whole(*dims):
    return pl.BlockSpec(dims, lambda *_: (0,) * len(dims))


def call(body, grid, inputs, outputs, scratch=(), prefetch=(), after=(), carry=(), large=False):
    count, waits, kept = len(prefetch) + len(inputs), len(after) + len(carry), len(carry)
    results = len(outputs)

    def kernel(*refs):
        own, rest = refs[:count], refs[count + waits :]
        body(*own, *rest[:results], *rest[results + kept :])

    anywhere = pl.BlockSpec(memory_space=pl.ANY)
    need = sum(math.prod(ref.shape) * jnp.dtype(ref.dtype).itemsize for ref in scratch) + ROOM
    for spec, value in [(spec, value) for value, spec in inputs] + [(spec, out) for out, spec in outputs]:
        once = math.prod(spec.block_shape) * jnp.dtype(value.dtype).itemsize
        need += once if spec.pipeline_mode is not None else 2 * once
    need = VMEM if large else min(need, VMEM)
    results_ = pl.pallas_call(
        kernel,
        grid_spec=pltpu.PrefetchScalarGridSpec(
            num_scalar_prefetch=len(prefetch),
            grid=grid,
            in_specs=[spec for _, spec in inputs] + [anywhere] * waits,
            out_specs=[spec for _, spec in outputs] + [anywhere] * kept,
            scratch_shapes=list(scratch),
        ),
        out_shape=[out for out, _ in outputs] + [shape(*c.shape, dtype=c.dtype) for c in carry],
        input_output_aliases={count + len(after) + i: results + i for i in range(kept)},
        compiler_params=pltpu.CompilerParams(vmem_limit_bytes=need),
        cost_estimate=pl.CostEstimate(flops=1000, bytes_accessed=1000, transcendentals=0),
    )(*prefetch, *[value for value, _ in inputs], *after, *carry)
    return list(results_)


def pack_kernel(order, sx, qkv, fc1, dense, fc2, near1, near3, far2, own, to_y, to_z):
    step = pl.program_id(0)
    x = sx[0]

    def write(put, parts):
        fc2_t = fc2[...].T
        dense_t = dense[...].T
        for s in range(parts):

            def pick(low, high, s=s):
                return jnp.where(x == s, low, high)

            put(s, 0, pick(fc2_t[:256], fc2_t[256:]))
            put(s, 256, pick(fc1[:256], fc1[256:]))
            for part in range(3):
                put(s, 512 + 64 * part, pick(qkv[part, :64], qkv[part, 64:]))
            put(s, 704, pick(dense_t[:64], dense_t[64:]))

    def both(ref):
        def put(s, row, value):
            ref[s, row : row + value.shape[0], :] = value

        return put

    def one(ref):
        def put(s, row, value):
            ref[row : row + value.shape[0], :] = value

        return put

    for at, (ref, parts) in enumerate(((near3, 1), (near1, 2), (far2, 1), (own, 2))):

        @pl.when(step == at)
        def _(ref=ref, parts=parts):
            write(both(ref) if parts == 2 else one(ref), parts)

    @pl.when(step == 2)
    def _():
        to_y[0] = far2[:EARLY, :]

    @pl.when(step == 3)
    def _():
        to_z[0] = own[0, :EARLY, :]


EARLY = 528


def pack(order, sx, qkv, fc1, dense, fc2):
    return call(
        pack_kernel,
        (4,),
        [
            (qkv, pl.BlockSpec((3, 128, 512), lambda i, o, x: (0, o[i], 0))),
            (fc1, pl.BlockSpec((512, 512), lambda i, o, x: (o[i], 0))),
            (dense, pl.BlockSpec((512, 128), lambda i, o, x: (0, o[i]))),
            (fc2, pl.BlockSpec((512, 512), lambda i, o, x: (0, o[i]))),
        ],
        [
            (shape(2, 768, 512), whole(2, 768, 512)),
            (shape(768, 512), whole(768, 512)),
            (shape(768, 512), whole(768, 512)),
            (shape(2, 768, 512), whole(2, 768, 512)),
            (shape(1, EARLY, 512), whole(1, EARLY, 512)),
            (shape(1, EARLY, 512), whole(1, EARLY, 512)),
        ],
        large=True,
        prefetch=(order, sx),
    )


def split_first(near3, near1, after=()):
    def body(near3, near1, mlp_y, mlp_z):
        mlp_y[0] = near3[...]
        mlp_z[0] = near1[0]

    mlp_out = (shape(1, 512, 512), whole(1, 512, 512))
    return call(
        body,
        (1,),
        [(near3, whole(512, 512)), (near1, whole(1, 512, 512))],
        [mlp_out, mlp_out],
        after=after,
    )


def stack_mlp(y2, y3, z0, z1, far2, near3, own, near1, after=()):
    def body(y2, y3, z0, z1, far2, near3, own, near1, to_x, to_z, att_y, att_z):
        for at, ref in enumerate((y2, y3, z0, z1)):
            to_x[at] = ref[0, :512, :]
            if at < 2:
                to_z[at] = ref[0, :512, :]
        att_y[0] = far2[...]
        att_y[1] = near3[...]
        att_z[0] = own[0]
        att_z[1] = near1[0]

    flat = pl.BlockSpec((256, 512), lambda *_: (2, 0))
    deep = pl.BlockSpec((1, 256, 512), lambda *_: (0, 2, 0))
    att_out = (shape(2, 256, 512), whole(2, 256, 512))
    return call(
        body,
        (1,),
        [(value, whole(*value.shape)) for value in (y2, y3, z0, z1)]
        + [(far2, flat), (near3, flat), (own, deep), (near1, deep)],
        [
            (shape(4, 512, 512), whole(4, 512, 512)),
            (shape(2, 512, 512), whole(2, 512, 512)),
            att_out,
            att_out,
        ],
        after=after,
    )


def gate(after, carry):
    def body(out):
        out[...] = jnp.zeros_like(out)

    token, *carry = call(
        body, (1,), [], [(shape(8, 128, dtype=F32), whole(8, 128))], after=after, carry=carry
    )
    return token, carry


def piece(array, lead, row, rows=256):
    return (
        array,
        pl.BlockSpec(
            (1, rows, 512),
            lambda *_: (lead, row, 0),
            pipeline_mode=pl.Buffered(buffer_count=1),
        ),
    )


def unpack(place, sx, pieces, select, outputs, store, after=()):
    count = len(pieces) // 2

    def body(place, sx, *refs):
        for r in range(4):

            @pl.when(place[pl.program_id(0)] == r)
            def _(r=r):
                a = select(refs[:count], r).astype(F32)
                b = select(refs[count : 2 * count], r).astype(F32)
                store(jnp.where(sx[0] == 0, a, b), jnp.where(sx[0] == 0, b, a), *refs[2 * count :])

    return call(
        body,
        (4,),
        [(value, whole(*value.shape)) for value in pieces],
        outputs,
        prefetch=(place, sx),
        after=after,
    )


def unpack_fc2(place, sx, pieces, after=()):
    def store(low, high, out):
        out[:, :256] = low.T
        out[:, 256:] = high.T

    block = pl.BlockSpec((512, 512), lambda i, o, x: (0, i))
    out = [(shape(512, 2048, dtype=F32), block)]
    return unpack(place, sx, pieces, lambda refs, r: refs[r // 2][2 * (r % 2)], out, store, after)[0]


def unpack_fc1(place, sx, pieces, after=()):
    def store(low, high, out):
        out[:256, :] = low
        out[256:, :] = high

    block = pl.BlockSpec((512, 512), lambda i, o, x: (i, 0))
    out = [(shape(2048, 512, dtype=F32), block)]
    return unpack(place, sx, pieces, lambda refs, r: refs[r // 2][2 * (r % 2) + 1], out, store, after)[0]


def unpack_att(place, sx, pieces, after=()):
    def store(low, high, qkv_out, dense_out):
        for part in range(3):
            qkv_out[part, :64, :] = low[64 * part : 64 * part + 64]
            qkv_out[part, 64:, :] = high[64 * part : 64 * part + 64]
        dense_out[...] = jnp.concatenate([low[192:], high[192:]], axis=0).T

    outputs = [
        (shape(3, 512, 512, dtype=F32), pl.BlockSpec((3, 128, 512), lambda i, o, x: (0, i, 0))),
        (shape(512, 512, dtype=F32), pl.BlockSpec((512, 128), lambda i, o, x: (0, i))),
    ]
    return unpack(place, sx, pieces, lambda refs, r: refs[0][r], outputs, store, after)


def norm_kernel(place, xs, scale, normed, stats):
    total = jnp.zeros((256, 1), F32)
    square = jnp.zeros((256, 1), F32)
    for q in range(4):
        value = xs[0, q].astype(F32)
        total += jnp.sum(value, axis=1, keepdims=True)
        square += jnp.sum(value * value, axis=1, keepdims=True)
    average = total / MODEL_WIDTH
    inverse = lax.rsqrt(square / MODEL_WIDTH - average * average + EPSILON)
    for r in range(4):
        value = xs[0, place[r]].astype(F32)
        centered = (value - average) * inverse
        normed[:, 512 * r : 512 * r + 512] = (
            centered * scale[2 * r : 2 * r + 1, :] + scale[2 * r + 1 : 2 * r + 2, :]
        ).astype(BF)
    stats[:, :128] = jnp.broadcast_to(average, (256, 128))
    stats[:, 128:] = jnp.broadcast_to(inverse, (256, 128))


def norm_tokens(place, gathered, scale, after=()):
    return call(
        norm_kernel,
        (8,),
        [
            (gathered, pl.BlockSpec((1, 4, 256, 512), lambda i, o: (i // 4, 0, i % 4, 0))),
            (scale, whole(8, 512)),
        ],
        [
            (shape(SEQ, MODEL_WIDTH), pl.BlockSpec((256, 2048), lambda i, o: (i, 0))),
            (shape(SEQ, 256, dtype=F32), pl.BlockSpec((256, 256), lambda i, o: (i, 0))),
        ],
        prefetch=(place,),
        large=True,
        after=after,
    )


ROOT = math.sqrt(2.0 / math.pi)
CUBIC = 0.044715
TILE = 512
HALF = SEQ // 2


def token_inputs(normed, cot):
    per = HALF // TILE
    return [
        (normed, pl.BlockSpec((TILE, MODEL_WIDTH), lambda i, *_: (i, 0))),
        (cot, pl.BlockSpec((1, 4, TILE, 512), lambda i, *_: (i // per, 0, i % per, 0))),
    ]


def store_grad(out, row, value):
    for at, r in enumerate((0, 2, 1, 3)):
        out[at, row : row + value.shape[0], :] = value[:, 512 * r : 512 * r + 512].astype(BF)


def units_kernel(n, *refs):
    weights, (bias, act_out, slope_out, w1) = refs[:8], refs[8:]

    @pl.when(pl.program_id(0) == 0)
    def _():
        for s in range(2):
            for r in range(4):
                rows, cols = slice(256 * s, 256 * s + 256), slice(512 * r, 512 * r + 512)
                w1[rows, cols] = weights[4 * s + r][0]

    pre = nt(n[...], w1[...]) + bias[...]
    square = pre * pre
    angle = jnp.tanh(ROOT * pre * (1.0 + CUBIC * square))
    half = 0.5 * (1.0 + angle)
    act_out[...] = (pre * half).astype(BF)
    slope = half + 0.5 * pre * (1.0 - angle * angle) * (ROOT * (1.0 + 3.0 * CUBIC * square))
    slope_out[...] = slope.astype(BF)


def hidden_units(normed, weights, bias, after=()):
    units = pl.BlockSpec((TILE, 512), lambda i, *_: (i, 0))
    return call(
        units_kernel,
        (SEQ // TILE,),
        [(normed, pl.BlockSpec((TILE, MODEL_WIDTH), lambda i, *_: (i, 0)))]
        + [piece(array, lead, 1) for array, lead in weights]
        + [(bias, whole(1, 512))],
        [(shape(SEQ, 512), units)] * 2,
        [pltpu.VMEM((512, MODEL_WIDTH), BF)],
        large=True,
        after=after,
    )


def mlp_kernel(place, n, c, act, slope, *refs):
    weights, (dfc_out, *grads, sums, w2, acc1, acc2) = refs[:8], refs[8:]
    step = pl.program_id(0)

    @pl.when(step == 0)
    def _():
        acc1[...] = jnp.zeros_like(acc1)
        acc2[...] = jnp.zeros_like(acc2)
        sums[...] = jnp.zeros_like(sums)
        for s in range(2):
            for r in range(4):
                rows, cols = slice(256 * s, 256 * s + 256), slice(512 * r, 512 * r + 512)
                w2[rows, cols] = weights[4 * s + r][0]

    back = jnp.zeros((TILE, 512), F32)
    for r in range(4):
        back += nt(c[0, place[r]], w2[:, 512 * r : 512 * r + 512])
    dfc = back * slope[...].astype(F32)
    sums[...] += jnp.sum(dfc, axis=0, keepdims=True)
    dfc = dfc.astype(BF)
    dfc_out[...] = dfc
    for r in range(4):
        acc2[:, 512 * r : 512 * r + 512] += tn(act[...], c[0, place[r]])
    acc1[...] += tn(dfc, n[...])

    @pl.when(step == SEQ // TILE - 1)
    def _():
        for s in range(2):
            store_grad(grads[s], 0, acc2[256 * s : 256 * s + 256])
            store_grad(grads[2 + s], 0, acc1[256 * s : 256 * s + 256])


def mlp(place, normed, cot, act, slope, weights, after=()):
    units = pl.BlockSpec((TILE, 512), lambda i, *_: (i, 0))
    grad = (shape(4, 256, 512), whole(4, 256, 512))
    return call(
        mlp_kernel,
        (SEQ // TILE,),
        token_inputs(normed, cot)
        + [(act, units), (slope, units)]
        + [piece(array, lead, 0) for array, lead in weights],
        [(shape(SEQ, 512), units)] + [grad] * 4 + [(shape(1, 512, dtype=F32), whole(1, 512))],
        [
            pltpu.VMEM((512, MODEL_WIDTH), BF),
            pltpu.VMEM((512, MODEL_WIDTH), F32),
            pltpu.VMEM((512, MODEL_WIDTH), F32),
        ],
        prefetch=(place,),
        large=True,
        after=after,
    )


def rotated(value, tables, sign):
    return (
        value * tables[0]
        + pltpu.roll(value, 112, 1) * (sign * tables[1])
        + pltpu.roll(value, 16, 1) * (sign * tables[2])
    )


def rotary_tables(cosine, sine, after=()):
    half = ROT // 2

    def body(cosine, sine, out):
        line = lax.broadcasted_iota(jnp.int32, (half, 128), 0)
        lane = lax.broadcasted_iota(jnp.int32, (half, 128), 1) % HEAD_DIM
        first = jnp.where(lane == line, 1.0, 0.0)
        second = jnp.where(lane == line + half, 1.0, 0.0)

        def spread(value, places):
            return jnp.dot(
                value, places, precision=lax.Precision.HIGHEST, preferred_element_type=F32
            )

        feature = lax.broadcasted_iota(jnp.int32, (TILE, 128), 1) % HEAD_DIM
        out[0] = jnp.where(feature < ROT, spread(cosine[...], first + second), 1.0)
        out[1] = spread(sine[...], -first)
        out[2] = spread(sine[...], second)

    rows = pl.BlockSpec((TILE, half), lambda i: (i, 0))
    return call(
        body,
        (SEQ // TILE,),
        [(cosine, rows), (sine, rows)],
        [(shape(3, SEQ, 128, dtype=F32), pl.BlockSpec((3, TILE, 128), lambda i: (0, i, 0)))],
        after=after,
    )[0]


def heads_kernel(place, n, c, *refs):
    weights, (bias, tables, q_out, k_out, v0_out, v1_out, d_out, joined) = refs[:8], refs[8:]

    @pl.when(pl.program_id(0) == 0)
    def _():
        for s in range(2):
            for r in range(4):
                for part in range(4):
                    row = 128 * part + 64 * s
                    joined[row : row + 64, 512 * r : 512 * r + 512] = weights[4 * s + r][
                        0, 64 * part : 64 * part + 64, :
                    ]

    pre = nt(n[...], joined[:384]) + bias[...]
    q_out[...] = (rotated(pre[:, :128], tables, 1.0) * SCALE).astype(BF)
    k_out[...] = rotated(pre[:, 128:256], tables, 1.0).astype(BF)
    value = pre[:, 256:].astype(BF)
    lane = lax.broadcasted_iota(jnp.int32, value.shape, 1)
    one = jnp.ones_like(value)
    v0_out[...] = jnp.where(lane < HEAD_DIM, value, one)
    v1_out[...] = jnp.where(lane < HEAD_DIM, one, value)
    back = jnp.zeros((TILE, 128), F32)
    for r in range(4):
        back += nt(c[0, place[r]], joined[384:, 512 * r : 512 * r + 512])
    d_out[...] = back.astype(BF)


def heads(place, normed, cot, weights, bias, tables, after=()):
    head = pl.BlockSpec((TILE, 128), lambda i, *_: (i, 0))
    return call(
        heads_kernel,
        (SEQ // TILE,),
        token_inputs(normed, cot)
        + [piece(*weight) for weight in weights]
        + [
            (bias, whole(1, 384)),
            (tables, pl.BlockSpec((3, TILE, 128), lambda i, *_: (0, i, 0))),
        ],
        [(shape(SEQ, 128), head)] * 5,
        [pltpu.VMEM((512, MODEL_WIDTH), BF)],
        prefetch=(place,),
        large=True,
        after=after,
    )


BLOCK = 512
BLOCKS = SEQ // BLOCK


def attend_kernel(low, *refs):
    ins, (start, tables), refs = refs[:10], refs[10:12], refs[12:]
    outs, refs = refs[:10], refs[10:]
    scores, probs, dk_acc, dv_acc, peak_acc, o_acc, dq_acc = refs
    i = pl.program_id(0)

    @pl.when(i == 0)
    def _():
        dk_acc[...] = jnp.zeros_like(dk_acc)
        dv_acc[...] = jnp.zeros_like(dv_acc)
        for block in range(2):
            outs[5 * block + 4][...] = jnp.zeros_like(outs[5 * block + 4])

    lane = lax.broadcasted_iota(jnp.int32, (BLOCK, 128), 1)
    masks = (lane < HEAD_DIM, lane >= HEAD_DIM)
    zero = jnp.zeros((BLOCK, 128), BF)
    queries = [jnp.where(masks[h % 2], ins[5 * (h // 2)][...], zero) for h in range(4)]
    keys = [ins[5 * (h // 2) + 1] for h in range(4)]
    values = [ins[5 * (h // 2) + 2 + h % 2] for h in range(4)]
    col = lax.broadcasted_iota(jnp.int32, (BLOCK, BLOCK), 1)
    row = lax.broadcasted_iota(jnp.int32, (BLOCK, BLOCK), 0) + i * BLOCK
    begin = start[:, :1]

    def each(step):
        for j in range(BLOCKS):

            @pl.when((j >= low[i]) & (j <= i))
            def _(j=j):
                step(j, slice(j * BLOCK, j * BLOCK + BLOCK))

    peak_acc[...] = jnp.full_like(peak_acc, MASKED)
    o_acc[...] = jnp.zeros_like(o_acc)
    dq_acc[...] = jnp.zeros_like(dq_acc)

    def score(j, at):
        here = col + j * BLOCK
        allowed = (here >= begin) & (here <= row)
        for h in range(4):
            s = jnp.where(allowed, nt(queries[h], keys[h][at, :]), MASKED)
            scores[h, j] = s
            peak = peak_acc[h]
            for lanes in range(0, BLOCK, 128):
                peak = jnp.maximum(peak, s[:, lanes : lanes + 128])
            peak_acc[h] = peak

    each(score)
    peaks = [jnp.max(peak_acc[h], axis=1, keepdims=True) for h in range(4)]

    def weigh(j, at):
        for h in range(4):
            p = jnp.exp(scores[h, j] - peaks[h]).astype(BF)
            probs[h, j] = p
            o_acc[h] += nn(p, values[h][at, :])

    each(weigh)
    grads, shifted = [], []
    for block in range(2):
        scaled = []
        for h in range(2):
            out = o_acc[2 * block + h]
            first = HEAD_DIM * (1 - h)
            inverse = 1.0 / out[:, first : first + 1]
            out = out * inverse
            grad = jnp.where(masks[h], ins[5 * block + 4][...].astype(F32) * inverse, 0.0).astype(BF)
            wide = grad.astype(F32)
            delta = jnp.sum(wide * out, axis=1, keepdims=True)
            coarse = delta.astype(BF).astype(F32)
            wide = jnp.where(lane == first, -coarse, wide)
            shifted.append(jnp.where(lane == first + 1, coarse - delta, wide).astype(BF))
            grads.append(grad)
            scaled.append(out)
        outs[5 * block][...] = jnp.where(masks[0], *scaled).astype(BF)

    def back(j, at):
        for h in range(4):
            p = probs[h, j]
            d_scores = (p.astype(F32) * nt(shifted[h], values[h][at, :])).astype(BF)
            dq_acc[h] += nn(d_scores, keys[h][at, :])
            dk_acc[h // 2, at, :] += tn(d_scores, queries[h])
            dv_acc[h // 2, at, :] += tn(p, grads[h])

    each(back)
    rows = pl.ds(pl.multiple_of(i * BLOCK, BLOCK), BLOCK)
    for block in range(2):
        dq = jnp.where(masks[0], dq_acc[2 * block], dq_acc[2 * block + 1]) * SCALE
        dq = rotated(dq, [tables[t, rows, :] for t in range(3)], -1.0)
        outs[5 * block + 1][...] = dq.astype(BF)
        outs[5 * block + 4][0:1, :] += jnp.sum(dq, axis=0, keepdims=True)

    @pl.when(i == BLOCKS - 1)
    def _():
        for block in range(2):
            _, _, dk_out, dv_out, sums = outs[5 * block : 5 * block + 5]
            for j in range(8):
                rows = slice(j * 256, j * 256 + 256)
                dk = rotated(dk_acc[block, rows], [tables[t, rows] for t in range(3)], -1.0)
                dv = dv_acc[block, rows]
                dk_out[rows, :] = dk.astype(BF)
                dv_out[rows, :] = dv.astype(BF)
                sums[1:2, :] += jnp.sum(dk, axis=0, keepdims=True)
                sums[2:3, :] += jnp.sum(dv, axis=0, keepdims=True)


def attend(low, heads, start, tables, after=()):
    tile = pl.BlockSpec((BLOCK, 128), lambda i, o: (i, 0))
    full = whole(SEQ, 128)
    head = shape(SEQ, 128)
    return call(
        attend_kernel,
        (BLOCKS,),
        [(value, (tile, full, full, full, tile)[at % 5]) for at, value in enumerate(heads)]
        + [(start, tile), (tables, whole(3, SEQ, 128))],
        [
            (head, tile),
            (head, tile),
            (head, full),
            (head, full),
            (shape(8, 128, dtype=F32), whole(8, 128)),
        ]
        * 2,
        [
            pltpu.VMEM((4, BLOCKS, BLOCK, BLOCK), F32),
            pltpu.VMEM((4, BLOCKS, BLOCK, BLOCK), BF),
            pltpu.VMEM((2, SEQ, 128), F32),
            pltpu.VMEM((2, SEQ, 128), F32),
            pltpu.VMEM((4, BLOCK, 128), F32),
            pltpu.VMEM((4, BLOCK, 128), F32),
            pltpu.VMEM((4, BLOCK, 128), F32),
        ],
        prefetch=(low,),
        large=True,
        after=after,
    )


def att_grad_kernel(place, n, c, dq, dk, dv, o, grad0, grad1, grad2, acc):
    step = pl.program_id(0)

    @pl.when(step == 0)
    def _():
        acc[...] = jnp.zeros_like(acc)

    acc[:384] += tn(jnp.concatenate([dq[...], dk[...], dv[...]], axis=1), n[...])
    for r in range(4):
        acc[384:, 512 * r : 512 * r + 512] += tn(o[...], c[0, place[r]])

    @pl.when(step == SEQ // TILE - 1)
    def _():
        for part in range(4):
            row, rows = 128 * part, slice(64 * part, 64 * part + 64)
            store_grad(grad0, 64 * part, acc[row : row + 64])
            value = acc[row + 64 : row + 128]
            for at, (grad, r) in enumerate(((grad1, 0), (grad1, 2), (grad2, 1), (grad2, 3))):
                grad[at % 2, rows, :] = value[:, 512 * r : 512 * r + 512].astype(BF)


def att_grad(place, normed, cot, dq, dk, dv, o, after=()):
    head = pl.BlockSpec((TILE, 128), lambda i, *_: (i, 0))
    return call(
        att_grad_kernel,
        (SEQ // TILE,),
        token_inputs(normed, cot) + [(value, head) for value in (dq, dk, dv, o)],
        [(shape(4, 256, 512), whole(4, 256, 512))] + [(shape(2, 256, 512), whole(2, 256, 512))] * 2,
        [pltpu.VMEM((512, MODEL_WIDTH), F32)],
        prefetch=(place,),
        large=True,
        after=after,
    )


def join(joined, spans, rights):
    row = 0
    for at, (first, size) in enumerate(spans):
        for r in range(4):
            joined[row : row + size, 512 * r : 512 * r + 512] = rights[4 * at + r][
                0, first : first + size, :
            ]
        row += size


def project(prefetch, items, tokens, outputs, store, after=()):
    lefts = [left for left, _ in items]
    parts = [part for _, rows in items for part in rows]
    spans = [(first, size) for _, first, size in parts]
    rights = [piece(*one) for pieces, _, _ in parts for one in pieces]

    def body(*refs):
        scalars, refs = refs[: len(prefetch)], refs[len(prefetch) :]
        left_refs, refs = refs[: len(lefts)], refs[len(lefts) :]
        right_refs, refs = refs[: len(rights)], refs[len(rights) :]
        *outs, joined = refs

        @pl.when(pl.program_id(0) == 0)
        def _():
            join(joined, spans, right_refs)

        left = jnp.concatenate([ref[...] for ref in left_refs], axis=1)
        store(scalars, outs, lambda r: nn(left, joined[:, 512 * r : 512 * r + 512]).astype(BF))

    return call(
        body,
        (SEQ // TILE,),
        [(left, pl.BlockSpec((TILE, left.shape[1]), tokens)) for left in lefts] + rights,
        outputs,
        [pltpu.VMEM((sum(size for _, size in spans), MODEL_WIDTH), BF)],
        prefetch=prefetch,
        large=True,
        after=after,
    )


def project_near(sz, items, after=()):
    per = HALF // TILE

    def store(scalars, outs, value):
        for out, pieces in zip(outs, ((1, 3), (0, 2)), strict=True):
            for at, r in enumerate(pieces):
                out[at, 0] = value(r)

    out = pl.BlockSpec((2, 1, TILE, 512), lambda i, *_: (0, i // per, i % per, 0))
    return project(
        (sz,),
        items,
        lambda i, s: (((i // per) ^ s[0]) * per + i % per, 0),
        [(shape(2, 2, HALF, 512), out)] * 2,
        store,
        after,
    )


def added(values):
    total = values[0].astype(F32)
    for value in values[1:]:
        total = total + value.astype(F32)
    return total.astype(BF)


def grad_inputs(values):
    inputs, reads = [], []
    for value in values:
        at = len(inputs)
        if isinstance(value, list):
            inputs += [(one, whole(2, 256, 512)) for one in value]
            reads.append(lambda refs, step, at=at: refs[at + step // 2][step % 2])
        else:
            inputs.append((value, whole(4, 256, 512)))
            reads.append(lambda refs, step, at=at: refs[at][step])
    return inputs, reads


def add(left, right, after=()):
    inputs, reads = grad_inputs([left, right])

    def body(*refs):
        for step in range(4):
            refs[-1][step] = added([read(refs, step) for read in reads])

    return call(
        body, (1,), inputs, [(shape(4, 256, 512), whole(4, 256, 512))], after=after
    )


def total_grad(groups, after=()):
    inputs, reads = [], []
    for group in groups:
        found, read = grad_inputs(group)
        reads.append((len(inputs), len(found), read))
        inputs += found
    rows = 256 * len(groups)

    def body(*refs):
        near, same = refs[-2:]
        for step in range(4):
            out = same if step < 2 else near
            for g, (at, size, read) in enumerate(reads):
                mine = refs[at : at + size]
                out[step % 2, 256 * g : 256 * g + 256, :] = added([one(mine, step) for one in read])

    out = (shape(2, rows, 512), whole(2, rows, 512))
    return call(body, (1,), inputs, [out, out], after=after)


def quarters(value):
    return [value[256 * k : 256 * k + 256, :] for k in range(value.shape[0] // 256)]


def blocks(count):
    return (shape(count, 256, 512), whole(count, 256, 512))


FLAT = (shape(HALF, 512), whole(HALF, 512))


def quarter(array, piece, half):
    return (array, pl.BlockSpec((1, 1, HALF, 512), lambda *_: (piece, half, 0, 0)))


def scatter_far(same, near, counts, grad, after=()):
    over_z, over_y = counts
    groups = grad[0].shape[1] // 256

    def body(same, near, grad_same, grad_near, to_z, to_y, to_x):
        far = quarters(added([same[0, 0], near[0, 0]]))
        for k in range(over_z):
            to_z[k] = far[k]
        for k in range(over_y):
            to_y[k] = far[over_z + k]
        for at, ref in enumerate((grad_same, grad_near)):
            for g in range(groups):
                rows = slice(256 * g, 256 * g + 256)
                to_x[groups * at + g] = ref[0, rows, :]
                to_y[over_y + groups * at + g] = ref[1, rows, :]

    pair = whole(2, 256 * groups, 512)
    return call(
        body,
        (1,),
        [quarter(same, 1, 1), quarter(near, 1, 1), (grad[0], pair), (grad[1], pair)],
        [blocks(over_z), blocks(over_y + 2 * groups), blocks(2 * groups)],
        after=after,
    )


def scatter_kept(same, near, after=(), carry=()):
    places = ((0, 0), (1, 0), (0, 1))

    def body(*refs):
        for at in range(3):
            refs[6 + at][...] = added([refs[2 * at][0, 0], refs[2 * at + 1][0, 0]])

    return call(
        body,
        (1,),
        [quarter(value, *place) for place in places for value in (same, near)],
        [FLAT] * 3,
        after=after,
        carry=carry,
    )


def scatter_second(for_y, from_z, after=()):
    def body(for_y, from_z, to_y):
        for k in range(4):
            rows = slice(256 * k, 256 * k + 256)
            to_y[rows, :] = added([for_y[rows, :], from_z[k]])

    return call(
        body,
        (1,),
        [(for_y, FLAT[1]), (from_z, whole(4, 256, 512))],
        [FLAT],
        after=after,
    )[0]


def scatter_last(for_y, from_z, for_z, from_y, near_grad, after=()):
    def body(for_y, from_z, for_z, from_y, near_grad, to_z, to_y, grad):
        for k in range(4):
            rows = slice(256 * k, 256 * k + 256)
            to_y[rows, :] = added([for_y[rows, :], from_z[k]]) if k < 3 else for_y[rows, :]
            to_z[rows, :] = for_z[rows, :] if k < 3 else added([for_z[rows, :], from_y[0]])
        for k in range(2):
            grad[k] = near_grad[k]
            grad[2 + k] = from_y[1 + k]

    three = whole(3, 256, 512)
    return call(
        body,
        (1,),
        [
            (for_y, FLAT[1]),
            (from_z, three),
            (for_z, FLAT[1]),
            (from_y, three),
            (near_grad, whole(2, 256, 512)),
        ],
        [FLAT, FLAT, blocks(4)],
        after=after,
    )


def more_dp(value):
    if lax.axis_size("xo") > 1:
        return lax.psum(value, "xo")
    return value


def on_device(
    block_input,
    cotangent,
    doc_lengths,
    layernorm_gain,
    layernorm_bias,
    qkv_weight,
    qkv_bias,
    fc1_weight,
    fc1_bias,
    dense_weight,
    fc2_weight,
    out_bias,
):
    x, zh, zl = lax.axis_index("x"), lax.axis_index("zh"), lax.axis_index("zl")
    here = 2 * lax.axis_index("y") + lax.axis_index("c")
    place = jnp.stack([here ^ r for r in range(4)]).astype(jnp.int32)
    sx = x.astype(jnp.int32).reshape(1)
    sz = zl.astype(jnp.int32).reshape(1)

    tokens = lax.all_gather(block_input, ("zl", "y", "c"), axis=0, tiled=False)
    cot = lax.all_gather(cotangent, ("zl", "y", "c"), axis=0, tiled=False)
    tokens, cot = (value.reshape(2, 4, HALF, 512) for value in (tokens, cot))

    scale = jnp.stack([layernorm_gain, layernorm_bias])
    scale = jnp.concatenate([scale, swap(scale, "c")], axis=0)
    heads_bias = qkv_bias.reshape(3, 2, HEAD_DIM)
    units_bias = fc1_bias.reshape(2, 256)
    heads_bias = jnp.where(x == 0, heads_bias, heads_bias[:, ::-1])
    units_bias = jnp.where(x == 0, units_bias, units_bias[::-1])
    own_bias = jnp.concatenate([heads_bias.reshape(1, 384), units_bias.reshape(1, 512)], axis=1)

    order = jnp.stack([here ^ r for r in (3, 1, 2, 0)]).astype(jnp.int32)
    near1, near3, far2, r0, to_y2, to_z0 = pack(order, sx, qkv_weight, fc1_weight, dense_weight, fc2_weight)
    near3 = swap(near3, "c")
    r1 = swap(near1, "c")

    lengths = lax.dynamic_index_in_dim(doc_lengths, zh, 0, keepdims=False)
    ends = jnp.cumsum(lengths)
    spot = jnp.arange(SEQ, dtype=jnp.int32)
    begin = jnp.sum(jnp.where(spot[:, None] >= ends[None, :], lengths[None, :], 0), axis=1)
    low = (begin[::BLOCK] // BLOCK).astype(jnp.int32)
    start = jnp.broadcast_to(begin[:, None], (SEQ, 128)).astype(jnp.int32)
    freqs = jnp.exp(jnp.arange(ROT // 2, dtype=F32) * (-2.0 * math.log(10000.0) / ROT))
    angle = spot.astype(F32)[:, None] * freqs[None, :]
    cosine, sine = jnp.cos(angle), jnp.sin(angle)
    def rows(weights, row, first, size):
        return [
            ([(*one[:2], one[2] if row is None else row) for one in weights[4 * s : 4 * s + 4]], first, size)
            for s in range(2)
        ]

    input_single = block_input.astype(F32)
    branch_gradient = cotangent.astype(F32)

    from_y2, from_z0 = swap(to_y2, "y"), swap(to_z0, "zh")
    to_y3, to_z1 = split_first(near3, r1, after=[scale])
    from_y3, from_z1 = swap(to_y3, "y"), swap(to_z1, "zh")
    tables = rotary_tables(cosine, sine, after=[to_z1])
    scale = jnp.concatenate([scale, swap(scale, "y")], axis=0)
    token, (other_bias,) = gate(
        [tables, start, from_y2, from_z0, from_y3, from_z1], [own_bias]
    )

    to_x, to_z, att_y, att01 = stack_mlp(
        from_y2, from_y3, from_z0, from_z1, far2, near3, r0, r1, after=[token]
    )
    normed, stats = norm_tokens(place, tokens, scale, after=[to_x])
    att23, other_bias = swap(att_y, "y"), swap(other_bias, "zh")
    from_x, other23 = swap(to_x, "x"), swap(to_z, "zh")
    token, (other23, att23, att01) = gate([stats, from_x, other_bias], [other23, att23, att01])
    mine = lax.dynamic_slice_in_dim(stats, zl * HALF, HALF, axis=0)
    average, inverse = mine[:, :1], mine[:, 128:129]
    centered = (input_single - average) * inverse

    next23, att01 = swap(other23, "x"), swap(att01, "zh")
    own_w = [(r0, 0), (r1, 0), (from_y2, 0), (from_y3, 0)]
    own_w += [(r0, 1), (r1, 1), (from_x, 0), (from_x, 1)]
    own_act, own_slope = hidden_units(normed, own_w, own_bias[:, 384:], after=[token])
    token, (att01, att23) = gate([own_act, next23], [att01, att23])

    other_w = [(from_z0, 0), (from_z1, 0), (other23, 0), (other23, 1)]
    other_w += [(from_x, 2), (from_x, 3), (next23, 0), (next23, 1)]
    next_att01, other_att23, next_att23 = swap(att01, "x"), swap(att23, "zh"), swap(att23, "x")
    other_act, other_slope = hidden_units(normed, other_w, other_bias[:, 384:], after=[token])
    other_dfc, *other_mlp, other_units = mlp(
        place, normed, cot, other_act, other_slope, other_w
    )
    token, (other_att23, other_mlp[1]) = gate(
        [other_units, next_att01, next_att23], [other_att23, other_mlp[1]]
    )

    from_x, next_other23 = swap(other_mlp[1], "x"), swap(other_att23, "x")
    own_dfc, *own_mlp, own_units = mlp(
        place, normed, cot, own_act, own_slope, own_w, after=[token]
    )
    own_a = [(r0, 0, 2), (r1, 0, 2), (att23, 0, 0), (att23, 1, 0)]
    own_a += [(r0, 1, 2), (r1, 1, 2), (next_att23, 0, 0), (next_att23, 1, 0)]
    own_qkv = heads(place, normed, cot, own_a, own_bias[:, :384], tables, after=[own_units])
    token, (other_mlp[3], own_mlp[1]) = gate(
        [own_qkv[0], from_x, next_other23], [other_mlp[3], own_mlp[1]]
    )

    other_a = [
        (array, i, 0) for array in (att01, other_att23, next_att01, next_other23) for i in range(2)
    ]
    fc2 = add(other_mlp[0], from_x, after=[token])[0]
    to_fc2 = swap(fc2, "zh")
    from_x, own_fc2 = swap(other_mlp[3], "x"), swap(own_mlp[1], "x")
    other_qkv = heads(place, normed, cot, other_a, other_bias[:, :384], tables, after=[fc2])
    attended = attend(low, own_qkv + other_qkv, start, tables)
    own_o, own_dq, own_dk, own_dv, own_sums = attended[:5]
    other_o, other_dq, other_dk, other_dv, other_sums = attended[5:]
    other_sums = jnp.concatenate([other_sums[:3].reshape(1, 384), other_units], axis=1)
    token, (own_mlp[3], other_sums) = gate(
        [own_o, to_fc2, from_x, own_fc2], [own_mlp[3], other_sums]
    )

    fc1 = add(other_mlp[2], from_x, after=[token])[0]
    to_fc1 = swap(fc1, "zh")
    other_att = att_grad(
        place, normed, cot, other_dq, other_dk, other_dv, other_o, after=[fc1]
    )
    other_sums = swap(other_sums, "zh")
    from_x, own_fc1 = swap_all(other_att[1:], "x"), swap(own_mlp[3], "x")
    items = [(own_dfc, rows(own_w, 1, 0, 256)), (other_dfc, rows(other_w, 1, 0, 256))]
    for part, (left, right) in enumerate(
        ((own_dq, other_dq), (own_dk, other_dk), (own_dv, other_dv))
    ):
        items.append((left, rows(own_a, None, 64 * part, 64)))
        items.append((right, rows(other_a, None, 64 * part, 64)))
    dn_near, dn_same = project_near(sz, items, after=[other_att[0]])
    own_sums = jnp.concatenate([own_sums[:3].reshape(1, 384), own_units], axis=1)
    token, (dn_near,) = gate([dn_same, own_sums, to_fc1, *from_x, own_fc1, other_sums], [dn_near])

    sums = own_sums + other_sums
    heads_sum, units_sum = sums[0, :384].reshape(3, 2, HEAD_DIM), sums[0, 384:].reshape(2, 256)
    heads_sum = jnp.where(x == 0, heads_sum, heads_sum[:, ::-1]).reshape(1, 384)
    units_sum = jnp.where(x == 0, units_sum, units_sum[::-1]).reshape(1, 512)
    sums = jnp.concatenate([heads_sum, units_sum], axis=1)
    dn_near, sums_x = swap(dn_near, "c"), swap(sums, "x")
    mlp_near, mlp_same = total_grad(
        [[own_mlp[0], own_fc2, to_fc2], [own_mlp[2], own_fc1, to_fc1]], after=[token]
    )
    mlp_near, mlp_same = swap(more_dp(mlp_near), "c"), more_dp(mlp_same)
    att = add(other_att[0], from_x, after=[mlp_same])[0]
    token, (att,) = gate([dn_near, mlp_near, sums_x], [att])

    to_z, to_y, mlp01 = scatter_far(
        dn_same, dn_near, (4, 0), (mlp_same, mlp_near), after=[token]
    )
    from_z, mlp23 = swap(to_z, "zl"), swap(to_y, "y")
    own_att = att_grad(place, normed, cot, own_dq, own_dk, own_dv, own_o, after=[to_z])
    dn, for_y, for_z = scatter_kept(dn_same, dn_near, after=[own_att[0]])
    own_from_att, to_att = swap_all(own_att[1:], "x"), swap(att, "zh")
    items = [
        (own_act, rows(own_w, 0, 0, 256)),
        (other_act, rows(other_w, 0, 0, 256)),
        (own_o, rows(own_a, None, 192, 64)),
        (other_o, rows(other_a, None, 192, 64)),
    ]
    near, same = project_near(sz, items, after=[dn])
    token, (near, mlp01, mlp23, for_z) = gate(
        [same, to_att, *own_from_att, from_z], [near, mlp01, mlp23, for_z]
    )

    near, dn_z, next01 = swap(near, "c"), swap(for_z, "zl"), swap(mlp01, "x")
    to_y = scatter_second(for_y, from_z, after=[token])
    dn_y = swap(to_y, "y")
    att_near, att_same = total_grad([[own_att[0], own_from_att, to_att]], after=[to_y])
    att_near, att_same = swap(more_dp(att_near), "c"), more_dp(att_same)
    token, (mlp23,) = gate([att_same, near, dn_z, dn_y, next01, att_near], [mlp23])

    next23 = swap(mlp23, "x")
    to_z, to_y, att01 = scatter_far(same, near, (3, 1), (att_same, att_near), after=[token])
    from_z, from_y = swap(to_z, "zl"), swap(to_y, "y")
    branch, branch_y, branch_z, dn_y = scatter_kept(same, near, after=[to_z], carry=[dn_y])
    dn = dn.astype(F32) + dn_y.astype(F32) + dn_z.astype(F32)
    row_sums = jnp.stack(
        [jnp.sum(dn * layernorm_gain, axis=1), jnp.sum(dn * layernorm_gain * centered, axis=1)]
    )
    col_sums = jnp.stack(
        [
            jnp.sum(dn * centered, axis=0),
            jnp.sum(dn, axis=0),
            jnp.sum(branch_gradient, axis=0),
        ]
    )
    row_sums = row_sums + swap(row_sums, "c")
    row_sums = row_sums + swap(row_sums, "y")
    col_sums = col_sums + swap(col_sums, "zl")
    token, (col_sums,) = gate([branch, from_z, from_y, next23, row_sums], [col_sums])

    to_z, to_y, att_pieces = scatter_last(
        branch_y, from_z, branch_z, from_y, att01, after=[token]
    )
    branch_z, branch_y = swap(to_z, "zl"), swap(to_y, "y")
    next_att = swap(att_pieces, "x")
    mlp_pieces = (mlp01, mlp23, next01, next23)
    fc2_grad = unpack_fc2(place, sx, mlp_pieces, after=[to_y])
    fc1_grad = unpack_fc1(place, sx, mlp_pieces, after=[fc2_grad])
    token, (col_sums,) = gate([fc1_grad], [col_sums])
    for axis in ("zh", "x"):
        col_sums = col_sums + swap(col_sums, axis)
    qkv_grad, dense_grad = unpack_att(place, sx, (att_pieces, next_att), after=[token])
    sums = more_dp(sums + sums_x)

    qkv_bias_grad, fc1_bias_grad = sums[0, :384].reshape(3, 128), sums[0, 384:]

    branch = branch.astype(F32) + branch_y.astype(F32) + branch_z.astype(F32)
    result = (input_single + (branch + out_bias)).astype(BF)
    input_grad = branch_gradient + inverse * (
        dn * layernorm_gain
        - row_sums[0][:, None] / MODEL_WIDTH
        - centered * (row_sums[1][:, None] / MODEL_WIDTH)
    )
    col_sums = more_dp(col_sums)
    return (
        result,
        input_grad,
        col_sums[0],
        col_sums[1],
        qkv_grad,
        qkv_bias_grad,
        fc1_grad,
        fc1_bias_grad,
        dense_grad,
        fc2_grad,
        col_sums[2],
    )


def solution(mesh):
    dp, row, col = mesh.devices.shape
    assert dp % 2 == 0 and row == 4 and col == 4
    parts = Mesh(
        mesh.devices.reshape(dp // 2, 2, 2, 2, 2, 2), ("xo", "x", "zh", "zl", "y", "c")
    )
    data, rows, cols = ("xo", "x"), ("zh", "zl"), ("y", "c")
    return jax.shard_map(
        on_device,
        mesh=parts,
        in_specs=(
            P(data + rows, cols),
            P(data + rows, cols),
            P(data, None),
            P(cols),
            P(cols),
            P(None, rows, cols),
            P(None, rows + cols),
            P(rows, cols),
            P(rows + cols),
            P(cols, rows),
            P(cols, rows),
            P(cols),
        ),
        out_specs=(
            P(data + rows, cols),
            P(data + rows, cols),
            P(cols),
            P(cols),
            P(None, rows, cols),
            P(None, rows + cols),
            P(rows, cols),
            P(rows + cols),
            P(cols, rows),
            P(cols, rows),
            P(cols),
        ),
        check_vma=False,
    )
```

```python
import math

import jax
import jax.numpy as jnp
from jax import lax
from jax.experimental import pallas as pl
from jax.experimental.pallas import tpu as pltpu
from jax.sharding import Mesh
from jax.sharding import PartitionSpec as P

MODEL_WIDTH = 2048
HEAD_DIM = 64
ROT = 32
SEQ = 2048
EPSILON = 1e-05
MASKED = -1e30
SCALE = HEAD_DIM ** (-0.5)
VMEM = 60 * 1024 * 1024
ROOM = 12 * 1024 * 1024

BF = jnp.bfloat16
F32 = jnp.float32


def swap(value, axis):
    return lax.ppermute(value, axis, [(0, 1), (1, 0)])


def swap_all(values, axis):
    return [swap(value, axis) for value in values]


def nt(left, right):
    return lax.dot_general(left, right, (((1,), (1,)), ((), ())), preferred_element_type=F32)


def tn(left, right):
    return lax.dot_general(left, right, (((0,), (0,)), ((), ())), preferred_element_type=F32)


def nn(left, right):
    return lax.dot_general(left, right, (((1,), (0,)), ((), ())), preferred_element_type=F32)


def shape(*dims, dtype=BF):
    return jax.ShapeDtypeStruct(dims, dtype)


def whole(*dims):
    return pl.BlockSpec(dims, lambda *_: (0,) * len(dims))


def call(body, grid, inputs, outputs, scratch=(), prefetch=(), after=(), carry=(), large=False):
    count, waits, kept = len(prefetch) + len(inputs), len(after) + len(carry), len(carry)
    results = len(outputs)

    def kernel(*refs):
        own, rest = refs[:count], refs[count + waits :]
        body(*own, *rest[:results], *rest[results + kept :])

    anywhere = pl.BlockSpec(memory_space=pl.ANY)
    need = sum(math.prod(ref.shape) * jnp.dtype(ref.dtype).itemsize for ref in scratch) + ROOM
    for spec, value in [(spec, value) for value, spec in inputs] + [(spec, out) for out, spec in outputs]:
        once = math.prod(spec.block_shape) * jnp.dtype(value.dtype).itemsize
        need += once if spec.pipeline_mode is not None else 2 * once
    need = VMEM if large else min(need, VMEM)
    results_ = pl.pallas_call(
        kernel,
        grid_spec=pltpu.PrefetchScalarGridSpec(
            num_scalar_prefetch=len(prefetch),
            grid=grid,
            in_specs=[spec for _, spec in inputs] + [anywhere] * waits,
            out_specs=[spec for _, spec in outputs] + [anywhere] * kept,
            scratch_shapes=list(scratch),
        ),
        out_shape=[out for out, _ in outputs] + [shape(*c.shape, dtype=c.dtype) for c in carry],
        input_output_aliases={count + len(after) + i: results + i for i in range(kept)},
        compiler_params=pltpu.CompilerParams(vmem_limit_bytes=need),
        cost_estimate=pl.CostEstimate(flops=1000, bytes_accessed=1000, transcendentals=0),
    )(*prefetch, *[value for value, _ in inputs], *after, *carry)
    return list(results_)


def pack_kernel(order, sx, qkv, fc1, dense, fc2, near1, near3, far2, own, to_y, to_z):
    step = pl.program_id(0)
    x = sx[0]

    def write(put, parts):
        fc2_t = fc2[...].T
        dense_t = dense[...].T
        for s in range(parts):

            def pick(low, high, s=s):
                return jnp.where(x == s, low, high)

            put(s, 0, pick(fc2_t[:256], fc2_t[256:]))
            put(s, 256, pick(fc1[:256], fc1[256:]))
            for part in range(3):
                put(s, 512 + 64 * part, pick(qkv[part, :64], qkv[part, 64:]))
            put(s, 704, pick(dense_t[:64], dense_t[64:]))

    def both(ref):
        def put(s, row, value):
            ref[s, row : row + value.shape[0], :] = value

        return put

    def one(ref):
        def put(s, row, value):
            ref[row : row + value.shape[0], :] = value

        return put

    for at, (ref, parts) in enumerate(((near3, 1), (near1, 2), (far2, 1), (own, 2))):

        @pl.when(step == at)
        def _(ref=ref, parts=parts):
            write(both(ref) if parts == 2 else one(ref), parts)

    @pl.when(step == 2)
    def _():
        to_y[0] = far2[:EARLY, :]

    @pl.when(step == 3)
    def _():
        to_z[0] = own[0, :EARLY, :]


EARLY = 528


def pack(order, sx, qkv, fc1, dense, fc2):
    return call(
        pack_kernel,
        (4,),
        [
            (qkv, pl.BlockSpec((3, 128, 512), lambda i, o, x: (0, o[i], 0))),
            (fc1, pl.BlockSpec((512, 512), lambda i, o, x: (o[i], 0))),
            (dense, pl.BlockSpec((512, 128), lambda i, o, x: (0, o[i]))),
            (fc2, pl.BlockSpec((512, 512), lambda i, o, x: (0, o[i]))),
        ],
        [
            (shape(2, 768, 512), whole(2, 768, 512)),
            (shape(768, 512), whole(768, 512)),
            (shape(768, 512), whole(768, 512)),
            (shape(2, 768, 512), whole(2, 768, 512)),
            (shape(1, EARLY, 512), whole(1, EARLY, 512)),
            (shape(1, EARLY, 512), whole(1, EARLY, 512)),
        ],
        large=True,
        prefetch=(order, sx),
    )


def split_first(near3, near1, after=()):
    def body(near3, near1, mlp_y, mlp_z):
        mlp_y[0] = near3[...]
        mlp_z[0] = near1[0]

    mlp_out = (shape(1, 512, 512), whole(1, 512, 512))
    return call(
        body,
        (1,),
        [(near3, whole(512, 512)), (near1, whole(1, 512, 512))],
        [mlp_out, mlp_out],
        after=after,
    )


def stack_mlp(y2, y3, z0, z1, far2, near3, own, near1, after=()):
    def body(y2, y3, z0, z1, far2, near3, own, near1, to_x, to_z, att_y, att_z):
        for at, ref in enumerate((y2, y3, z0, z1)):
            to_x[at] = ref[0, :512, :]
            if at < 2:
                to_z[at] = ref[0, :512, :]
        att_y[0] = far2[...]
        att_y[1] = near3[...]
        att_z[0] = own[0]
        att_z[1] = near1[0]

    flat = pl.BlockSpec((256, 512), lambda *_: (2, 0))
    deep = pl.BlockSpec((1, 256, 512), lambda *_: (0, 2, 0))
    att_out = (shape(2, 256, 512), whole(2, 256, 512))
    return call(
        body,
        (1,),
        [(value, whole(*value.shape)) for value in (y2, y3, z0, z1)]
        + [(far2, flat), (near3, flat), (own, deep), (near1, deep)],
        [
            (shape(4, 512, 512), whole(4, 512, 512)),
            (shape(2, 512, 512), whole(2, 512, 512)),
            att_out,
            att_out,
        ],
        after=after,
    )


def gate(after, carry):
    def body(out):
        out[...] = jnp.zeros_like(out)

    token, *carry = call(
        body, (1,), [], [(shape(8, 128, dtype=F32), whole(8, 128))], after=after, carry=carry
    )
    return token, carry


def piece(array, lead, row, rows=256):
    return (
        array,
        pl.BlockSpec(
            (1, rows, 512),
            lambda *_: (lead, row, 0),
            pipeline_mode=pl.Buffered(buffer_count=1),
        ),
    )


def unpack(place, sx, pieces, select, outputs, store, after=()):
    count = len(pieces) // 2

    def body(place, sx, *refs):
        for r in range(4):

            @pl.when(place[pl.program_id(0)] == r)
            def _(r=r):
                a = select(refs[:count], r).astype(F32)
                b = select(refs[count : 2 * count], r).astype(F32)
                store(jnp.where(sx[0] == 0, a, b), jnp.where(sx[0] == 0, b, a), *refs[2 * count :])

    return call(
        body,
        (4,),
        [(value, whole(*value.shape)) for value in pieces],
        outputs,
        prefetch=(place, sx),
        after=after,
    )


def unpack_fc2(place, sx, pieces, after=()):
    def store(low, high, out):
        out[:, :256] = low.T
        out[:, 256:] = high.T

    block = pl.BlockSpec((512, 512), lambda i, o, x: (0, i))
    out = [(shape(512, 2048, dtype=F32), block)]
    return unpack(place, sx, pieces, lambda refs, r: refs[r // 2][2 * (r % 2)], out, store, after)[0]


def unpack_fc1(place, sx, pieces, after=()):
    def store(low, high, out):
        out[:256, :] = low
        out[256:, :] = high

    block = pl.BlockSpec((512, 512), lambda i, o, x: (i, 0))
    out = [(shape(2048, 512, dtype=F32), block)]
    return unpack(place, sx, pieces, lambda refs, r: refs[r // 2][2 * (r % 2) + 1], out, store, after)[0]


def unpack_att(place, sx, pieces, after=()):
    def store(low, high, qkv_out, dense_out):
        for part in range(3):
            qkv_out[part, :64, :] = low[64 * part : 64 * part + 64]
            qkv_out[part, 64:, :] = high[64 * part : 64 * part + 64]
        dense_out[...] = jnp.concatenate([low[192:], high[192:]], axis=0).T

    outputs = [
        (shape(3, 512, 512, dtype=F32), pl.BlockSpec((3, 128, 512), lambda i, o, x: (0, i, 0))),
        (shape(512, 512, dtype=F32), pl.BlockSpec((512, 128), lambda i, o, x: (0, i))),
    ]
    return unpack(place, sx, pieces, lambda refs, r: refs[0][r], outputs, store, after)


def norm_kernel(place, xs, scale, normed, stats):
    total = jnp.zeros((256, 1), F32)
    square = jnp.zeros((256, 1), F32)
    for q in range(4):
        value = xs[0, q].astype(F32)
        total += jnp.sum(value, axis=1, keepdims=True)
        square += jnp.sum(value * value, axis=1, keepdims=True)
    average = total / MODEL_WIDTH
    inverse = lax.rsqrt(square / MODEL_WIDTH - average * average + EPSILON)
    for r in range(4):
        value = xs[0, place[r]].astype(F32)
        centered = (value - average) * inverse
        normed[:, 512 * r : 512 * r + 512] = (
            centered * scale[2 * r : 2 * r + 1, :] + scale[2 * r + 1 : 2 * r + 2, :]
        ).astype(BF)
    stats[:, :128] = jnp.broadcast_to(average, (256, 128))
    stats[:, 128:] = jnp.broadcast_to(inverse, (256, 128))


def norm_tokens(place, gathered, scale, after=()):
    return call(
        norm_kernel,
        (8,),
        [
            (gathered, pl.BlockSpec((1, 4, 256, 512), lambda i, o: (i // 4, 0, i % 4, 0))),
            (scale, whole(8, 512)),
        ],
        [
            (shape(SEQ, MODEL_WIDTH), pl.BlockSpec((256, 2048), lambda i, o: (i, 0))),
            (shape(SEQ, 256, dtype=F32), pl.BlockSpec((256, 256), lambda i, o: (i, 0))),
        ],
        prefetch=(place,),
        large=True,
        after=after,
    )


ROOT = math.sqrt(2.0 / math.pi)
CUBIC = 0.044715
TILE = 512
HALF = SEQ // 2


def token_inputs(normed, cot):
    per = HALF // TILE
    return [
        (normed, pl.BlockSpec((TILE, MODEL_WIDTH), lambda i, *_: (i, 0))),
        (cot, pl.BlockSpec((1, 4, TILE, 512), lambda i, *_: (i // per, 0, i % per, 0))),
    ]


def store_grad(out, row, value):
    for at, r in enumerate((0, 2, 1, 3)):
        out[at, row : row + value.shape[0], :] = value[:, 512 * r : 512 * r + 512].astype(BF)


def units_kernel(n, *refs):
    weights, (bias, act_out, slope_out, w1) = refs[:8], refs[8:]

    @pl.when(pl.program_id(0) == 0)
    def _():
        for s in range(2):
            for r in range(4):
                rows, cols = slice(256 * s, 256 * s + 256), slice(512 * r, 512 * r + 512)
                w1[rows, cols] = weights[4 * s + r][0]

    def part(k, carry):
        rows = pl.ds(pl.multiple_of(k * 256, 256), 256)
        pre = nt(n[rows, :], w1[...]) + bias[...]
        square = pre * pre
        angle = jnp.tanh(ROOT * pre * (1.0 + CUBIC * square))
        half = 0.5 * (1.0 + angle)
        act_out[rows, :] = (pre * half).astype(BF)
        slope = half + 0.5 * pre * (1.0 - angle * angle) * (ROOT * (1.0 + 3.0 * CUBIC * square))
        slope_out[rows, :] = slope.astype(BF)
        return carry

    lax.fori_loop(0, TILE // 256, part, 0)


def hidden_units(normed, weights, bias, after=()):
    units = pl.BlockSpec((TILE, 512), lambda i, *_: (i, 0))
    return call(
        units_kernel,
        (SEQ // TILE,),
        [(normed, pl.BlockSpec((TILE, MODEL_WIDTH), lambda i, *_: (i, 0)))]
        + [piece(array, lead, 1) for array, lead in weights]
        + [(bias, whole(1, 512))],
        [(shape(SEQ, 512), units)] * 2,
        [pltpu.VMEM((512, MODEL_WIDTH), BF)],
        large=True,
        after=after,
    )


def mlp_kernel(place, n, c, act, slope, *refs):
    weights, (dfc_out, *grads, sums, w2, acc1, acc2) = refs[:8], refs[8:]
    step = pl.program_id(0)

    @pl.when(step == 0)
    def _():
        acc1[...] = jnp.zeros_like(acc1)
        acc2[...] = jnp.zeros_like(acc2)
        sums[...] = jnp.zeros_like(sums)
        for s in range(2):
            for r in range(4):
                rows, cols = slice(256 * s, 256 * s + 256), slice(512 * r, 512 * r + 512)
                w2[rows, cols] = weights[4 * s + r][0]

    back = jnp.zeros((TILE, 512), F32)
    for r in range(4):
        back += nt(c[0, place[r]], w2[:, 512 * r : 512 * r + 512])
    dfc = back * slope[...].astype(F32)
    sums[...] += jnp.sum(dfc, axis=0, keepdims=True)
    dfc = dfc.astype(BF)
    dfc_out[...] = dfc
    for r in range(4):
        acc2[:, 512 * r : 512 * r + 512] += tn(act[...], c[0, place[r]])
    acc1[...] += tn(dfc, n[...])

    @pl.when(step == SEQ // TILE - 1)
    def _():
        for s in range(2):
            store_grad(grads[s], 0, acc2[256 * s : 256 * s + 256])
            store_grad(grads[2 + s], 0, acc1[256 * s : 256 * s + 256])


def mlp(place, normed, cot, act, slope, weights, after=()):
    units = pl.BlockSpec((TILE, 512), lambda i, *_: (i, 0))
    grad = (shape(4, 256, 512), whole(4, 256, 512))
    return call(
        mlp_kernel,
        (SEQ // TILE,),
        token_inputs(normed, cot)
        + [(act, units), (slope, units)]
        + [piece(array, lead, 0) for array, lead in weights],
        [(shape(SEQ, 512), units)] + [grad] * 4 + [(shape(1, 512, dtype=F32), whole(1, 512))],
        [
            pltpu.VMEM((512, MODEL_WIDTH), BF),
            pltpu.VMEM((512, MODEL_WIDTH), F32),
            pltpu.VMEM((512, MODEL_WIDTH), F32),
        ],
        prefetch=(place,),
        large=True,
        after=after,
    )


def rotated(value, tables, sign):
    return (
        value * tables[0]
        + pltpu.roll(value, 112, 1) * (sign * tables[1])
        + pltpu.roll(value, 16, 1) * (sign * tables[2])
    )


def rotary_tables(cosine, sine, after=()):
    half = ROT // 2

    def body(cosine, sine, out):
        line = lax.broadcasted_iota(jnp.int32, (half, 128), 0)
        lane = lax.broadcasted_iota(jnp.int32, (half, 128), 1) % HEAD_DIM
        first = jnp.where(lane == line, 1.0, 0.0)
        second = jnp.where(lane == line + half, 1.0, 0.0)

        def spread(value, places):
            return jnp.dot(
                value, places, precision=lax.Precision.HIGHEST, preferred_element_type=F32
            )

        feature = lax.broadcasted_iota(jnp.int32, (TILE, 128), 1) % HEAD_DIM
        out[0] = jnp.where(feature < ROT, spread(cosine[...], first + second), 1.0)
        out[1] = spread(sine[...], -first)
        out[2] = spread(sine[...], second)

    rows = pl.BlockSpec((TILE, half), lambda i: (i, 0))
    return call(
        body,
        (SEQ // TILE,),
        [(cosine, rows), (sine, rows)],
        [(shape(3, SEQ, 128, dtype=F32), pl.BlockSpec((3, TILE, 128), lambda i: (0, i, 0)))],
        after=after,
    )[0]


def heads_kernel(place, n, c, *refs):
    weights, (bias, tables, q_out, k_out, v0_out, v1_out, d_out, joined) = refs[:8], refs[8:]

    @pl.when(pl.program_id(0) == 0)
    def _():
        for s in range(2):
            for r in range(4):
                for part in range(4):
                    row = 128 * part + 64 * s
                    joined[row : row + 64, 512 * r : 512 * r + 512] = weights[4 * s + r][
                        0, 64 * part : 64 * part + 64, :
                    ]

    pre = nt(n[...], joined[:384]) + bias[...]
    q_out[...] = (rotated(pre[:, :128], tables, 1.0) * SCALE).astype(BF)
    k_out[...] = rotated(pre[:, 128:256], tables, 1.0).astype(BF)
    value = pre[:, 256:].astype(BF)
    lane = lax.broadcasted_iota(jnp.int32, value.shape, 1)
    one = jnp.ones_like(value)
    v0_out[...] = jnp.where(lane < HEAD_DIM, value, one)
    v1_out[...] = jnp.where(lane < HEAD_DIM, one, value)
    back = jnp.zeros((TILE, 128), F32)
    for r in range(4):
        back += nt(c[0, place[r]], joined[384:, 512 * r : 512 * r + 512])
    d_out[...] = back.astype(BF)


def heads(place, normed, cot, weights, bias, tables, after=()):
    head = pl.BlockSpec((TILE, 128), lambda i, *_: (i, 0))
    return call(
        heads_kernel,
        (SEQ // TILE,),
        token_inputs(normed, cot)
        + [piece(*weight) for weight in weights]
        + [
            (bias, whole(1, 384)),
            (tables, pl.BlockSpec((3, TILE, 128), lambda i, *_: (0, i, 0))),
        ],
        [(shape(SEQ, 128), head)] * 5,
        [pltpu.VMEM((512, MODEL_WIDTH), BF)],
        prefetch=(place,),
        large=True,
        after=after,
    )


BLOCK = 512
BLOCKS = SEQ // BLOCK


def attend_kernel(low, *refs):
    ins, (start, tables), refs = refs[:10], refs[10:12], refs[12:]
    outs, refs = refs[:10], refs[10:]
    scores, probs, dk_acc, dv_acc, peak_acc, o_acc, dq_acc = refs
    i = pl.program_id(0)

    @pl.when(i == 0)
    def _():
        dk_acc[...] = jnp.zeros_like(dk_acc)
        dv_acc[...] = jnp.zeros_like(dv_acc)
        for block in range(2):
            outs[5 * block + 4][...] = jnp.zeros_like(outs[5 * block + 4])

    lane = lax.broadcasted_iota(jnp.int32, (BLOCK, 128), 1)
    masks = (lane < HEAD_DIM, lane >= HEAD_DIM)
    zero = jnp.zeros((BLOCK, 128), BF)
    queries = [jnp.where(masks[h % 2], ins[5 * (h // 2)][...], zero) for h in range(4)]
    keys = [ins[5 * (h // 2) + 1] for h in range(4)]
    values = [ins[5 * (h // 2) + 2 + h % 2] for h in range(4)]
    col = lax.broadcasted_iota(jnp.int32, (BLOCK, BLOCK), 1)
    row = lax.broadcasted_iota(jnp.int32, (BLOCK, BLOCK), 0) + i * BLOCK
    begin = start[:, :1]

    def each(step):
        for j in range(BLOCKS):

            @pl.when((j >= low[i]) & (j <= i))
            def _(j=j):
                step(j, slice(j * BLOCK, j * BLOCK + BLOCK))

    peak_acc[...] = jnp.full_like(peak_acc, MASKED)
    o_acc[...] = jnp.zeros_like(o_acc)
    dq_acc[...] = jnp.zeros_like(dq_acc)

    def score(j, at):
        here = col + j * BLOCK
        allowed = (here >= begin) & (here <= row)
        for h in range(4):
            s = jnp.where(allowed, nt(queries[h], keys[h][at, :]), MASKED)
            scores[h, j] = s
            peak = peak_acc[h]
            for lanes in range(0, BLOCK, 128):
                peak = jnp.maximum(peak, s[:, lanes : lanes + 128])
            peak_acc[h] = peak

    each(score)
    peaks = [jnp.max(peak_acc[h], axis=1, keepdims=True) for h in range(4)]

    def weigh(j, at):
        for h in range(4):
            p = jnp.exp(scores[h, j] - peaks[h]).astype(BF)
            probs[h, j] = p
            o_acc[h] += nn(p, values[h][at, :])

    each(weigh)
    grads, shifted = [], []
    for block in range(2):
        scaled = []
        for h in range(2):
            out = o_acc[2 * block + h]
            first = HEAD_DIM * (1 - h)
            inverse = 1.0 / out[:, first : first + 1]
            out = out * inverse
            grad = jnp.where(masks[h], ins[5 * block + 4][...].astype(F32) * inverse, 0.0).astype(BF)
            wide = grad.astype(F32)
            delta = jnp.sum(wide * out, axis=1, keepdims=True)
            coarse = delta.astype(BF).astype(F32)
            wide = jnp.where(lane == first, -coarse, wide)
            shifted.append(jnp.where(lane == first + 1, coarse - delta, wide).astype(BF))
            grads.append(grad)
            scaled.append(out)
        outs[5 * block][...] = jnp.where(masks[0], *scaled).astype(BF)

    def back(j, at):
        for h in range(4):
            p = probs[h, j]
            d_scores = (p.astype(F32) * nt(shifted[h], values[h][at, :])).astype(BF)
            dq_acc[h] += nn(d_scores, keys[h][at, :])
            dk_acc[h // 2, at, :] += tn(d_scores, queries[h])
            dv_acc[h // 2, at, :] += tn(p, grads[h])

    each(back)
    rows = pl.ds(pl.multiple_of(i * BLOCK, BLOCK), BLOCK)
    for block in range(2):
        dq = jnp.where(masks[0], dq_acc[2 * block], dq_acc[2 * block + 1]) * SCALE
        dq = rotated(dq, [tables[t, rows, :] for t in range(3)], -1.0)
        outs[5 * block + 1][...] = dq.astype(BF)
        outs[5 * block + 4][0:1, :] += jnp.sum(dq, axis=0, keepdims=True)

    @pl.when(i == BLOCKS - 1)
    def _():
        for block in range(2):
            _, _, dk_out, dv_out, sums = outs[5 * block : 5 * block + 5]
            for j in range(8):
                rows = slice(j * 256, j * 256 + 256)
                dk = rotated(dk_acc[block, rows], [tables[t, rows] for t in range(3)], -1.0)
                dv = dv_acc[block, rows]
                dk_out[rows, :] = dk.astype(BF)
                dv_out[rows, :] = dv.astype(BF)
                sums[1:2, :] += jnp.sum(dk, axis=0, keepdims=True)
                sums[2:3, :] += jnp.sum(dv, axis=0, keepdims=True)


def attend(low, heads, start, tables, after=()):
    tile = pl.BlockSpec((BLOCK, 128), lambda i, o: (i, 0))
    full = whole(SEQ, 128)
    head = shape(SEQ, 128)
    return call(
        attend_kernel,
        (BLOCKS,),
        [(value, (tile, full, full, full, tile)[at % 5]) for at, value in enumerate(heads)]
        + [(start, tile), (tables, whole(3, SEQ, 128))],
        [
            (head, tile),
            (head, tile),
            (head, full),
            (head, full),
            (shape(8, 128, dtype=F32), whole(8, 128)),
        ]
        * 2,
        [
            pltpu.VMEM((4, BLOCKS, BLOCK, BLOCK), F32),
            pltpu.VMEM((4, BLOCKS, BLOCK, BLOCK), BF),
            pltpu.VMEM((2, SEQ, 128), F32),
            pltpu.VMEM((2, SEQ, 128), F32),
            pltpu.VMEM((4, BLOCK, 128), F32),
            pltpu.VMEM((4, BLOCK, 128), F32),
            pltpu.VMEM((4, BLOCK, 128), F32),
        ],
        prefetch=(low,),
        large=True,
        after=after,
    )


def att_grad_kernel(place, n, c, dq, dk, dv, o, grad0, grad1, grad2, acc):
    step = pl.program_id(0)

    @pl.when(step == 0)
    def _():
        acc[...] = jnp.zeros_like(acc)

    acc[:384] += tn(jnp.concatenate([dq[...], dk[...], dv[...]], axis=1), n[...])
    for r in range(4):
        acc[384:, 512 * r : 512 * r + 512] += tn(o[...], c[0, place[r]])

    @pl.when(step == SEQ // TILE - 1)
    def _():
        for part in range(4):
            row, rows = 128 * part, slice(64 * part, 64 * part + 64)
            store_grad(grad0, 64 * part, acc[row : row + 64])
            value = acc[row + 64 : row + 128]
            for at, (grad, r) in enumerate(((grad1, 0), (grad1, 2), (grad2, 1), (grad2, 3))):
                grad[at % 2, rows, :] = value[:, 512 * r : 512 * r + 512].astype(BF)


def att_grad(place, normed, cot, dq, dk, dv, o, after=()):
    head = pl.BlockSpec((TILE, 128), lambda i, *_: (i, 0))
    return call(
        att_grad_kernel,
        (SEQ // TILE,),
        token_inputs(normed, cot) + [(value, head) for value in (dq, dk, dv, o)],
        [(shape(4, 256, 512), whole(4, 256, 512))] + [(shape(2, 256, 512), whole(2, 256, 512))] * 2,
        [pltpu.VMEM((512, MODEL_WIDTH), F32)],
        prefetch=(place,),
        large=True,
        after=after,
    )


def join(joined, spans, rights):
    row = 0
    for at, (first, size) in enumerate(spans):
        for r in range(4):
            joined[row : row + size, 512 * r : 512 * r + 512] = rights[4 * at + r][
                0, first : first + size, :
            ]
        row += size


def project(prefetch, items, tokens, outputs, store, after=()):
    lefts = [left for left, _ in items]
    parts = [part for _, rows in items for part in rows]
    spans = [(first, size) for _, first, size in parts]
    rights = [piece(*one) for pieces, _, _ in parts for one in pieces]

    def body(*refs):
        scalars, refs = refs[: len(prefetch)], refs[len(prefetch) :]
        left_refs, refs = refs[: len(lefts)], refs[len(lefts) :]
        right_refs, refs = refs[: len(rights)], refs[len(rights) :]
        *outs, joined = refs

        @pl.when(pl.program_id(0) == 0)
        def _():
            join(joined, spans, right_refs)

        left = jnp.concatenate([ref[...] for ref in left_refs], axis=1)
        store(scalars, outs, lambda r: nn(left, joined[:, 512 * r : 512 * r + 512]).astype(BF))

    return call(
        body,
        (SEQ // TILE,),
        [(left, pl.BlockSpec((TILE, left.shape[1]), tokens)) for left in lefts] + rights,
        outputs,
        [pltpu.VMEM((sum(size for _, size in spans), MODEL_WIDTH), BF)],
        prefetch=prefetch,
        large=True,
        after=after,
    )


def project_near(sz, items, after=()):
    per = HALF // TILE

    def store(scalars, outs, value):
        for out, pieces in zip(outs, ((1, 3), (0, 2)), strict=True):
            for at, r in enumerate(pieces):
                out[at, 0] = value(r)

    out = pl.BlockSpec((2, 1, TILE, 512), lambda i, *_: (0, i // per, i % per, 0))
    return project(
        (sz,),
        items,
        lambda i, s: (((i // per) ^ s[0]) * per + i % per, 0),
        [(shape(2, 2, HALF, 512), out)] * 2,
        store,
        after,
    )


def added(values):
    total = values[0].astype(F32)
    for value in values[1:]:
        total = total + value.astype(F32)
    return total.astype(BF)


def grad_inputs(values):
    inputs, reads = [], []
    for value in values:
        at = len(inputs)
        if isinstance(value, list):
            inputs += [(one, whole(2, 256, 512)) for one in value]
            reads.append(lambda refs, step, at=at: refs[at + step // 2][step % 2])
        else:
            inputs.append((value, whole(4, 256, 512)))
            reads.append(lambda refs, step, at=at: refs[at][step])
    return inputs, reads


def add(left, right, after=()):
    inputs, reads = grad_inputs([left, right])

    def body(*refs):
        for step in range(4):
            refs[-1][step] = added([read(refs, step) for read in reads])

    return call(
        body, (1,), inputs, [(shape(4, 256, 512), whole(4, 256, 512))], after=after
    )


def total_grad(groups, after=()):
    inputs, reads = [], []
    for group in groups:
        found, read = grad_inputs(group)
        reads.append((len(inputs), len(found), read))
        inputs += found
    rows = 256 * len(groups)

    def body(*refs):
        near, same = refs[-2:]
        for step in range(4):
            out = same if step < 2 else near
            for g, (at, size, read) in enumerate(reads):
                mine = refs[at : at + size]
                out[step % 2, 256 * g : 256 * g + 256, :] = added([one(mine, step) for one in read])

    out = (shape(2, rows, 512), whole(2, rows, 512))
    return call(body, (1,), inputs, [out, out], after=after)


def quarters(value):
    return [value[256 * k : 256 * k + 256, :] for k in range(value.shape[0] // 256)]


def blocks(count):
    return (shape(count, 256, 512), whole(count, 256, 512))


FLAT = (shape(HALF, 512), whole(HALF, 512))


def quarter(array, piece, half):
    return (array, pl.BlockSpec((1, 1, HALF, 512), lambda *_: (piece, half, 0, 0)))


def scatter_far(same, near, counts, grad, after=()):
    over_z, over_y = counts
    groups = grad[0].shape[1] // 256

    def body(same, near, grad_same, grad_near, to_z, to_y, to_x):
        far = quarters(added([same[0, 0], near[0, 0]]))
        for k in range(over_z):
            to_z[k] = far[k]
        for k in range(over_y):
            to_y[k] = far[over_z + k]
        for at, ref in enumerate((grad_same, grad_near)):
            for g in range(groups):
                rows = slice(256 * g, 256 * g + 256)
                to_x[groups * at + g] = ref[0, rows, :]
                to_y[over_y + groups * at + g] = ref[1, rows, :]

    pair = whole(2, 256 * groups, 512)
    return call(
        body,
        (1,),
        [quarter(same, 1, 1), quarter(near, 1, 1), (grad[0], pair), (grad[1], pair)],
        [blocks(over_z), blocks(over_y + 2 * groups), blocks(2 * groups)],
        after=after,
    )


def scatter_kept(same, near, after=(), carry=()):
    places = ((0, 0), (1, 0), (0, 1))

    def body(*refs):
        for at in range(3):
            refs[6 + at][...] = added([refs[2 * at][0, 0], refs[2 * at + 1][0, 0]])

    return call(
        body,
        (1,),
        [quarter(value, *place) for place in places for value in (same, near)],
        [FLAT] * 3,
        after=after,
        carry=carry,
    )


def scatter_second(for_y, from_z, after=()):
    def body(for_y, from_z, to_y):
        for k in range(4):
            rows = slice(256 * k, 256 * k + 256)
            to_y[rows, :] = added([for_y[rows, :], from_z[k]])

    return call(
        body,
        (1,),
        [(for_y, FLAT[1]), (from_z, whole(4, 256, 512))],
        [FLAT],
        after=after,
    )[0]


def scatter_last(for_y, from_z, for_z, from_y, near_grad, after=()):
    def body(for_y, from_z, for_z, from_y, near_grad, to_z, to_y, grad):
        for k in range(4):
            rows = slice(256 * k, 256 * k + 256)
            to_y[rows, :] = added([for_y[rows, :], from_z[k]]) if k < 3 else for_y[rows, :]
            to_z[rows, :] = for_z[rows, :] if k < 3 else added([for_z[rows, :], from_y[0]])
        for k in range(2):
            grad[k] = near_grad[k]
            grad[2 + k] = from_y[1 + k]

    three = whole(3, 256, 512)
    return call(
        body,
        (1,),
        [
            (for_y, FLAT[1]),
            (from_z, three),
            (for_z, FLAT[1]),
            (from_y, three),
            (near_grad, whole(2, 256, 512)),
        ],
        [FLAT, FLAT, blocks(4)],
        after=after,
    )


def more_dp(value):
    if lax.axis_size("xo") > 1:
        return lax.psum(value, "xo")
    return value


def on_device(
    block_input,
    cotangent,
    doc_lengths,
    layernorm_gain,
    layernorm_bias,
    qkv_weight,
    qkv_bias,
    fc1_weight,
    fc1_bias,
    dense_weight,
    fc2_weight,
    out_bias,
):
    x, zh, zl = lax.axis_index("x"), lax.axis_index("zh"), lax.axis_index("zl")
    here = 2 * lax.axis_index("y") + lax.axis_index("c")
    place = jnp.stack([here ^ r for r in range(4)]).astype(jnp.int32)
    sx = x.astype(jnp.int32).reshape(1)
    sz = zl.astype(jnp.int32).reshape(1)

    tokens = lax.all_gather(block_input, ("zl", "y", "c"), axis=0, tiled=False)
    cot = lax.all_gather(cotangent, ("zl", "y", "c"), axis=0, tiled=False)
    tokens, cot = (value.reshape(2, 4, HALF, 512) for value in (tokens, cot))

    scale = jnp.stack([layernorm_gain, layernorm_bias])
    scale = jnp.concatenate([scale, swap(scale, "c")], axis=0)
    heads_bias = qkv_bias.reshape(3, 2, HEAD_DIM)
    units_bias = fc1_bias.reshape(2, 256)
    heads_bias = jnp.where(x == 0, heads_bias, heads_bias[:, ::-1])
    units_bias = jnp.where(x == 0, units_bias, units_bias[::-1])
    own_bias = jnp.concatenate([heads_bias.reshape(1, 384), units_bias.reshape(1, 512)], axis=1)

    order = jnp.stack([here ^ r for r in (3, 1, 2, 0)]).astype(jnp.int32)
    near1, near3, far2, r0, to_y2, to_z0 = pack(order, sx, qkv_weight, fc1_weight, dense_weight, fc2_weight)
    near3 = swap(near3, "c")
    r1 = swap(near1, "c")

    lengths = lax.dynamic_index_in_dim(doc_lengths, zh, 0, keepdims=False)
    ends = jnp.cumsum(lengths)
    spot = jnp.arange(SEQ, dtype=jnp.int32)
    begin = jnp.sum(jnp.where(spot[:, None] >= ends[None, :], lengths[None, :], 0), axis=1)
    low = (begin[::BLOCK] // BLOCK).astype(jnp.int32)
    start = jnp.broadcast_to(begin[:, None], (SEQ, 128)).astype(jnp.int32)
    freqs = jnp.exp(jnp.arange(ROT // 2, dtype=F32) * (-2.0 * math.log(10000.0) / ROT))
    angle = spot.astype(F32)[:, None] * freqs[None, :]
    cosine, sine = jnp.cos(angle), jnp.sin(angle)
    def rows(weights, row, first, size):
        return [
            ([(*one[:2], one[2] if row is None else row) for one in weights[4 * s : 4 * s + 4]], first, size)
            for s in range(2)
        ]

    input_single = block_input.astype(F32)
    branch_gradient = cotangent.astype(F32)

    from_y2, from_z0 = swap(to_y2, "y"), swap(to_z0, "zh")
    to_y3, to_z1 = split_first(near3, r1, after=[scale])
    from_y3, from_z1 = swap(to_y3, "y"), swap(to_z1, "zh")
    tables = rotary_tables(cosine, sine, after=[to_z1])
    scale = jnp.concatenate([scale, swap(scale, "y")], axis=0)
    token, (other_bias,) = gate(
        [tables, start, from_y2, from_z0, from_y3, from_z1], [own_bias]
    )

    to_x, to_z, att_y, att01 = stack_mlp(
        from_y2, from_y3, from_z0, from_z1, far2, near3, r0, r1, after=[token]
    )
    normed, stats = norm_tokens(place, tokens, scale, after=[to_x])
    att23, other_bias = swap(att_y, "y"), swap(other_bias, "zh")
    from_x, other23 = swap(to_x, "x"), swap(to_z, "zh")
    token, (other23, att23, att01) = gate([stats, from_x, other_bias], [other23, att23, att01])
    mine = lax.dynamic_slice_in_dim(stats, zl * HALF, HALF, axis=0)
    average, inverse = mine[:, :1], mine[:, 128:129]
    centered = (input_single - average) * inverse

    next23, att01 = swap(other23, "x"), swap(att01, "zh")
    own_w = [(r0, 0), (r1, 0), (from_y2, 0), (from_y3, 0)]
    own_w += [(r0, 1), (r1, 1), (from_x, 0), (from_x, 1)]
    own_act, own_slope = hidden_units(normed, own_w, own_bias[:, 384:], after=[token])
    token, (att01, att23) = gate([own_act, next23], [att01, att23])

    other_w = [(from_z0, 0), (from_z1, 0), (other23, 0), (other23, 1)]
    other_w += [(from_x, 2), (from_x, 3), (next23, 0), (next23, 1)]
    next_att01, other_att23, next_att23 = swap(att01, "x"), swap(att23, "zh"), swap(att23, "x")
    other_act, other_slope = hidden_units(normed, other_w, other_bias[:, 384:], after=[token])
    other_dfc, *other_mlp, other_units = mlp(
        place, normed, cot, other_act, other_slope, other_w
    )
    token, (other_att23, other_mlp[1]) = gate(
        [other_units, next_att01, next_att23], [other_att23, other_mlp[1]]
    )

    from_x, next_other23 = swap(other_mlp[1], "x"), swap(other_att23, "x")
    own_dfc, *own_mlp, own_units = mlp(
        place, normed, cot, own_act, own_slope, own_w, after=[token]
    )
    own_a = [(r0, 0, 2), (r1, 0, 2), (att23, 0, 0), (att23, 1, 0)]
    own_a += [(r0, 1, 2), (r1, 1, 2), (next_att23, 0, 0), (next_att23, 1, 0)]
    own_qkv = heads(place, normed, cot, own_a, own_bias[:, :384], tables, after=[own_units])
    token, (other_mlp[3], own_mlp[1]) = gate(
        [own_qkv[0], from_x, next_other23], [other_mlp[3], own_mlp[1]]
    )

    other_a = [
        (array, i, 0) for array in (att01, other_att23, next_att01, next_other23) for i in range(2)
    ]
    fc2 = add(other_mlp[0], from_x, after=[token])[0]
    to_fc2 = swap(fc2, "zh")
    from_x, own_fc2 = swap(other_mlp[3], "x"), swap(own_mlp[1], "x")
    other_qkv = heads(place, normed, cot, other_a, other_bias[:, :384], tables, after=[fc2])
    attended = attend(low, own_qkv + other_qkv, start, tables)
    own_o, own_dq, own_dk, own_dv, own_sums = attended[:5]
    other_o, other_dq, other_dk, other_dv, other_sums = attended[5:]
    other_sums = jnp.concatenate([other_sums[:3].reshape(1, 384), other_units], axis=1)
    token, (own_mlp[3], other_sums) = gate(
        [own_o, to_fc2, from_x, own_fc2], [own_mlp[3], other_sums]
    )

    fc1 = add(other_mlp[2], from_x, after=[token])[0]
    to_fc1 = swap(fc1, "zh")
    other_att = att_grad(
        place, normed, cot, other_dq, other_dk, other_dv, other_o, after=[fc1]
    )
    other_sums = swap(other_sums, "zh")
    from_x, own_fc1 = swap_all(other_att[1:], "x"), swap(own_mlp[3], "x")
    items = [(own_dfc, rows(own_w, 1, 0, 256)), (other_dfc, rows(other_w, 1, 0, 256))]
    for part, (left, right) in enumerate(
        ((own_dq, other_dq), (own_dk, other_dk), (own_dv, other_dv))
    ):
        items.append((left, rows(own_a, None, 64 * part, 64)))
        items.append((right, rows(other_a, None, 64 * part, 64)))
    dn_near, dn_same = project_near(sz, items, after=[other_att[0]])
    own_sums = jnp.concatenate([own_sums[:3].reshape(1, 384), own_units], axis=1)
    token, (dn_near,) = gate([dn_same, own_sums, to_fc1, *from_x, own_fc1, other_sums], [dn_near])

    sums = own_sums + other_sums
    heads_sum, units_sum = sums[0, :384].reshape(3, 2, HEAD_DIM), sums[0, 384:].reshape(2, 256)
    heads_sum = jnp.where(x == 0, heads_sum, heads_sum[:, ::-1]).reshape(1, 384)
    units_sum = jnp.where(x == 0, units_sum, units_sum[::-1]).reshape(1, 512)
    sums = jnp.concatenate([heads_sum, units_sum], axis=1)
    dn_near, sums_x = swap(dn_near, "c"), swap(sums, "x")
    mlp_near, mlp_same = total_grad(
        [[own_mlp[0], own_fc2, to_fc2], [own_mlp[2], own_fc1, to_fc1]], after=[token]
    )
    mlp_near, mlp_same = swap(more_dp(mlp_near), "c"), more_dp(mlp_same)
    att = add(other_att[0], from_x, after=[mlp_same])[0]
    token, (att,) = gate([dn_near, mlp_near, sums_x], [att])

    to_z, to_y, mlp01 = scatter_far(
        dn_same, dn_near, (4, 0), (mlp_same, mlp_near), after=[token]
    )
    from_z, mlp23 = swap(to_z, "zl"), swap(to_y, "y")
    own_att = att_grad(place, normed, cot, own_dq, own_dk, own_dv, own_o, after=[to_z])
    dn, for_y, for_z = scatter_kept(dn_same, dn_near, after=[own_att[0]])
    own_from_att, to_att = swap_all(own_att[1:], "x"), swap(att, "zh")
    items = [
        (own_act, rows(own_w, 0, 0, 256)),
        (other_act, rows(other_w, 0, 0, 256)),
        (own_o, rows(own_a, None, 192, 64)),
        (other_o, rows(other_a, None, 192, 64)),
    ]
    near, same = project_near(sz, items, after=[dn])
    token, (near, mlp01, mlp23, for_z) = gate(
        [same, to_att, *own_from_att, from_z], [near, mlp01, mlp23, for_z]
    )

    near, dn_z, next01 = swap(near, "c"), swap(for_z, "zl"), swap(mlp01, "x")
    to_y = scatter_second(for_y, from_z, after=[token])
    dn_y = swap(to_y, "y")
    att_near, att_same = total_grad([[own_att[0], own_from_att, to_att]], after=[to_y])
    att_near, att_same = swap(more_dp(att_near), "c"), more_dp(att_same)
    token, (mlp23,) = gate([att_same, near, dn_z, dn_y, next01, att_near], [mlp23])

    next23 = swap(mlp23, "x")
    to_z, to_y, att01 = scatter_far(same, near, (3, 1), (att_same, att_near), after=[token])
    from_z, from_y = swap(to_z, "zl"), swap(to_y, "y")
    branch, branch_y, branch_z, dn_y = scatter_kept(same, near, after=[to_z], carry=[dn_y])
    dn = dn.astype(F32) + dn_y.astype(F32) + dn_z.astype(F32)
    row_sums = jnp.stack(
        [jnp.sum(dn * layernorm_gain, axis=1), jnp.sum(dn * layernorm_gain * centered, axis=1)]
    )
    col_sums = jnp.stack(
        [
            jnp.sum(dn * centered, axis=0),
            jnp.sum(dn, axis=0),
            jnp.sum(branch_gradient, axis=0),
        ]
    )
    row_sums = row_sums + swap(row_sums, "c")
    row_sums = row_sums + swap(row_sums, "y")
    col_sums = col_sums + swap(col_sums, "zl")
    token, (col_sums,) = gate([branch, from_z, from_y, next23, row_sums], [col_sums])

    to_z, to_y, att_pieces = scatter_last(
        branch_y, from_z, branch_z, from_y, att01, after=[token]
    )
    branch_z, branch_y = swap(to_z, "zl"), swap(to_y, "y")
    next_att = swap(att_pieces, "x")
    mlp_pieces = (mlp01, mlp23, next01, next23)
    fc2_grad = unpack_fc2(place, sx, mlp_pieces, after=[to_y])
    fc1_grad = unpack_fc1(place, sx, mlp_pieces, after=[fc2_grad])
    token, (col_sums,) = gate([fc1_grad], [col_sums])
    for axis in ("zh", "x"):
        col_sums = col_sums + swap(col_sums, axis)
    qkv_grad, dense_grad = unpack_att(place, sx, (att_pieces, next_att), after=[token])
    sums = more_dp(sums + sums_x)

    qkv_bias_grad, fc1_bias_grad = sums[0, :384].reshape(3, 128), sums[0, 384:]

    branch = branch.astype(F32) + branch_y.astype(F32) + branch_z.astype(F32)
    result = (input_single + (branch + out_bias)).astype(BF)
    input_grad = branch_gradient + inverse * (
        dn * layernorm_gain
        - row_sums[0][:, None] / MODEL_WIDTH
        - centered * (row_sums[1][:, None] / MODEL_WIDTH)
    )
    col_sums = more_dp(col_sums)
    return (
        result,
        input_grad,
        col_sums[0],
        col_sums[1],
        qkv_grad,
        qkv_bias_grad,
        fc1_grad,
        fc1_bias_grad,
        dense_grad,
        fc2_grad,
        col_sums[2],
    )


def solution(mesh):
    dp, row, col = mesh.devices.shape
    assert dp % 2 == 0 and row == 4 and col == 4
    parts = Mesh(
        mesh.devices.reshape(dp // 2, 2, 2, 2, 2, 2), ("xo", "x", "zh", "zl", "y", "c")
    )
    data, rows, cols = ("xo", "x"), ("zh", "zl"), ("y", "c")
    return jax.shard_map(
        on_device,
        mesh=parts,
        in_specs=(
            P(data + rows, cols),
            P(data + rows, cols),
            P(data, None),
            P(cols),
            P(cols),
            P(None, rows, cols),
            P(None, rows + cols),
            P(rows, cols),
            P(rows + cols),
            P(cols, rows),
            P(cols, rows),
            P(cols),
        ),
        out_specs=(
            P(data + rows, cols),
            P(data + rows, cols),
            P(cols),
            P(cols),
            P(None, rows, cols),
            P(None, rows + cols),
            P(rows, cols),
            P(rows + cols),
            P(cols, rows),
            P(cols, rows),
            P(cols),
        ),
        check_vma=False,
    )
```

```python
import math

import jax
import jax.numpy as jnp
from jax import lax
from jax.experimental import pallas as pl
from jax.experimental.pallas import tpu as pltpu
from jax.sharding import Mesh
from jax.sharding import PartitionSpec as P

MODEL_WIDTH = 2048
HEAD_DIM = 64
ROT = 32
SEQ = 2048
EPSILON = 1e-05
MASKED = -1e30
SCALE = HEAD_DIM ** (-0.5)
VMEM = 60 * 1024 * 1024
ROOM = 12 * 1024 * 1024

BF = jnp.bfloat16
F32 = jnp.float32


def swap(value, axis):
    return lax.ppermute(value, axis, [(0, 1), (1, 0)])


def swap_all(values, axis):
    return [swap(value, axis) for value in values]


def nt(left, right):
    return lax.dot_general(left, right, (((1,), (1,)), ((), ())), preferred_element_type=F32)


def tn(left, right):
    return lax.dot_general(left, right, (((0,), (0,)), ((), ())), preferred_element_type=F32)


def nn(left, right):
    return lax.dot_general(left, right, (((1,), (0,)), ((), ())), preferred_element_type=F32)


def shape(*dims, dtype=BF):
    return jax.ShapeDtypeStruct(dims, dtype)


def whole(*dims):
    return pl.BlockSpec(dims, lambda *_: (0,) * len(dims))


def call(body, grid, inputs, outputs, scratch=(), prefetch=(), after=(), carry=(), large=False):
    count, waits, kept = len(prefetch) + len(inputs), len(after) + len(carry), len(carry)
    results = len(outputs)

    def kernel(*refs):
        own, rest = refs[:count], refs[count + waits :]
        body(*own, *rest[:results], *rest[results + kept :])

    anywhere = pl.BlockSpec(memory_space=pl.ANY)
    need = sum(math.prod(ref.shape) * jnp.dtype(ref.dtype).itemsize for ref in scratch) + ROOM
    for spec, value in [(spec, value) for value, spec in inputs] + [(spec, out) for out, spec in outputs]:
        once = math.prod(spec.block_shape) * jnp.dtype(value.dtype).itemsize
        need += once if spec.pipeline_mode is not None else 2 * once
    need = VMEM if large else min(need, VMEM)
    results_ = pl.pallas_call(
        kernel,
        grid_spec=pltpu.PrefetchScalarGridSpec(
            num_scalar_prefetch=len(prefetch),
            grid=grid,
            in_specs=[spec for _, spec in inputs] + [anywhere] * waits,
            out_specs=[spec for _, spec in outputs] + [anywhere] * kept,
            scratch_shapes=list(scratch),
        ),
        out_shape=[out for out, _ in outputs] + [shape(*c.shape, dtype=c.dtype) for c in carry],
        input_output_aliases={count + len(after) + i: results + i for i in range(kept)},
        compiler_params=pltpu.CompilerParams(vmem_limit_bytes=need),
        cost_estimate=pl.CostEstimate(flops=1000, bytes_accessed=1000, transcendentals=0),
    )(*prefetch, *[value for value, _ in inputs], *after, *carry)
    return list(results_)


def pack_kernel(order, sx, qkv, fc1, dense, fc2, near1, near3, far2, own, to_y, to_z):
    step = pl.program_id(0)
    x = sx[0]

    def write(put, parts):
        fc2_t = fc2[...].T
        dense_t = dense[...].T
        for s in range(parts):

            def pick(low, high, s=s):
                return jnp.where(x == s, low, high)

            put(s, 0, pick(fc2_t[:256], fc2_t[256:]))
            put(s, 256, pick(fc1[:256], fc1[256:]))
            for part in range(3):
                put(s, 512 + 64 * part, pick(qkv[part, :64], qkv[part, 64:]))
            put(s, 704, pick(dense_t[:64], dense_t[64:]))

    def both(ref):
        def put(s, row, value):
            ref[s, row : row + value.shape[0], :] = value

        return put

    def one(ref):
        def put(s, row, value):
            ref[row : row + value.shape[0], :] = value

        return put

    for at, (ref, parts) in enumerate(((near3, 1), (near1, 2), (far2, 1), (own, 2))):

        @pl.when(step == at)
        def _(ref=ref, parts=parts):
            write(both(ref) if parts == 2 else one(ref), parts)

    @pl.when(step == 2)
    def _():
        to_y[0] = far2[:EARLY, :]

    @pl.when(step == 3)
    def _():
        to_z[0] = own[0, :EARLY, :]


EARLY = 528


def pack(order, sx, qkv, fc1, dense, fc2):
    return call(
        pack_kernel,
        (4,),
        [
            (qkv, pl.BlockSpec((3, 128, 512), lambda i, o, x: (0, o[i], 0))),
            (fc1, pl.BlockSpec((512, 512), lambda i, o, x: (o[i], 0))),
            (dense, pl.BlockSpec((512, 128), lambda i, o, x: (0, o[i]))),
            (fc2, pl.BlockSpec((512, 512), lambda i, o, x: (0, o[i]))),
        ],
        [
            (shape(2, 768, 512), whole(2, 768, 512)),
            (shape(768, 512), whole(768, 512)),
            (shape(768, 512), whole(768, 512)),
            (shape(2, 768, 512), whole(2, 768, 512)),
            (shape(1, EARLY, 512), whole(1, EARLY, 512)),
            (shape(1, EARLY, 512), whole(1, EARLY, 512)),
        ],
        large=True,
        prefetch=(order, sx),
    )


def split_first(near3, near1, after=()):
    def body(near3, near1, mlp_y, mlp_z):
        mlp_y[0] = near3[...]
        mlp_z[0] = near1[0]

    mlp_out = (shape(1, 512, 512), whole(1, 512, 512))
    return call(
        body,
        (1,),
        [(near3, whole(512, 512)), (near1, whole(1, 512, 512))],
        [mlp_out, mlp_out],
        after=after,
    )


def stack_mlp(y2, y3, z0, z1, far2, near3, own, near1, after=()):
    def body(y2, y3, z0, z1, far2, near3, own, near1, to_x, to_z, att_y, att_z):
        for at, ref in enumerate((y2, y3, z0, z1)):
            to_x[at] = ref[0, :512, :]
            if at < 2:
                to_z[at] = ref[0, :512, :]
        att_y[0] = far2[...]
        att_y[1] = near3[...]
        att_z[0] = own[0]
        att_z[1] = near1[0]

    flat = pl.BlockSpec((256, 512), lambda *_: (2, 0))
    deep = pl.BlockSpec((1, 256, 512), lambda *_: (0, 2, 0))
    att_out = (shape(2, 256, 512), whole(2, 256, 512))
    return call(
        body,
        (1,),
        [(value, whole(*value.shape)) for value in (y2, y3, z0, z1)]
        + [(far2, flat), (near3, flat), (own, deep), (near1, deep)],
        [
            (shape(4, 512, 512), whole(4, 512, 512)),
            (shape(2, 512, 512), whole(2, 512, 512)),
            att_out,
            att_out,
        ],
        after=after,
    )


def gate(after, carry):
    def body(out):
        out[...] = jnp.zeros_like(out)

    token, *carry = call(
        body, (1,), [], [(shape(8, 128, dtype=F32), whole(8, 128))], after=after, carry=carry
    )
    return token, carry


def piece(array, lead, row, rows=256):
    return (
        array,
        pl.BlockSpec(
            (1, rows, 512),
            lambda *_: (lead, row, 0),
            pipeline_mode=pl.Buffered(buffer_count=1),
        ),
    )


def unpack(place, sx, pieces, select, outputs, store, after=()):
    count = len(pieces) // 2

    def body(place, sx, *refs):
        for r in range(4):

            @pl.when(place[pl.program_id(0)] == r)
            def _(r=r):
                a = select(refs[:count], r).astype(F32)
                b = select(refs[count : 2 * count], r).astype(F32)
                store(jnp.where(sx[0] == 0, a, b), jnp.where(sx[0] == 0, b, a), *refs[2 * count :])

    return call(
        body,
        (4,),
        [(value, whole(*value.shape)) for value in pieces],
        outputs,
        prefetch=(place, sx),
        after=after,
    )


def unpack_fc2(place, sx, pieces, after=()):
    def store(low, high, out):
        out[:, :256] = low.T
        out[:, 256:] = high.T

    block = pl.BlockSpec((512, 512), lambda i, o, x: (0, i))
    out = [(shape(512, 2048, dtype=F32), block)]
    return unpack(place, sx, pieces, lambda refs, r: refs[r // 2][2 * (r % 2)], out, store, after)[0]


def unpack_fc1(place, sx, pieces, after=()):
    def store(low, high, out):
        out[:256, :] = low
        out[256:, :] = high

    block = pl.BlockSpec((512, 512), lambda i, o, x: (i, 0))
    out = [(shape(2048, 512, dtype=F32), block)]
    return unpack(place, sx, pieces, lambda refs, r: refs[r // 2][2 * (r % 2) + 1], out, store, after)[0]


def unpack_att(place, sx, pieces, after=()):
    def store(low, high, qkv_out, dense_out):
        for part in range(3):
            qkv_out[part, :64, :] = low[64 * part : 64 * part + 64]
            qkv_out[part, 64:, :] = high[64 * part : 64 * part + 64]
        dense_out[...] = jnp.concatenate([low[192:], high[192:]], axis=0).T

    outputs = [
        (shape(3, 512, 512, dtype=F32), pl.BlockSpec((3, 128, 512), lambda i, o, x: (0, i, 0))),
        (shape(512, 512, dtype=F32), pl.BlockSpec((512, 128), lambda i, o, x: (0, i))),
    ]
    return unpack(place, sx, pieces, lambda refs, r: refs[0][r], outputs, store, after)


def norm_kernel(place, xs, scale, normed, stats):
    total = jnp.zeros((256, 1), F32)
    square = jnp.zeros((256, 1), F32)
    for q in range(4):
        value = xs[0, q].astype(F32)
        total += jnp.sum(value, axis=1, keepdims=True)
        square += jnp.sum(value * value, axis=1, keepdims=True)
    average = total / MODEL_WIDTH
    inverse = lax.rsqrt(square / MODEL_WIDTH - average * average + EPSILON)
    for r in range(4):
        value = xs[0, place[r]].astype(F32)
        centered = (value - average) * inverse
        normed[:, 512 * r : 512 * r + 512] = (
            centered * scale[2 * r : 2 * r + 1, :] + scale[2 * r + 1 : 2 * r + 2, :]
        ).astype(BF)
    stats[:, :128] = jnp.broadcast_to(average, (256, 128))
    stats[:, 128:] = jnp.broadcast_to(inverse, (256, 128))


def norm_tokens(place, gathered, scale, after=()):
    return call(
        norm_kernel,
        (8,),
        [
            (gathered, pl.BlockSpec((1, 4, 256, 512), lambda i, o: (i // 4, 0, i % 4, 0))),
            (scale, whole(8, 512)),
        ],
        [
            (shape(SEQ, MODEL_WIDTH), pl.BlockSpec((256, 2048), lambda i, o: (i, 0))),
            (shape(SEQ, 256, dtype=F32), pl.BlockSpec((256, 256), lambda i, o: (i, 0))),
        ],
        prefetch=(place,),
        large=True,
        after=after,
    )


ROOT = math.sqrt(2.0 / math.pi)
CUBIC = 0.044715
TILE = 512
HALF = SEQ // 2


def token_inputs(normed, cot):
    per = HALF // TILE
    return [
        (normed, pl.BlockSpec((TILE, MODEL_WIDTH), lambda i, *_: (i, 0))),
        (cot, pl.BlockSpec((1, 4, TILE, 512), lambda i, *_: (i // per, 0, i % per, 0))),
    ]


def store_grad(out, row, value):
    for at, r in enumerate((0, 2, 1, 3)):
        out[at, row : row + value.shape[0], :] = value[:, 512 * r : 512 * r + 512].astype(BF)


def units_kernel(n, *refs):
    weights, (bias, act_out, slope_out, w1) = refs[:8], refs[8:]

    @pl.when(pl.program_id(0) == 0)
    def _():
        for s in range(2):
            for r in range(4):
                rows, cols = slice(256 * s, 256 * s + 256), slice(512 * r, 512 * r + 512)
                w1[rows, cols] = weights[4 * s + r][0]

    def part(k, carry):
        rows = pl.ds(pl.multiple_of(k * 256, 256), 256)
        pre = nt(n[rows, :], w1[...]) + bias[...]
        square = pre * pre
        angle = jnp.tanh(ROOT * pre * (1.0 + CUBIC * square))
        half = 0.5 * (1.0 + angle)
        act_out[rows, :] = (pre * half).astype(BF)
        slope = half + 0.5 * pre * (1.0 - angle * angle) * (ROOT * (1.0 + 3.0 * CUBIC * square))
        slope_out[rows, :] = slope.astype(BF)
        return carry

    lax.fori_loop(0, TILE // 256, part, 0)


def hidden_units(normed, weights, bias, after=()):
    units = pl.BlockSpec((TILE, 512), lambda i, *_: (i, 0))
    return call(
        units_kernel,
        (SEQ // TILE,),
        [(normed, pl.BlockSpec((TILE, MODEL_WIDTH), lambda i, *_: (i, 0)))]
        + [piece(array, lead, 1) for array, lead in weights]
        + [(bias, whole(1, 512))],
        [(shape(SEQ, 512), units)] * 2,
        [pltpu.VMEM((512, MODEL_WIDTH), BF)],
        after=after,
    )


def mlp_kernel(place, n, c, act, slope, *refs):
    weights, (dfc_out, *grads, sums, w2, acc1, acc2) = refs[:8], refs[8:]
    step = pl.program_id(0)

    @pl.when(step == 0)
    def _():
        acc1[...] = jnp.zeros_like(acc1)
        acc2[...] = jnp.zeros_like(acc2)
        sums[...] = jnp.zeros_like(sums)
        for s in range(2):
            for r in range(4):
                rows, cols = slice(256 * s, 256 * s + 256), slice(512 * r, 512 * r + 512)
                w2[rows, cols] = weights[4 * s + r][0]

    back = jnp.zeros((TILE, 512), F32)
    for r in range(4):
        back += nt(c[0, place[r]], w2[:, 512 * r : 512 * r + 512])
    dfc = back * slope[...].astype(F32)
    sums[...] += jnp.sum(dfc, axis=0, keepdims=True)
    dfc = dfc.astype(BF)
    dfc_out[...] = dfc
    for r in range(4):
        acc2[:, 512 * r : 512 * r + 512] += tn(act[...], c[0, place[r]])
    acc1[...] += tn(dfc, n[...])

    @pl.when(step == SEQ // TILE - 1)
    def _():
        for s in range(2):
            store_grad(grads[s], 0, acc2[256 * s : 256 * s + 256])
            store_grad(grads[2 + s], 0, acc1[256 * s : 256 * s + 256])


def mlp(place, normed, cot, act, slope, weights, after=()):
    units = pl.BlockSpec((TILE, 512), lambda i, *_: (i, 0))
    grad = (shape(4, 256, 512), whole(4, 256, 512))
    return call(
        mlp_kernel,
        (SEQ // TILE,),
        token_inputs(normed, cot)
        + [(act, units), (slope, units)]
        + [piece(array, lead, 0) for array, lead in weights],
        [(shape(SEQ, 512), units)] + [grad] * 4 + [(shape(1, 512, dtype=F32), whole(1, 512))],
        [
            pltpu.VMEM((512, MODEL_WIDTH), BF),
            pltpu.VMEM((512, MODEL_WIDTH), F32),
            pltpu.VMEM((512, MODEL_WIDTH), F32),
        ],
        prefetch=(place,),
        large=True,
        after=after,
    )


def rotated(value, tables, sign):
    return (
        value * tables[0]
        + pltpu.roll(value, 112, 1) * (sign * tables[1])
        + pltpu.roll(value, 16, 1) * (sign * tables[2])
    )


def rotary_tables(cosine, sine, after=()):
    half = ROT // 2

    def body(cosine, sine, out):
        line = lax.broadcasted_iota(jnp.int32, (half, 128), 0)
        lane = lax.broadcasted_iota(jnp.int32, (half, 128), 1) % HEAD_DIM
        first = jnp.where(lane == line, 1.0, 0.0)
        second = jnp.where(lane == line + half, 1.0, 0.0)

        def spread(value, places):
            return jnp.dot(
                value, places, precision=lax.Precision.HIGHEST, preferred_element_type=F32
            )

        feature = lax.broadcasted_iota(jnp.int32, (TILE, 128), 1) % HEAD_DIM
        out[0] = jnp.where(feature < ROT, spread(cosine[...], first + second), 1.0)
        out[1] = spread(sine[...], -first)
        out[2] = spread(sine[...], second)

    rows = pl.BlockSpec((TILE, half), lambda i: (i, 0))
    return call(
        body,
        (SEQ // TILE,),
        [(cosine, rows), (sine, rows)],
        [(shape(3, SEQ, 128, dtype=F32), pl.BlockSpec((3, TILE, 128), lambda i: (0, i, 0)))],
        after=after,
    )[0]


def heads_kernel(place, n, c, *refs):
    weights, (bias, tables, q_out, k_out, v0_out, v1_out, d_out, joined) = refs[:8], refs[8:]

    @pl.when(pl.program_id(0) == 0)
    def _():
        for s in range(2):
            for r in range(4):
                for part in range(4):
                    row = 128 * part + 64 * s
                    joined[row : row + 64, 512 * r : 512 * r + 512] = weights[4 * s + r][
                        0, 64 * part : 64 * part + 64, :
                    ]

    pre = nt(n[...], joined[:384]) + bias[...]
    q_out[...] = (rotated(pre[:, :128], tables, 1.0) * SCALE).astype(BF)
    k_out[...] = rotated(pre[:, 128:256], tables, 1.0).astype(BF)
    value = pre[:, 256:].astype(BF)
    lane = lax.broadcasted_iota(jnp.int32, value.shape, 1)
    one = jnp.ones_like(value)
    v0_out[...] = jnp.where(lane < HEAD_DIM, value, one)
    v1_out[...] = jnp.where(lane < HEAD_DIM, one, value)
    back = jnp.zeros((TILE, 128), F32)
    for r in range(4):
        back += nt(c[0, place[r]], joined[384:, 512 * r : 512 * r + 512])
    d_out[...] = back.astype(BF)


def heads(place, normed, cot, weights, bias, tables, after=()):
    head = pl.BlockSpec((TILE, 128), lambda i, *_: (i, 0))
    return call(
        heads_kernel,
        (SEQ // TILE,),
        token_inputs(normed, cot)
        + [piece(*weight) for weight in weights]
        + [
            (bias, whole(1, 384)),
            (tables, pl.BlockSpec((3, TILE, 128), lambda i, *_: (0, i, 0))),
        ],
        [(shape(SEQ, 128), head)] * 5,
        [pltpu.VMEM((512, MODEL_WIDTH), BF)],
        prefetch=(place,),
        large=True,
        after=after,
    )


BLOCK = 512
BLOCKS = SEQ // BLOCK


def attend_kernel(low, *refs):
    ins, (start, tables), refs = refs[:10], refs[10:12], refs[12:]
    outs, refs = refs[:10], refs[10:]
    scores, probs, dk_acc, dv_acc, peak_acc, o_acc, dq_acc = refs
    i = pl.program_id(0)

    @pl.when(i == 0)
    def _():
        dk_acc[...] = jnp.zeros_like(dk_acc)
        dv_acc[...] = jnp.zeros_like(dv_acc)
        for block in range(2):
            outs[5 * block + 4][...] = jnp.zeros_like(outs[5 * block + 4])

    lane = lax.broadcasted_iota(jnp.int32, (BLOCK, 128), 1)
    masks = (lane < HEAD_DIM, lane >= HEAD_DIM)
    zero = jnp.zeros((BLOCK, 128), BF)
    queries = [jnp.where(masks[h % 2], ins[5 * (h // 2)][...], zero) for h in range(4)]
    keys = [ins[5 * (h // 2) + 1] for h in range(4)]
    values = [ins[5 * (h // 2) + 2 + h % 2] for h in range(4)]
    col = lax.broadcasted_iota(jnp.int32, (BLOCK, BLOCK), 1)
    row = lax.broadcasted_iota(jnp.int32, (BLOCK, BLOCK), 0) + i * BLOCK
    begin = start[:, :1]

    def each(step):
        for j in range(BLOCKS):

            @pl.when((j >= low[i]) & (j <= i))
            def _(j=j):
                step(j, slice(j * BLOCK, j * BLOCK + BLOCK))

    peak_acc[...] = jnp.full_like(peak_acc, MASKED)
    o_acc[...] = jnp.zeros_like(o_acc)
    dq_acc[...] = jnp.zeros_like(dq_acc)

    def score(j, at):
        here = col + j * BLOCK
        allowed = (here >= begin) & (here <= row)
        for h in range(4):
            s = jnp.where(allowed, nt(queries[h], keys[h][at, :]), MASKED)
            scores[h, j] = s
            peak = peak_acc[h]
            for lanes in range(0, BLOCK, 128):
                peak = jnp.maximum(peak, s[:, lanes : lanes + 128])
            peak_acc[h] = peak

    each(score)
    peaks = [jnp.max(peak_acc[h], axis=1, keepdims=True) for h in range(4)]

    def weigh(j, at):
        for h in range(4):
            p = jnp.exp(scores[h, j] - peaks[h]).astype(BF)
            probs[h, j] = p
            o_acc[h] += nn(p, values[h][at, :])

    each(weigh)
    grads, shifted = [], []
    for block in range(2):
        scaled = []
        for h in range(2):
            out = o_acc[2 * block + h]
            first = HEAD_DIM * (1 - h)
            inverse = 1.0 / out[:, first : first + 1]
            out = out * inverse
            grad = jnp.where(masks[h], ins[5 * block + 4][...].astype(F32) * inverse, 0.0).astype(BF)
            wide = grad.astype(F32)
            delta = jnp.sum(wide * out, axis=1, keepdims=True)
            coarse = delta.astype(BF).astype(F32)
            wide = jnp.where(lane == first, -coarse, wide)
            shifted.append(jnp.where(lane == first + 1, coarse - delta, wide).astype(BF))
            grads.append(grad)
            scaled.append(out)
        outs[5 * block][...] = jnp.where(masks[0], *scaled).astype(BF)

    def back(j, at):
        for h in range(4):
            p = probs[h, j]
            d_scores = (p.astype(F32) * nt(shifted[h], values[h][at, :])).astype(BF)
            dq_acc[h] += nn(d_scores, keys[h][at, :])
            dk_acc[h // 2, at, :] += tn(d_scores, queries[h])
            dv_acc[h // 2, at, :] += tn(p, grads[h])

    each(back)
    rows = pl.ds(pl.multiple_of(i * BLOCK, BLOCK), BLOCK)
    for block in range(2):
        dq = jnp.where(masks[0], dq_acc[2 * block], dq_acc[2 * block + 1]) * SCALE
        dq = rotated(dq, [tables[t, rows, :] for t in range(3)], -1.0)
        outs[5 * block + 1][...] = dq.astype(BF)
        outs[5 * block + 4][0:1, :] += jnp.sum(dq, axis=0, keepdims=True)

    @pl.when(i == BLOCKS - 1)
    def _():
        for block in range(2):
            _, _, dk_out, dv_out, sums = outs[5 * block : 5 * block + 5]
            for j in range(8):
                rows = slice(j * 256, j * 256 + 256)
                dk = rotated(dk_acc[block, rows], [tables[t, rows] for t in range(3)], -1.0)
                dv = dv_acc[block, rows]
                dk_out[rows, :] = dk.astype(BF)
                dv_out[rows, :] = dv.astype(BF)
                sums[1:2, :] += jnp.sum(dk, axis=0, keepdims=True)
                sums[2:3, :] += jnp.sum(dv, axis=0, keepdims=True)


def attend(low, heads, start, tables, after=()):
    tile = pl.BlockSpec((BLOCK, 128), lambda i, o: (i, 0))
    full = whole(SEQ, 128)
    head = shape(SEQ, 128)
    return call(
        attend_kernel,
        (BLOCKS,),
        [(value, (tile, full, full, full, tile)[at % 5]) for at, value in enumerate(heads)]
        + [(start, tile), (tables, whole(3, SEQ, 128))],
        [
            (head, tile),
            (head, tile),
            (head, full),
            (head, full),
            (shape(8, 128, dtype=F32), whole(8, 128)),
        ]
        * 2,
        [
            pltpu.VMEM((4, BLOCKS, BLOCK, BLOCK), F32),
            pltpu.VMEM((4, BLOCKS, BLOCK, BLOCK), BF),
            pltpu.VMEM((2, SEQ, 128), F32),
            pltpu.VMEM((2, SEQ, 128), F32),
            pltpu.VMEM((4, BLOCK, 128), F32),
            pltpu.VMEM((4, BLOCK, 128), F32),
            pltpu.VMEM((4, BLOCK, 128), F32),
        ],
        prefetch=(low,),
        large=True,
        after=after,
    )


def att_grad_kernel(place, n, c, dq, dk, dv, o, grad0, grad1, grad2, acc):
    step = pl.program_id(0)

    @pl.when(step == 0)
    def _():
        acc[...] = jnp.zeros_like(acc)

    acc[:384] += tn(jnp.concatenate([dq[...], dk[...], dv[...]], axis=1), n[...])
    for r in range(4):
        acc[384:, 512 * r : 512 * r + 512] += tn(o[...], c[0, place[r]])

    @pl.when(step == SEQ // TILE - 1)
    def _():
        for part in range(4):
            row, rows = 128 * part, slice(64 * part, 64 * part + 64)
            store_grad(grad0, 64 * part, acc[row : row + 64])
            value = acc[row + 64 : row + 128]
            for at, (grad, r) in enumerate(((grad1, 0), (grad1, 2), (grad2, 1), (grad2, 3))):
                grad[at % 2, rows, :] = value[:, 512 * r : 512 * r + 512].astype(BF)


def att_grad(place, normed, cot, dq, dk, dv, o, after=()):
    head = pl.BlockSpec((TILE, 128), lambda i, *_: (i, 0))
    return call(
        att_grad_kernel,
        (SEQ // TILE,),
        token_inputs(normed, cot) + [(value, head) for value in (dq, dk, dv, o)],
        [(shape(4, 256, 512), whole(4, 256, 512))] + [(shape(2, 256, 512), whole(2, 256, 512))] * 2,
        [pltpu.VMEM((512, MODEL_WIDTH), F32)],
        prefetch=(place,),
        large=True,
        after=after,
    )


def join(joined, spans, rights):
    row = 0
    for at, (first, size) in enumerate(spans):
        for r in range(4):
            joined[row : row + size, 512 * r : 512 * r + 512] = rights[4 * at + r][
                0, first : first + size, :
            ]
        row += size


def project(prefetch, items, tokens, outputs, store, after=()):
    lefts = [left for left, _ in items]
    parts = [part for _, rows in items for part in rows]
    spans = [(first, size) for _, first, size in parts]
    rights = [piece(*one) for pieces, _, _ in parts for one in pieces]

    def body(*refs):
        scalars, refs = refs[: len(prefetch)], refs[len(prefetch) :]
        left_refs, refs = refs[: len(lefts)], refs[len(lefts) :]
        right_refs, refs = refs[: len(rights)], refs[len(rights) :]
        *outs, joined = refs

        @pl.when(pl.program_id(0) == 0)
        def _():
            join(joined, spans, right_refs)

        left = jnp.concatenate([ref[...] for ref in left_refs], axis=1)
        store(scalars, outs, lambda r: nn(left, joined[:, 512 * r : 512 * r + 512]).astype(BF))

    return call(
        body,
        (SEQ // TILE,),
        [(left, pl.BlockSpec((TILE, left.shape[1]), tokens)) for left in lefts] + rights,
        outputs,
        [pltpu.VMEM((sum(size for _, size in spans), MODEL_WIDTH), BF)],
        prefetch=prefetch,
        large=True,
        after=after,
    )


def project_near(sz, items, after=()):
    per = HALF // TILE

    def store(scalars, outs, value):
        for out, pieces in zip(outs, ((1, 3), (0, 2)), strict=True):
            for at, r in enumerate(pieces):
                out[at, 0] = value(r)

    out = pl.BlockSpec((2, 1, TILE, 512), lambda i, *_: (0, i // per, i % per, 0))
    return project(
        (sz,),
        items,
        lambda i, s: (((i // per) ^ s[0]) * per + i % per, 0),
        [(shape(2, 2, HALF, 512), out)] * 2,
        store,
        after,
    )


def added(values):
    total = values[0].astype(F32)
    for value in values[1:]:
        total = total + value.astype(F32)
    return total.astype(BF)


def grad_inputs(values):
    inputs, reads = [], []
    for value in values:
        at = len(inputs)
        if isinstance(value, list):
            inputs += [(one, whole(2, 256, 512)) for one in value]
            reads.append(lambda refs, step, at=at: refs[at + step // 2][step % 2])
        else:
            inputs.append((value, whole(4, 256, 512)))
            reads.append(lambda refs, step, at=at: refs[at][step])
    return inputs, reads


def add(left, right, after=()):
    inputs, reads = grad_inputs([left, right])

    def body(*refs):
        for step in range(4):
            refs[-1][step] = added([read(refs, step) for read in reads])

    return call(
        body, (1,), inputs, [(shape(4, 256, 512), whole(4, 256, 512))], after=after
    )


def total_grad(groups, after=()):
    inputs, reads = [], []
    for group in groups:
        found, read = grad_inputs(group)
        reads.append((len(inputs), len(found), read))
        inputs += found
    rows = 256 * len(groups)

    def body(*refs):
        near, same = refs[-2:]
        for step in range(4):
            out = same if step < 2 else near
            for g, (at, size, read) in enumerate(reads):
                mine = refs[at : at + size]
                out[step % 2, 256 * g : 256 * g + 256, :] = added([one(mine, step) for one in read])

    out = (shape(2, rows, 512), whole(2, rows, 512))
    return call(body, (1,), inputs, [out, out], after=after)


def quarters(value):
    return [value[256 * k : 256 * k + 256, :] for k in range(value.shape[0] // 256)]


def blocks(count):
    return (shape(count, 256, 512), whole(count, 256, 512))


FLAT = (shape(HALF, 512), whole(HALF, 512))


def quarter(array, piece, half):
    return (array, pl.BlockSpec((1, 1, HALF, 512), lambda *_: (piece, half, 0, 0)))


def scatter_far(same, near, counts, grad, after=()):
    over_z, over_y = counts
    groups = grad[0].shape[1] // 256

    def body(same, near, grad_same, grad_near, to_z, to_y, to_x):
        far = quarters(added([same[0, 0], near[0, 0]]))
        for k in range(over_z):
            to_z[k] = far[k]
        for k in range(over_y):
            to_y[k] = far[over_z + k]
        for at, ref in enumerate((grad_same, grad_near)):
            for g in range(groups):
                rows = slice(256 * g, 256 * g + 256)
                to_x[groups * at + g] = ref[0, rows, :]
                to_y[over_y + groups * at + g] = ref[1, rows, :]

    pair = whole(2, 256 * groups, 512)
    return call(
        body,
        (1,),
        [quarter(same, 1, 1), quarter(near, 1, 1), (grad[0], pair), (grad[1], pair)],
        [blocks(over_z), blocks(over_y + 2 * groups), blocks(2 * groups)],
        after=after,
    )


def scatter_kept(same, near, after=(), carry=()):
    places = ((0, 0), (1, 0), (0, 1))

    def body(*refs):
        for at in range(3):
            refs[6 + at][...] = added([refs[2 * at][0, 0], refs[2 * at + 1][0, 0]])

    return call(
        body,
        (1,),
        [quarter(value, *place) for place in places for value in (same, near)],
        [FLAT] * 3,
        after=after,
        carry=carry,
    )


def scatter_second(for_y, from_z, after=()):
    def body(for_y, from_z, to_y):
        for k in range(4):
            rows = slice(256 * k, 256 * k + 256)
            to_y[rows, :] = added([for_y[rows, :], from_z[k]])

    return call(
        body,
        (1,),
        [(for_y, FLAT[1]), (from_z, whole(4, 256, 512))],
        [FLAT],
        after=after,
    )[0]


def scatter_last(for_y, from_z, for_z, from_y, near_grad, after=()):
    def body(for_y, from_z, for_z, from_y, near_grad, to_z, to_y, grad):
        for k in range(4):
            rows = slice(256 * k, 256 * k + 256)
            to_y[rows, :] = added([for_y[rows, :], from_z[k]]) if k < 3 else for_y[rows, :]
            to_z[rows, :] = for_z[rows, :] if k < 3 else added([for_z[rows, :], from_y[0]])
        for k in range(2):
            grad[k] = near_grad[k]
            grad[2 + k] = from_y[1 + k]

    three = whole(3, 256, 512)
    return call(
        body,
        (1,),
        [
            (for_y, FLAT[1]),
            (from_z, three),
            (for_z, FLAT[1]),
            (from_y, three),
            (near_grad, whole(2, 256, 512)),
        ],
        [FLAT, FLAT, blocks(4)],
        after=after,
    )


def more_dp(value):
    if lax.axis_size("xo") > 1:
        return lax.psum(value, "xo")
    return value


def on_device(
    block_input,
    cotangent,
    doc_lengths,
    layernorm_gain,
    layernorm_bias,
    qkv_weight,
    qkv_bias,
    fc1_weight,
    fc1_bias,
    dense_weight,
    fc2_weight,
    out_bias,
):
    x, zh, zl = lax.axis_index("x"), lax.axis_index("zh"), lax.axis_index("zl")
    here = 2 * lax.axis_index("y") + lax.axis_index("c")
    place = jnp.stack([here ^ r for r in range(4)]).astype(jnp.int32)
    sx = x.astype(jnp.int32).reshape(1)
    sz = zl.astype(jnp.int32).reshape(1)

    tokens = lax.all_gather(block_input, ("zl", "y", "c"), axis=0, tiled=False)
    cot = lax.all_gather(cotangent, ("zl", "y", "c"), axis=0, tiled=False)
    tokens, cot = (value.reshape(2, 4, HALF, 512) for value in (tokens, cot))

    scale = jnp.stack([layernorm_gain, layernorm_bias])
    scale = jnp.concatenate([scale, swap(scale, "c")], axis=0)
    heads_bias = qkv_bias.reshape(3, 2, HEAD_DIM)
    units_bias = fc1_bias.reshape(2, 256)
    heads_bias = jnp.where(x == 0, heads_bias, heads_bias[:, ::-1])
    units_bias = jnp.where(x == 0, units_bias, units_bias[::-1])
    own_bias = jnp.concatenate([heads_bias.reshape(1, 384), units_bias.reshape(1, 512)], axis=1)

    order = jnp.stack([here ^ r for r in (3, 1, 2, 0)]).astype(jnp.int32)
    near1, near3, far2, r0, to_y2, to_z0 = pack(order, sx, qkv_weight, fc1_weight, dense_weight, fc2_weight)
    near3 = swap(near3, "c")
    r1 = swap(near1, "c")

    lengths = lax.dynamic_index_in_dim(doc_lengths, zh, 0, keepdims=False)
    ends = jnp.cumsum(lengths)
    spot = jnp.arange(SEQ, dtype=jnp.int32)
    begin = jnp.sum(jnp.where(spot[:, None] >= ends[None, :], lengths[None, :], 0), axis=1)
    low = (begin[::BLOCK] // BLOCK).astype(jnp.int32)
    start = jnp.broadcast_to(begin[:, None], (SEQ, 128)).astype(jnp.int32)
    freqs = jnp.exp(jnp.arange(ROT // 2, dtype=F32) * (-2.0 * math.log(10000.0) / ROT))
    angle = spot.astype(F32)[:, None] * freqs[None, :]
    cosine, sine = jnp.cos(angle), jnp.sin(angle)
    def rows(weights, row, first, size):
        return [
            ([(*one[:2], one[2] if row is None else row) for one in weights[4 * s : 4 * s + 4]], first, size)
            for s in range(2)
        ]

    input_single = block_input.astype(F32)
    branch_gradient = cotangent.astype(F32)

    from_y2, from_z0 = swap(to_y2, "y"), swap(to_z0, "zh")
    to_y3, to_z1 = split_first(near3, r1, after=[scale])
    from_y3, from_z1 = swap(to_y3, "y"), swap(to_z1, "zh")
    tables = rotary_tables(cosine, sine, after=[to_z1])
    scale = jnp.concatenate([scale, swap(scale, "y")], axis=0)
    token, (other_bias,) = gate(
        [tables, start, from_y2, from_z0, from_y3, from_z1], [own_bias]
    )

    to_x, to_z, att_y, att01 = stack_mlp(
        from_y2, from_y3, from_z0, from_z1, far2, near3, r0, r1, after=[token]
    )
    normed, stats = norm_tokens(place, tokens, scale, after=[to_x])
    att23, other_bias = swap(att_y, "y"), swap(other_bias, "zh")
    from_x, other23 = swap(to_x, "x"), swap(to_z, "zh")
    token, (other23, att23, att01) = gate([stats, from_x, other_bias], [other23, att23, att01])
    mine = lax.dynamic_slice_in_dim(stats, zl * HALF, HALF, axis=0)
    average, inverse = mine[:, :1], mine[:, 128:129]
    centered = (input_single - average) * inverse

    next23, att01 = swap(other23, "x"), swap(att01, "zh")
    own_w = [(r0, 0), (r1, 0), (from_y2, 0), (from_y3, 0)]
    own_w += [(r0, 1), (r1, 1), (from_x, 0), (from_x, 1)]
    own_act, own_slope = hidden_units(normed, own_w, own_bias[:, 384:], after=[token])
    token, (att01, att23) = gate([own_act, next23], [att01, att23])

    other_w = [(from_z0, 0), (from_z1, 0), (other23, 0), (other23, 1)]
    other_w += [(from_x, 2), (from_x, 3), (next23, 0), (next23, 1)]
    next_att01, other_att23, next_att23 = swap(att01, "x"), swap(att23, "zh"), swap(att23, "x")
    other_act, other_slope = hidden_units(normed, other_w, other_bias[:, 384:], after=[token])
    other_dfc, *other_mlp, other_units = mlp(
        place, normed, cot, other_act, other_slope, other_w
    )
    token, (other_att23, other_mlp[1]) = gate(
        [other_units, next_att01, next_att23], [other_att23, other_mlp[1]]
    )

    from_x, next_other23 = swap(other_mlp[1], "x"), swap(other_att23, "x")
    own_dfc, *own_mlp, own_units = mlp(
        place, normed, cot, own_act, own_slope, own_w, after=[token]
    )
    own_a = [(r0, 0, 2), (r1, 0, 2), (att23, 0, 0), (att23, 1, 0)]
    own_a += [(r0, 1, 2), (r1, 1, 2), (next_att23, 0, 0), (next_att23, 1, 0)]
    own_qkv = heads(place, normed, cot, own_a, own_bias[:, :384], tables, after=[own_units])
    token, (other_mlp[3], own_mlp[1]) = gate(
        [own_qkv[0], from_x, next_other23], [other_mlp[3], own_mlp[1]]
    )

    other_a = [
        (array, i, 0) for array in (att01, other_att23, next_att01, next_other23) for i in range(2)
    ]
    fc2 = add(other_mlp[0], from_x, after=[token])[0]
    to_fc2 = swap(fc2, "zh")
    from_x, own_fc2 = swap(other_mlp[3], "x"), swap(own_mlp[1], "x")
    other_qkv = heads(place, normed, cot, other_a, other_bias[:, :384], tables, after=[fc2])
    attended = attend(low, own_qkv + other_qkv, start, tables)
    own_o, own_dq, own_dk, own_dv, own_sums = attended[:5]
    other_o, other_dq, other_dk, other_dv, other_sums = attended[5:]
    other_sums = jnp.concatenate([other_sums[:3].reshape(1, 384), other_units], axis=1)
    token, (own_mlp[3], other_sums) = gate(
        [own_o, to_fc2, from_x, own_fc2], [own_mlp[3], other_sums]
    )

    fc1 = add(other_mlp[2], from_x, after=[token])[0]
    to_fc1 = swap(fc1, "zh")
    other_att = att_grad(
        place, normed, cot, other_dq, other_dk, other_dv, other_o, after=[fc1]
    )
    other_sums = swap(other_sums, "zh")
    from_x, own_fc1 = swap_all(other_att[1:], "x"), swap(own_mlp[3], "x")
    items = [(own_dfc, rows(own_w, 1, 0, 256)), (other_dfc, rows(other_w, 1, 0, 256))]
    for part, (left, right) in enumerate(
        ((own_dq, other_dq), (own_dk, other_dk), (own_dv, other_dv))
    ):
        items.append((left, rows(own_a, None, 64 * part, 64)))
        items.append((right, rows(other_a, None, 64 * part, 64)))
    dn_near, dn_same = project_near(sz, items, after=[other_att[0]])
    own_sums = jnp.concatenate([own_sums[:3].reshape(1, 384), own_units], axis=1)
    token, (dn_near,) = gate([dn_same, own_sums, to_fc1, *from_x, own_fc1, other_sums], [dn_near])

    sums = own_sums + other_sums
    heads_sum, units_sum = sums[0, :384].reshape(3, 2, HEAD_DIM), sums[0, 384:].reshape(2, 256)
    heads_sum = jnp.where(x == 0, heads_sum, heads_sum[:, ::-1]).reshape(1, 384)
    units_sum = jnp.where(x == 0, units_sum, units_sum[::-1]).reshape(1, 512)
    sums = jnp.concatenate([heads_sum, units_sum], axis=1)
    dn_near, sums_x = swap(dn_near, "c"), swap(sums, "x")
    mlp_near, mlp_same = total_grad(
        [[own_mlp[0], own_fc2, to_fc2], [own_mlp[2], own_fc1, to_fc1]], after=[token]
    )
    mlp_near, mlp_same = swap(more_dp(mlp_near), "c"), more_dp(mlp_same)
    att = add(other_att[0], from_x, after=[mlp_same])[0]
    token, (att,) = gate([dn_near, mlp_near, sums_x], [att])

    to_z, to_y, mlp01 = scatter_far(
        dn_same, dn_near, (4, 0), (mlp_same, mlp_near), after=[token]
    )
    from_z, mlp23 = swap(to_z, "zl"), swap(to_y, "y")
    own_att = att_grad(place, normed, cot, own_dq, own_dk, own_dv, own_o, after=[to_z])
    dn, for_y, for_z = scatter_kept(dn_same, dn_near, after=[own_att[0]])
    own_from_att, to_att = swap_all(own_att[1:], "x"), swap(att, "zh")
    items = [
        (own_act, rows(own_w, 0, 0, 256)),
        (other_act, rows(other_w, 0, 0, 256)),
        (own_o, rows(own_a, None, 192, 64)),
        (other_o, rows(other_a, None, 192, 64)),
    ]
    near, same = project_near(sz, items, after=[dn])
    token, (near, mlp01, mlp23, for_z) = gate(
        [same, to_att, *own_from_att, from_z], [near, mlp01, mlp23, for_z]
    )

    near, dn_z, next01 = swap(near, "c"), swap(for_z, "zl"), swap(mlp01, "x")
    to_y = scatter_second(for_y, from_z, after=[token])
    dn_y = swap(to_y, "y")
    att_near, att_same = total_grad([[own_att[0], own_from_att, to_att]], after=[to_y])
    att_near, att_same = swap(more_dp(att_near), "c"), more_dp(att_same)
    token, (mlp23,) = gate([att_same, near, dn_z, dn_y, next01, att_near], [mlp23])

    next23 = swap(mlp23, "x")
    to_z, to_y, att01 = scatter_far(same, near, (3, 1), (att_same, att_near), after=[token])
    from_z, from_y = swap(to_z, "zl"), swap(to_y, "y")
    branch, branch_y, branch_z, dn_y = scatter_kept(same, near, after=[to_z], carry=[dn_y])
    dn = dn.astype(F32) + dn_y.astype(F32) + dn_z.astype(F32)
    row_sums = jnp.stack(
        [jnp.sum(dn * layernorm_gain, axis=1), jnp.sum(dn * layernorm_gain * centered, axis=1)]
    )
    col_sums = jnp.stack(
        [
            jnp.sum(dn * centered, axis=0),
            jnp.sum(dn, axis=0),
            jnp.sum(branch_gradient, axis=0),
        ]
    )
    row_sums = row_sums + swap(row_sums, "c")
    row_sums = row_sums + swap(row_sums, "y")
    col_sums = col_sums + swap(col_sums, "zl")
    token, (col_sums,) = gate([branch, from_z, from_y, next23, row_sums], [col_sums])

    to_z, to_y, att_pieces = scatter_last(
        branch_y, from_z, branch_z, from_y, att01, after=[token]
    )
    branch_z, branch_y = swap(to_z, "zl"), swap(to_y, "y")
    next_att = swap(att_pieces, "x")
    mlp_pieces = (mlp01, mlp23, next01, next23)
    fc2_grad = unpack_fc2(place, sx, mlp_pieces, after=[to_y])
    fc1_grad = unpack_fc1(place, sx, mlp_pieces, after=[fc2_grad])
    token, (col_sums,) = gate([fc1_grad], [col_sums])
    for axis in ("zh", "x"):
        col_sums = col_sums + swap(col_sums, axis)
    qkv_grad, dense_grad = unpack_att(place, sx, (att_pieces, next_att), after=[token])
    sums = more_dp(sums + sums_x)

    qkv_bias_grad, fc1_bias_grad = sums[0, :384].reshape(3, 128), sums[0, 384:]

    branch = branch.astype(F32) + branch_y.astype(F32) + branch_z.astype(F32)
    result = (input_single + (branch + out_bias)).astype(BF)
    input_grad = branch_gradient + inverse * (
        dn * layernorm_gain
        - row_sums[0][:, None] / MODEL_WIDTH
        - centered * (row_sums[1][:, None] / MODEL_WIDTH)
    )
    col_sums = more_dp(col_sums)
    return (
        result,
        input_grad,
        col_sums[0],
        col_sums[1],
        qkv_grad,
        qkv_bias_grad,
        fc1_grad,
        fc1_bias_grad,
        dense_grad,
        fc2_grad,
        col_sums[2],
    )


def solution(mesh):
    dp, row, col = mesh.devices.shape
    assert dp % 2 == 0 and row == 4 and col == 4
    parts = Mesh(
        mesh.devices.reshape(dp // 2, 2, 2, 2, 2, 2), ("xo", "x", "zh", "zl", "y", "c")
    )
    data, rows, cols = ("xo", "x"), ("zh", "zl"), ("y", "c")
    return jax.shard_map(
        on_device,
        mesh=parts,
        in_specs=(
            P(data + rows, cols),
            P(data + rows, cols),
            P(data, None),
            P(cols),
            P(cols),
            P(None, rows, cols),
            P(None, rows + cols),
            P(rows, cols),
            P(rows + cols),
            P(cols, rows),
            P(cols, rows),
            P(cols),
        ),
        out_specs=(
            P(data + rows, cols),
            P(data + rows, cols),
            P(cols),
            P(cols),
            P(None, rows, cols),
            P(None, rows + cols),
            P(rows, cols),
            P(rows + cols),
            P(cols, rows),
            P(cols, rows),
            P(cols),
        ),
        check_vma=False,
    )
```
